256 devices in a mesh: ctx: 32 (over z, x_hi, core), chan: 8 (over y, x_lo).
Axes of the slice: x: 4 (x_hi: 2, x_lo: 2; x = x_hi * 2 + x_lo), y: 4, z: 8, core: 2. Of those that a mesh axis runs over, the one named last changes fastest.
Arguments:
- queries: bfloat16 [4096, 4096], P('ctx', 'chan'), may hold values from -6 to 6
- key_input: bfloat16 [4096, 4096], P('ctx', 'chan'), may hold values from -6 to 6
- gate_values: bfloat16 [4096, 4096], P('ctx', 'chan'), may hold values from -6 to 6
- cotangent: bfloat16 [4096, 4096], P('ctx', 'chan'), may hold values from -6 to 6
- out_weight: bfloat16 [4096, 4096], P('chan', 'ctx'), may hold values from -0.09375 to 0.09375
- decay_rates: float32 [4096, 16], P('chan'), may hold values from 2.4414062e-06 to 0.033
- residues: float32 [4096, 16], P('chan'), may hold values from -1.5 to 1.5
- skip_gain: float32 [4096], P('chan'), may hold values from 0.5 to 1.5
Outputs:
- final: bfloat16 [4096, 4096], P('ctx', 'chan')
- grad_queries: bfloat16 [4096, 4096], P('ctx', 'chan')
- grad_keys: bfloat16 [4096, 4096], P('ctx', 'chan')
- grad_gates: bfloat16 [4096, 4096], P('ctx', 'chan')
- grad_weight: bfloat16 [4096, 4096], P('chan', 'ctx')
- grad_residues: float32 [4096, 16], P('chan')
- grad_skip: float32 [4096], P('chan')
The draws below stay inside these ranges and needn't reach their ends.
All inputs are finite; a program needn't handle non-finite values.
Results may differ from the reference program's by a relative error of at most 0.013.
Values may be sent and summed in bfloat16 or wider, within the bound.
A program may use at most 128 MiB of HBM per device.

```python
import math
import jax
import jax.numpy as jnp
from jax import lax

C = 4096
M = 16
LENGTH = 4096


def strengthened(array, stream_key, source, target, parts, factor):
    owner, partner = [(jnp.arange(array.shape[position]) // (array.shape[position] // parts)).reshape([-1 if axis == position else 1 for axis in range(array.ndim)]) for position in (source, target)]
    chosen = jax.random.permutation(stream_key, parts)[partner]
    strong = (owner == chosen) | (owner == (partner + parts // 2) % parts)
    return jnp.where(strong, factor * array, array)


def steps_of(rng, extent, pieces, least, largest):
    def one(dim, parts):
        heights = jax.random.uniform(jax.random.fold_in(jax.random.fold_in(rng, 6), dim), (parts,), jnp.float32, least / len(pieces), largest / len(pieces))
        return jnp.repeat(jnp.exp(heights), extent[dim] // parts).reshape((-1,) + (1,) * (len(extent) - dim - 1))

    factor_of = one(*pieces[0])
    for cut in pieces[1:]:
        factor_of = factor_of * one(*cut)
    return factor_of


def centred(own_key, extent, spread, bound, shards=(), kind=jnp.bfloat16):
    values = jax.random.normal(own_key, extent, jnp.float32) * spread
    if len(shards) > 0:
        values = steps_of(own_key, extent, shards, -0.22, 0.18) * values
    return jnp.clip(values, min=-bound, max=bound).astype(kind)


def noise_with(rng, dims, spread, limit, cuts, heavy, kind=jnp.bfloat16):
    entries = spread * jax.random.normal(rng, dims, jnp.float32)
    if cuts:
        entries = entries * steps_of(rng, dims, cuts, -0.22, 0.18)
    return jnp.clip(strengthened(entries, jax.random.fold_in(rng, 3), *heavy), -limit, limit).astype(kind)


def setup_inputs(seed: int = 0) -> dict:
    key_list = jax.random.split(jax.random.key(seed), 9)
    return {
        "queries": centred(key_list[0], (LENGTH, C), 1.0, 6.0, ((0, 32), (1, 8))),
        "key_input": centred(key_list[1], (LENGTH, C), 1.0, 6.0, ((0, 32), (1, 8))),
        "gate_values": centred(key_list[2], (LENGTH, C), 1.0, 6.0, ((0, 32), (1, 8))),
        "cotangent": noise_with(key_list[3], (LENGTH, C), 1.0, 6.0, ((0, 32), (1, 8)), (0, 1, 32, 2.75)),
        "out_weight": centred(key_list[4], (C, C), C ** -0.5, 0.09375, ((0, 8), (1, 32))),
        "decay_rates": jnp.clip(jnp.exp(math.log(0.033) - 9.5116887 * jax.random.uniform(key_list[5], (C, M), jnp.float32) ** steps_of(key_list[5], (C, M), ((0, 8),), -0.2, 0.2)), 2.441406195430318e-06, 0.033),
        "residues": centred(key_list[6], (C, M), 0.25, 1.5, ((0, 8),), jnp.float32),
        "skip_gain": jnp.clip(1.0 + 0.1 * jax.random.normal(key_list[7], (C,), jnp.float32), 0.5, 1.5),
    }


channel_block = 64

def causal_filter(gated, rates, gains):
    positions = gated.shape[0]
    chans = gated.shape[1]
    groups = chans // channel_block
    steps = jnp.arange(positions, dtype=jnp.float32)
    padded_len = 2 * positions

    def one_block(operands):
        signal, rate_rows, gain_rows = operands
        filter_taps = lax.optimization_barrier(jnp.sum(gain_rows[:, :, None] * jnp.exp(-rate_rows[:, :, None] * steps[None, None, :]), axis=1))
        spectrum = jnp.fft.rfft(signal, padded_len, axis=0) * jnp.fft.rfft(filter_taps.T, padded_len, axis=0)
        return jnp.fft.irfft(spectrum, padded_len, axis=0)[:positions]
    split = gated.reshape(positions, groups, channel_block).transpose(1, 0, 2)
    result = lax.map(one_block, (split, rates.reshape(groups, channel_block, -1), gains.reshape(groups, channel_block, -1)))
    return result.transpose(1, 0, 2).reshape(positions, chans)

def reference(queries, key_input, gate_values, cotangent, out_weight, decay_rates, residues, skip_gain):
    query_f = queries.astype(jnp.float32)
    key_f = key_input.astype(jnp.float32)
    gate_f = gate_values.astype(jnp.float32)
    gated = query_f * key_f
    twice = -2.0 * decay_rates
    norms = jnp.sqrt(jnp.expm1(twice * LENGTH) / jnp.expm1(twice))

    def filtered(signal, residue_in, skip_in):
        return causal_filter(signal, decay_rates, residue_in / norms) + skip_in[None, :] * signal
    conv_out, pullback = jax.vjp(filtered, gated, residues, skip_gain)
    mixed = (gate_f * conv_out).astype(jnp.bfloat16)
    final = jnp.dot(mixed, out_weight, preferred_element_type=jnp.float32).astype(jnp.bfloat16)
    out_grad = jnp.dot(cotangent, out_weight.T, preferred_element_type=jnp.float32).astype(jnp.bfloat16)
    conv_grad = out_grad.astype(jnp.float32) * gate_f
    gated_grad, residue_grad, skip_grad = pullback(conv_grad)
    scale = LENGTH ** (-0.5)
    grad_weight = (jnp.dot(mixed.T, cotangent, preferred_element_type=jnp.float32) * scale).astype(jnp.bfloat16)
    return (final, (gated_grad * key_f).astype(jnp.bfloat16), (gated_grad * query_f).astype(jnp.bfloat16), (out_grad.astype(jnp.float32) * conv_out).astype(jnp.bfloat16), grad_weight, residue_grad * scale, skip_grad * scale)
```

```python
import functools
import math

import jax
import jax.numpy as jnp
from jax import lax
from jax.experimental import pallas as pl
from jax.experimental.pallas import tpu as pltpu
from jax.sharding import PartitionSpec as P

MESH = pl.DeviceIdType.MESH
f32 = jnp.float32
bf16 = jnp.bfloat16

GROUP = 4
LANES = 128
SUBS = 8
MODES = 16
COPIES = 96


def one_minus_exp(x):
    series = jnp.ones_like(x)
    for n in range(9, 1, -1):
        series = 1.0 - x * (1.0 / n) * series
    return jnp.where(x < 0.5, x * series, 1.0 - jnp.exp(-x))


def kernel(
    zs, chans, length,
    q_ref, key_ref, gate_ref, cot_ref, w_ref, rate_ref, res_ref, skip_ref,
    final_ref, gq_ref, gk_ref, gg_ref, gw_ref, gres_ref, gskip_ref,
    gat_s, cotall, wall, xg, gateg, x_f, co_f, cg_f, pre_f, pre_b, e_all, b_all, l_all,
    mixed_all, og_own, og_send, og_recv, og_mid, fp, frecv, fin_g, fin_pos, gp, rsbuf,
    ggrp, ggpos, gates_g, gates_pos, tot_all,
    ss, rs,
):
    rows = q_ref.shape[0]
    span = rows * GROUP
    step_len = span // SUBS
    half = w_ref.shape[0] // 2
    scale = 1.0 / math.sqrt(length)

    i = lax.axis_index("ctx")
    j = lax.axis_index("chan")
    z = lax.div(i, GROUP)
    k = lax.rem(i, GROUP)
    k1 = k + 1 - 2 * lax.rem(k, 2)
    k2 = lax.rem(k + 2, GROUP)
    k3 = GROUP - 1 - k
    kp = {1: k1, 2: k2, 3: k3}

    def zmod(d):
        return lax.rem(z + d + zs, zs)

    def jmod(d):
        return lax.rem(j + d, chans)

    def g_peer(d):
        return {"ctx": z * GROUP + kp[d]}

    def z_peer(d):
        return {"ctx": zmod(d) * GROUP + k}

    def c_peer(d):
        return {"chan": jmod(d)}

    def lane(index):
        return pl.ds(pl.multiple_of(index * LANES, LANES), LANES)

    def row(index):
        return pl.ds(pl.multiple_of(index * rows, rows), rows)

    count = [0]
    started = []

    def remote(src, dst, peer):
        n = count[0]
        count[0] += 1
        copy = pltpu.make_async_remote_copy(
            src_ref=src, dst_ref=dst, send_sem=ss.at[n], recv_sem=rs.at[n],
            device_id=peer, device_id_type=MESH,
        )
        copy.start()
        started.append(copy)
        return copy

    barrier = pltpu.get_barrier_semaphore()
    peers = [g_peer(d) for d in (1, 2, 3)]
    peers += [z_peer(d) for d in range(1, zs)]
    peers += [c_peer(d) for d in range(1, chans)]
    for peer in peers:
        pl.semaphore_signal(barrier, inc=1, device_id=peer, device_id_type=MESH)

    own = pl.ds(pl.multiple_of(k * LANES, LANES), LANES)
    rate = jnp.transpose(rate_ref[own, :])
    inv_norm = jnp.sqrt(one_minus_exp(2.0 * rate) / one_minus_exp(2.0 * length * rate))
    gain = jnp.transpose(res_ref[own, :]) * inv_norm
    decay = jnp.exp(-rate)
    decay_sub = jnp.exp(-step_len * rate)
    decay_span = jnp.exp(-span * rate)
    skip = skip_ref[:, lane(k)]
    skip_b = jnp.broadcast_to(skip, (SUBS, LANES))
    sub = lax.broadcasted_iota(jnp.int32, (SUBS, LANES), 0)

    def spread(table, m):
        return jnp.broadcast_to(table[m : m + 1, :], (SUBS, LANES))

    gat_s[...] = (q_ref[...].astype(f32) * key_ref[...].astype(f32)).astype(bf16)
    pl.semaphore_wait(barrier, len(peers))

    chunk = (pl.ds(0, half), pl.ds(half, half))
    ring = {}
    lanes_for = ((1, 0, 4), (-1, 1, 4), (1, 1, 3), (-1, 0, 3))

    def weight_hop(h):
        for d, c, hops in lanes_for:
            if h > hops:
                continue
            block = lane(zmod(-d * (h - 1)))
            if h == 1:
                src = w_ref.at[chunk[c], :]
            else:
                ring[d, c, h - 1].wait_recv()
                src = wall.at[chunk[c], block]
            ring[d, c, h] = remote(src, wall.at[chunk[c], block], z_peer(d))

    cot_ex = [
        remote(cot_ref.at[:, lane(kp[d])], cotall.at[row(k), lane(j)], g_peer(d))
        for d in (2, 3, 1)
    ]
    weight_hop(1)
    sig_ex = []
    for d in (2, 3, 1):
        sig_ex.append(remote(gat_s.at[:, lane(kp[d])], xg.at[row(k), :], g_peer(d)))
        sig_ex.append(remote(gate_ref.at[:, lane(kp[d])], gateg.at[row(k), :], g_peer(d)))
    cotall[row(k), lane(j)] = cot_ref[:, lane(k)]
    xg[row(k), :] = gat_s[:, lane(k)]
    gateg[row(k), :] = gate_ref[:, lane(k)]
    wall[:, lane(z)] = w_ref[...]

    for copy in cot_ex:
        copy.wait_recv()
    cot_ag = [
        remote(cotall.at[:, lane(j)], cotall.at[:, lane(j)], c_peer(d))
        for d in range(1, chans)
    ]
    weight_hop(2)

    decays = [spread(decay, m) for m in range(MODES)]
    zero = jnp.zeros((SUBS, LANES), f32)

    def at_step(t):
        return pl.ds(t, SUBS, stride=step_len)

    def ends(src, backward):
        def body(s, state):
            t = step_len - 1 - s if backward else s
            value = src[at_step(t), :]
            return tuple(decays[m] * state[m] + value for m in range(MODES))

        return lax.fori_loop(0, step_len, body, (zero,) * MODES, unroll=4)

    def prefix(state, pre, backward, all_ref):
        for m in range(MODES):
            factor = spread(decay_sub, m)
            total = state[m]
            for shift in (1, 2, 4):
                moved = pltpu.roll(total, SUBS - shift if backward else shift, 0)
                keep = sub < SUBS - shift if backward else sub >= shift
                total = total + jnp.where(keep, factor * moved, 0.0)
                factor = factor * factor
            moved = pltpu.roll(total, SUBS - 1 if backward else 1, 0)
            pre[m] = jnp.where(sub < SUBS - 1 if backward else sub >= 1, moved, 0.0)
            edge = 0 if backward else SUBS - 1
            all_ref[z, m : m + 1, :] = total[edge : edge + 1, :]

    def carried(pre, all_ref, backward):
        carry = jnp.zeros((MODES, LANES), f32)
        for n in range(zs):
            other = zs - 1 - n if backward else n
            ahead = z < other if backward else z > other
            carry = jnp.where(ahead, decay_span * carry + all_ref[other], carry)
        steps = (SUBS - 1 - sub if backward else sub).astype(f32)
        return tuple(
            pre[m] + jnp.exp(-step_len * steps * spread(rate, m)) * spread(carry, m)
            for m in range(MODES)
        )

    def tree(terms):
        while len(terms) > 1:
            terms = [a + b for a, b in zip(terms[::2], terms[1::2])]
        return terms[0]

    gains = [spread(gain, m) for m in range(MODES)]

    def sweep(src, out, state, backward):
        def body(s, state):
            t = step_len - 1 - s if backward else s
            value = src[at_step(t), :]
            state = tuple(decays[m] * state[m] + value for m in range(MODES))
            out[at_step(t), :] = (
                tree([gains[m] * state[m] for m in range(MODES)]) + skip_b * value
            )
            return state

        lax.fori_loop(0, step_len, body, state, unroll=2)

    for copy in sig_ex:
        copy.wait_recv()
    x_f[...] = xg[...].astype(f32)
    prefix(ends(x_f, False), pre_f, False, e_all)
    e_ex = [
        remote(e_all.at[z], e_all.at[z], z_peer(d)) for d in (4, 3, 5, 2, 6, 1, 7)
    ]
    weight_hop(3)
    for copy in e_ex:
        copy.wait_recv()
    start_f = carried(pre_f, e_all, False)
    for m in range(MODES):
        pre_f[m] = start_f[m]
    sweep(x_f, co_f, start_f, False)
    mixed_all[:, lane(k)] = (gateg[...].astype(f32) * co_f[...]).astype(bf16)
    mix_2 = remote(mixed_all.at[:, lane(k)], mixed_all.at[:, lane(k)], g_peer(2))
    mix_1 = remote(mixed_all.at[:, lane(k)], mixed_all.at[:, lane(k)], g_peer(1))
    weight_hop(4)
    mix_2.wait_recv()
    mix_3 = remote(mixed_all.at[:, lane(k2)], mixed_all.at[:, lane(k2)], g_peer(1))
    for copy in cot_ag:
        copy.wait_recv()
    for d, c, hops in lanes_for:
        ring[d, c, hops].wait_recv()

    def out_grad_part(index):
        return lax.dot_general(
            cotall[...], wall[own_rows(index), :], (((1,), (1,)), ((), ())),
            preferred_element_type=f32,
        )

    def own_rows(index):
        return pl.ds(pl.multiple_of(index * LANES, LANES), LANES)

    og_send[0] = out_grad_part(k3).astype(bf16)
    og_a = remote(og_send.at[0], og_recv.at[0], g_peer(1))
    og_send[1] = out_grad_part(k1).astype(bf16)
    og_b = remote(og_send.at[1], og_recv.at[1], g_peer(1))
    og_mid[...] = out_grad_part(k2)
    og_own[...] = out_grad_part(k)
    og_a.wait_recv()
    og_send[2] = (og_mid[...] + og_recv[0].astype(f32)).astype(bf16)
    og_c = remote(og_send.at[2], og_recv.at[2], g_peer(2))

    mix_1.wait_recv()
    mix_3.wait_recv()
    pairs = wall.shape[1] // (2 * LANES)
    wide = 2 * LANES
    for n in range(pairs):
        fp[:, n * wide : (n + 1) * wide] = jnp.dot(
            mixed_all[...], wall[:, n * wide : (n + 1) * wide], preferred_element_type=f32
        ).astype(bf16)
    fin_ex = [
        remote(fp.at[:, lane(jmod(d))], frecv.at[d - 1], c_peer(d)) for d in range(1, chans)
    ]

    for n in range(pairs):
        gp[:, n * wide : (n + 1) * wide] = lax.dot_general(
            mixed_all[...], cotall[:, n * wide : (n + 1) * wide], (((0,), (0,)), ((), ())),
            preferred_element_type=f32,
        ).astype(bf16)
    sums = {}
    slots = {}
    for d, c, hops in lanes_for:
        for h in range(1, hops + 1):
            slots[d, c, h] = len(slots)

    def weight_sum_hop(h):
        for d, c, hops in lanes_for:
            if h > hops:
                continue
            block = lane(zmod(d * (hops - h + 1)))
            if h == 1:
                src = gp.at[chunk[c], block]
            else:
                sums[d, c, h - 1].wait_recv()
                slot = slots[d, c, h - 1]
                rsbuf[slot] = (
                    rsbuf[slot].astype(f32) + gp[chunk[c], block].astype(f32)
                ).astype(bf16)
                src = rsbuf.at[slot]
            sums[d, c, h] = remote(src, rsbuf.at[slots[d, c, h]], z_peer(d))

    weight_sum_hop(1)

    og_b.wait_recv()
    og_c.wait_recv()
    og = (og_own[...] + og_recv[1].astype(f32) + og_recv[2].astype(f32)).astype(bf16).astype(f32)
    cg_f[...] = og * gateg[...].astype(f32)
    gates_g[...] = (og * co_f[...]).astype(bf16)
    gate_ex = [
        remote(gates_g.at[row(kp[d]), :], gates_pos.at[:, lane(k)], g_peer(d)) for d in (2, 3, 1)
    ]
    gates_pos[:, lane(k)] = gates_g[row(k), :]
    prefix(ends(cg_f, True), pre_b, True, b_all)
    b_ex = [
        remote(b_all.at[z], b_all.at[z], z_peer(d)) for d in (4, 3, 5, 2, 6, 1, 7)
    ]
    weight_sum_hop(2)

    def residue_body(s, carry):
        state, sums_m = carry
        value = x_f[at_step(s), :]
        grad = cg_f[at_step(s), :]
        state = tuple(decays[m] * state[m] + value for m in range(MODES))
        return state, tuple(sums_m[m] + grad * state[m] for m in range(MODES))

    _, mode_sums = lax.fori_loop(
        0, step_len, residue_body,
        (tuple(pre_f[m] for m in range(MODES)), (zero,) * MODES), unroll=2,
    )
    for m in range(MODES):
        l_all[z, m : m + 1, :] = jnp.sum(mode_sums[m], axis=0, keepdims=True)
    l_all[z, MODES : MODES + 8, :] = jnp.broadcast_to(
        jnp.sum(cg_f[...] * x_f[...], axis=0, keepdims=True), (8, LANES)
    )
    l_ex = [
        remote(l_all.at[z], l_all.at[z], z_peer(d)) for d in (4, 3, 5, 2, 6, 1, 7)
    ]

    for copy in b_ex:
        copy.wait_recv()
    sweep(cg_f, co_f, carried(pre_b, b_all, True), True)
    ggrp[...] = co_f[...].astype(bf16)
    gg_ex = [
        remote(ggrp.at[row(kp[d]), :], ggpos.at[:, lane(k)], g_peer(d)) for d in (2, 3, 1)
    ]
    ggpos[:, lane(k)] = ggrp[row(k), :]
    weight_sum_hop(3)

    for copy in l_ex:
        copy.wait_recv()
    total = l_all[0]
    for n in range(1, zs):
        total = total + l_all[n]
    tot_all[0:MODES, lane(k)] = total[0:MODES] * inv_norm * scale
    tot_all[MODES : MODES + 8, lane(k)] = total[MODES : MODES + 8] * scale
    tot_ex = [
        remote(tot_all.at[:, lane(k)], tot_all.at[:, lane(k)], g_peer(d)) for d in (2, 3, 1)
    ]
    weight_sum_hop(4)

    for copy in gg_ex:
        copy.wait_recv()
    spread_grad = ggpos[...].astype(f32)
    gq_ref[...] = (spread_grad * key_ref[...].astype(f32)).astype(bf16)
    gk_ref[...] = (spread_grad * q_ref[...].astype(f32)).astype(bf16)
    for copy in gate_ex:
        copy.wait_recv()
    gg_ref[...] = gates_pos[...]

    for copy in fin_ex:
        copy.wait_recv()
    fin = fp[:, lane(j)].astype(f32)
    for n in range(chans - 1):
        fin = fin + frecv[n].astype(f32)
    fin_g[...] = fin.astype(bf16)
    out_ex = [
        remote(fin_g.at[row(kp[d]), :], fin_pos.at[:, lane(k)], g_peer(d)) for d in (2, 3, 1)
    ]
    fin_pos[:, lane(k)] = fin_g[row(k), :]

    for c in (0, 1):
        part = gp[chunk[c], lane(z)].astype(f32)
        for d, other, hops in lanes_for:
            if other == c:
                sums[d, c, hops].wait_recv()
                part = part + rsbuf[slots[d, c, hops]].astype(f32)
        gw_ref[chunk[c], :] = (part * scale).astype(bf16)

    for copy in tot_ex:
        copy.wait_recv()
    for n in range(GROUP):
        gres_ref[n * LANES : (n + 1) * LANES, :] = jnp.transpose(
            tot_all[0:MODES, n * LANES : (n + 1) * LANES]
        )
    gskip_ref[...] = tot_all[MODES : MODES + 1, :]
    for copy in out_ex:
        copy.wait_recv()
    final_ref[...] = fin_pos[...]
    for copy in started:
        copy.wait_send()


def shards(mesh, *args):
    q, key_input, gate, cot, weight, rates, residues, skip = args
    zs, chans = mesh.shape["ctx"] // GROUP, mesh.shape["chan"]
    rows, width = q.shape
    depth = weight.shape[0]
    span = rows * GROUP
    length = rows * mesh.shape["ctx"]
    columns = zs * LANES
    vmem = pl.BlockSpec(memory_space=pltpu.VMEM)
    shape = jax.ShapeDtypeStruct
    outs = pl.pallas_call(
        functools.partial(kernel, zs, chans, length),
        out_shape=(
            shape((rows, width), bf16),
            shape((rows, width), bf16),
            shape((rows, width), bf16),
            shape((rows, width), bf16),
            shape((depth, LANES), bf16),
            shape((width, MODES), f32),
            shape((1, width), f32),
        ),
        in_specs=[vmem] * 8,
        out_specs=(vmem,) * 7,
        scratch_shapes=[
            pltpu.VMEM((rows, width), bf16),
            pltpu.VMEM((span, columns), bf16),
            pltpu.VMEM((depth, columns), bf16),
            pltpu.VMEM((span, LANES), bf16),
            pltpu.VMEM((span, LANES), bf16),
            pltpu.VMEM((span, LANES), f32),
            pltpu.VMEM((span, LANES), f32),
            pltpu.VMEM((span, LANES), f32),
            pltpu.VMEM((MODES, SUBS, LANES), f32),
            pltpu.VMEM((MODES, SUBS, LANES), f32),
            pltpu.VMEM((zs, MODES, LANES), f32),
            pltpu.VMEM((zs, MODES, LANES), f32),
            pltpu.VMEM((zs, MODES + 8, LANES), f32),
            pltpu.VMEM((span, width), bf16),
            pltpu.VMEM((span, LANES), f32),
            pltpu.VMEM((3, span, LANES), bf16),
            pltpu.VMEM((3, span, LANES), bf16),
            pltpu.VMEM((span, LANES), f32),
            pltpu.VMEM((span, columns), bf16),
            pltpu.VMEM((chans - 1, span, LANES), bf16),
            pltpu.VMEM((span, LANES), bf16),
            pltpu.VMEM((rows, width), bf16),
            pltpu.VMEM((depth, columns), bf16),
            pltpu.VMEM((14, depth // 2, LANES), bf16),
            pltpu.VMEM((span, LANES), bf16),
            pltpu.VMEM((rows, width), bf16),
            pltpu.VMEM((span, LANES), bf16),
            pltpu.VMEM((rows, width), bf16),
            pltpu.VMEM((MODES + 8, width), f32),
            pltpu.SemaphoreType.DMA((COPIES,)),
            pltpu.SemaphoreType.DMA((COPIES,)),
        ],
        compiler_params=pltpu.CompilerParams(
            collective_id=0, has_side_effects=True, vmem_limit_bytes=48 * 2**20
        ),
    )(q, key_input, gate, cot, weight, rates, residues, skip.reshape(1, -1))
    return (*outs[:6], outs[6].reshape(-1))


def solution(mesh):
    placed = (
        P("ctx", "chan"),
        P("ctx", "chan"),
        P("ctx", "chan"),
        P("ctx", "chan"),
        P("chan", "ctx"),
        P("chan", None),
        P("chan", None),
        P("chan"),
    )
    return jax.shard_map(
        functools.partial(shards, mesh),
        mesh=mesh,
        in_specs=placed,
        out_specs=(
            P("ctx", "chan"),
            P("ctx", "chan"),
            P("ctx", "chan"),
            P("ctx", "chan"),
            P("chan", "ctx"),
            P("chan", None),
            P("chan"),
        ),
        check_vma=False,
    )
```

```python
import functools
import math

import jax
import jax.numpy as jnp
from jax import lax
from jax.experimental import pallas as pl
from jax.experimental.pallas import tpu as pltpu
from jax.sharding import PartitionSpec as P

MESH = pl.DeviceIdType.MESH
f32 = jnp.float32
bf16 = jnp.bfloat16

GROUP = 4
PAIR = 2
LANES = 128
SUBS = 8
MODES = 16


def one_minus_exp(x):
    series = jnp.ones_like(x)
    for n in range(9, 1, -1):
        series = 1.0 - x * (1.0 / n) * series
    return jnp.where(x < 0.5, x * series, 1.0 - jnp.exp(-x))


def kernel(
    zs, chans, length,
    q_hbm, key_hbm, gate_hbm, cot_hbm, w_hbm, rate_hbm, res_hbm, skip_hbm,
    final_ref, gq_ref, gk_ref, gg_ref, gw_ref, gres_ref, gskip_ref,
    q_ref, key_ref, gate_ref, cot_ref, w_ref, rate_ref, res_ref, skip_ref,
    gat_s, cotall, wall, xg, gateg, x_f, co_f, cg_f, pre_f, pre_b, e_all, b_all, l_all,
    mixed_all, og_acc, og_send, og_recv, fp, frecv, fin_y, fin_pos, gp, rsbuf,
    ggrp, ggpos, gates_g, tot_all, sizes,
    recv_sems, send_sems, load_sems,
):
    rows = q_ref.shape[0]
    span = rows * GROUP
    step_len = span // SUBS
    half = w_ref.shape[0] // 2
    ys = chans // PAIR
    wide = PAIR * LANES
    scale = 1.0 / math.sqrt(length)

    loads = [
        pltpu.make_async_copy(src, dst, load_sems.at[n])
        for n, (src, dst) in enumerate((
            (cot_hbm, cot_ref), (w_hbm, w_ref), (q_hbm, q_ref), (key_hbm, key_ref),
            (gate_hbm, gate_ref), (rate_hbm, rate_ref), (res_hbm, res_ref), (skip_hbm, skip_ref),
        ))
    ]
    for copy in loads:
        copy.start()

    i = lax.axis_index("ctx")
    j = lax.axis_index("chan")
    z = lax.div(i, GROUP)
    k = lax.rem(i, GROUP)
    y = lax.div(j, PAIR)
    xl = lax.rem(j, PAIR)
    k1 = k + 1 - 2 * lax.rem(k, 2)
    k2 = lax.rem(k + 2, GROUP)
    k3 = GROUP - 1 - k
    kp = {0: k, 1: k1, 2: k2, 3: k3}
    xp = {0: xl, 1: PAIR - 1 - xl}

    def zmod(d):
        return lax.rem(z + d + zs, zs)

    def ymod(d):
        return lax.rem(y + d + ys, ys)

    def x_peer(dk, dx):
        return {"ctx": z * GROUP + kp[dk], "chan": y * PAIR + xp[dx]}

    def z_peer(d):
        return {"ctx": zmod(d) * GROUP + k, "chan": j}

    def y_peer(d):
        return {"ctx": i, "chan": ymod(d) * PAIR + xl}

    x_order = [(dk, dx) for dk in (2, 3, 1, 0) for dx in (1, 0) if dk or dx]
    g_order = (2, 3, 1)
    z_order = [zs // 2] + [d for n in range(zs // 2 - 1, 0, -1) for d in (n, -n)]

    def lane(index):
        return pl.ds(pl.multiple_of(index * LANES, LANES), LANES)

    def pair(index):
        return pl.ds(pl.multiple_of(index * wide, wide), wide)

    def row(index):
        return pl.ds(pl.multiple_of(index * rows, rows), rows)

    counts = [0, 0]
    sent = []

    class Batch:
        def __init__(self, lane_class):
            self.recv = recv_sems.at[counts[0]]
            counts[0] += 1
            self.out = lane_class
            self.units = 0

        def send(self, src, dst, peer, units):
            pltpu.make_async_remote_copy(
                src_ref=src, dst_ref=dst, send_sem=self.out.sem, recv_sem=self.recv,
                device_id=peer, device_id_type=MESH,
            ).start()
            self.units += units
            self.out.units += units

        def wait(self):
            part = sizes.at[pl.ds(0, self.units)]
            pltpu.make_async_copy(part, part, self.recv).wait()

    class Outgoing:
        def __init__(self):
            self.sem = send_sems.at[counts[1]]
            counts[1] += 1
            self.units = 0
            sent.append(self)

        def wait(self):
            part = sizes.at[pl.ds(0, self.units)]
            pltpu.make_async_copy(part, part, self.sem).wait()

    block_u = rows // 16
    out_x, out_y, out_z, out_zs, out_s = (Outgoing() for _ in range(5))

    barrier = pltpu.get_barrier_semaphore()
    peers = [x_peer(*d) for d in x_order]
    peers += [z_peer(d) for d in z_order]
    peers += [y_peer(d) for d in range(1, ys)]
    for peer in peers:
        pl.semaphore_signal(barrier, inc=1, device_id=peer, device_id_type=MESH)

    for copy in loads:
        copy.wait()
    rate = rate_ref[:, lane(k)]
    inv_norm = jnp.sqrt(one_minus_exp(2.0 * rate) / one_minus_exp(2.0 * length * rate))
    gain = res_ref[:, lane(k)] * inv_norm
    decay = jnp.exp(-rate)
    decay_sub = jnp.exp(-step_len * rate)
    decay_span = jnp.exp(-span * rate)
    skip_b = jnp.broadcast_to(skip_ref[:, lane(k)], (SUBS, LANES))
    sub = lax.broadcasted_iota(jnp.int32, (SUBS, LANES), 0)

    def spread(table, m):
        return jnp.broadcast_to(table[m : m + 1, :], (SUBS, LANES))

    gat_s[...] = (q_ref[...].astype(f32) * key_ref[...].astype(f32)).astype(bf16)
    pl.semaphore_wait(barrier, len(peers))

    chunk = (pl.ds(0, half), pl.ds(half, half))
    ways = {0: ((1, 0, zs // 2), (-1, 1, zs // 2)), 1: ((1, 1, zs // 2 - 1), (-1, 0, zs // 2 - 1))}
    ring = {}
    chunk_u = half // 16

    def weight_hop(h, long):
        if h > 1:
            ring[h - 1, long].wait()
        if h > ways[long][0][2]:
            return
        ring[h, long] = Batch(out_z)
        for d, c, hops in ways[long]:
            block = lane(zmod(-d * (h - 1)))
            src = w_ref.at[chunk[c], :] if h == 1 else wall.at[chunk[c], block]
            ring[h, long].send(src, wall.at[chunk[c], block], z_peer(d), chunk_u)

    cot_x = Batch(out_x)
    for dk, dx in x_order:
        cot_x.send(
            cot_ref.at[:, lane(kp[dk])], cotall.at[row(k), lane(j)], x_peer(dk, dx), block_u
        )
    weight_hop(1, 0)
    weight_hop(1, 1)
    signals = Batch(out_x)
    for d in g_order:
        signals.send(gat_s.at[:, lane(kp[d])], xg.at[row(k), :], x_peer(d, 0), block_u)
        signals.send(gate_ref.at[:, lane(kp[d])], gateg.at[row(k), :], x_peer(d, 0), block_u)
    cotall[row(k), lane(j)] = cot_ref[:, lane(k)]
    xg[row(k), :] = gat_s[:, lane(k)]
    gateg[row(k), :] = gate_ref[:, lane(k)]
    wall[:, lane(z)] = w_ref[...]

    weight_hop(2, 0)
    cot_x.wait()
    cot_near = Batch(out_y)
    for d in (1, -1):
        cot_near.send(cotall.at[:, pair(y)], cotall.at[:, pair(y)], y_peer(d), 8 * block_u)
    cot_far = Batch(out_y)
    cot_far.send(cotall.at[:, pair(y)], cotall.at[:, pair(y)], y_peer(2), 8 * block_u)
    weight_hop(2, 1)

    decays = [spread(decay, m) for m in range(MODES)]
    gains = [spread(gain, m) for m in range(MODES)]
    zero = jnp.zeros((SUBS, LANES), f32)

    def at_step(t):
        return pl.ds(t, SUBS, stride=step_len)

    def ends(src, backward):
        def body(s, state):
            t = step_len - 1 - s if backward else s
            value = src[at_step(t), :]
            return tuple(decays[m] * state[m] + value for m in range(MODES))

        return lax.fori_loop(0, step_len, body, (zero,) * MODES, unroll=4)

    def prefix(state, pre, backward, all_ref):
        for m in range(MODES):
            factor = spread(decay_sub, m)
            total = state[m]
            for shift in (1, 2, 4):
                moved = pltpu.roll(total, SUBS - shift if backward else shift, 0)
                keep = sub < SUBS - shift if backward else sub >= shift
                total = total + jnp.where(keep, factor * moved, 0.0)
                factor = factor * factor
            moved = pltpu.roll(total, SUBS - 1 if backward else 1, 0)
            pre[m] = jnp.where(sub < SUBS - 1 if backward else sub >= 1, moved, 0.0)
            edge = 0 if backward else SUBS - 1
            all_ref[z, m : m + 1, :] = total[edge : edge + 1, :]

    def carried(pre, all_ref, backward):
        carry = jnp.zeros((MODES, LANES), f32)
        for n in range(zs):
            other = zs - 1 - n if backward else n
            ahead = z < other if backward else z > other
            carry = jnp.where(ahead, decay_span * carry + all_ref[other], carry)
        steps = (SUBS - 1 - sub if backward else sub).astype(f32)
        return tuple(
            pre[m] + jnp.exp(-step_len * steps * spread(rate, m)) * spread(carry, m)
            for m in range(MODES)
        )

    def tree(terms):
        while len(terms) > 1:
            terms = [a + b for a, b in zip(terms[::2], terms[1::2])]
        return terms[0]

    def sweep(src, out, state, backward):
        def body(s, state):
            t = step_len - 1 - s if backward else s
            value = src[at_step(t), :]
            state = tuple(decays[m] * state[m] + value for m in range(MODES))
            out[at_step(t), :] = (
                tree([gains[m] * state[m] for m in range(MODES)]) + skip_b * value
            )
            return state

        lax.fori_loop(0, step_len, body, state, unroll=2)

    def to_z(ref, units):
        batch = Batch(out_zs)
        for d in z_order:
            batch.send(ref.at[z], ref.at[z], z_peer(d), units)
        return batch

    signals.wait()
    x_f[...] = xg[...].astype(f32)
    prefix(ends(x_f, False), pre_f, False, e_all)
    e_batch = to_z(e_all, 2)
    weight_hop(3, 0)
    weight_hop(3, 1)
    e_batch.wait()
    start_f = carried(pre_f, e_all, False)
    for m in range(MODES):
        pre_f[m] = start_f[m]
    sweep(x_f, co_f, start_f, False)
    mixed_all[:, lane(k)] = (gateg[...].astype(f32) * co_f[...]).astype(bf16)
    mix_2 = Batch(out_x)
    mix_2.send(mixed_all.at[:, lane(k)], mixed_all.at[:, lane(k)], x_peer(2, 0), 4 * block_u)
    mix_1 = Batch(out_x)
    mix_1.send(mixed_all.at[:, lane(k)], mixed_all.at[:, lane(k)], x_peer(1, 0), 4 * block_u)
    weight_hop(4, 0)
    mix_2.wait()
    mix_1.send(mixed_all.at[:, lane(k2)], mixed_all.at[:, lane(k2)], x_peer(1, 0), 4 * block_u)
    weight_hop(4, 1)
    weight_hop(5, 0)
    mix_1.wait()

    for n in range(ys):
        cols = slice(n * wide, (n + 1) * wide)
        fp[:, cols] = jnp.dot(
            mixed_all[...], wall[:, cols], preferred_element_type=f32
        ).astype(bf16)
    fin_batch = Batch(out_y)
    for d in (1, -1, 2):
        fin_batch.send(
            fp.at[:, pair(ymod(d))], frecv.at[{1: 0, -1: 1, 2: 2}[d]], y_peer(d), 8 * block_u
        )

    def out_grad_part(d):
        return lax.dot_general(
            cotall[:, pair(ymod(d))], wall[:, pair(ymod(d))], (((1,), (1,)), ((), ())),
            preferred_element_type=f32,
        )

    cot_near.wait()
    og_acc[...] = out_grad_part(0)
    og_acc[...] += out_grad_part(1)
    og_acc[...] += out_grad_part(-1)
    cot_far.wait()
    og_acc[...] += out_grad_part(2)
    og_a = Batch(out_x)
    og_send[0] = og_acc[:, lane(k3)].astype(bf16)
    og_a.send(og_send.at[0], og_recv.at[0], x_peer(1, 0), 4 * block_u)
    og_b = Batch(out_x)
    og_send[1] = og_acc[:, lane(k1)].astype(bf16)
    og_b.send(og_send.at[1], og_recv.at[1], x_peer(1, 0), 4 * block_u)

    for n in range(ys):
        cols = slice(n * wide, (n + 1) * wide)
        gp[:, cols] = lax.dot_general(
            mixed_all[...], cotall[:, cols], (((0,), (0,)), ((), ())),
            preferred_element_type=f32,
        ).astype(bf16)
    sums = {}
    slots = {}
    for h in range(1, zs // 2 + 1):
        for long in (0, 1):
            for d, c, hops in ways[long]:
                if h <= hops:
                    slots[d, c, h] = len(slots)

    def weight_sum_hop(h, long):
        if h > 1:
            sums[h - 1, long].wait()
        if h > ways[long][0][2]:
            return
        sums[h, long] = Batch(out_s)
        for d, c, hops in ways[long]:
            block = lane(zmod(d * (hops - h + 1)))
            if h == 1:
                src = gp.at[chunk[c], block]
            else:
                slot = slots[d, c, h - 1]
                rsbuf[slot] = (
                    rsbuf[slot].astype(f32) + gp[chunk[c], block].astype(f32)
                ).astype(bf16)
                src = rsbuf.at[slot]
            sums[h, long].send(src, rsbuf.at[slots[d, c, h]], z_peer(d), chunk_u)

    weight_sum_hop(1, 0)
    weight_sum_hop(1, 1)
    og_a.wait()
    og_send[2] = (og_acc[:, lane(k2)] + og_recv[0].astype(f32)).astype(bf16)
    og_c = Batch(out_x)
    og_c.send(og_send.at[2], og_recv.at[2], x_peer(2, 0), 4 * block_u)
    weight_sum_hop(2, 0)

    og_b.wait()
    og_c.wait()
    og = og_acc[:, lane(k)] + og_recv[1].astype(f32) + og_recv[2].astype(f32)
    og = og.astype(bf16).astype(f32)
    cg_f[...] = og * gateg[...].astype(f32)
    prefix(ends(cg_f, True), pre_b, True, b_all)
    b_batch = to_z(b_all, 2)
    weight_sum_hop(2, 1)
    gates_g[...] = (og * co_f[...]).astype(bf16)
    gate_batch = Batch(out_x)
    for d in g_order:
        gate_batch.send(gates_g.at[row(kp[d]), :], gg_ref.at[:, lane(k)], x_peer(d, 0), block_u)
    gg_ref[:, lane(k)] = gates_g[row(k), :]

    def residue_body(s, carry):
        state, sums_m = carry
        value = x_f[at_step(s), :]
        grad = cg_f[at_step(s), :]
        state = tuple(decays[m] * state[m] + value for m in range(MODES))
        return state, tuple(sums_m[m] + grad * state[m] for m in range(MODES))

    _, mode_sums = lax.fori_loop(
        0, step_len, residue_body,
        (tuple(pre_f[m] for m in range(MODES)), (zero,) * MODES), unroll=2,
    )
    for m in range(MODES):
        l_all[z, m : m + 1, :] = jnp.sum(mode_sums[m], axis=0, keepdims=True)
    l_all[z, MODES : MODES + 8, :] = jnp.broadcast_to(
        jnp.sum(cg_f[...] * x_f[...], axis=0, keepdims=True), (8, LANES)
    )
    l_batch = to_z(l_all, 3)
    weight_sum_hop(3, 0)

    b_batch.wait()
    sweep(cg_f, co_f, carried(pre_b, b_all, True), True)
    ggrp[...] = co_f[...].astype(bf16)
    gg_batch = Batch(out_x)
    for d in g_order:
        gg_batch.send(ggrp.at[row(kp[d]), :], ggpos.at[:, lane(k)], x_peer(d, 0), block_u)
    ggpos[:, lane(k)] = ggrp[row(k), :]
    weight_sum_hop(3, 1)
    l_batch.wait()
    total = l_all[0]
    for n in range(1, zs):
        total = total + l_all[n]
    tot_all[0:MODES, lane(k)] = total[0:MODES] * inv_norm * scale
    tot_all[MODES : MODES + 8, lane(k)] = total[MODES : MODES + 8] * scale
    tot_batch = Batch(out_zs)
    for d in g_order:
        tot_batch.send(tot_all.at[:, lane(k)], tot_all.at[:, lane(k)], x_peer(d, 0), 3)
    weight_sum_hop(4, 0)

    fin_batch.wait()
    fin = fp[:, pair(y)].astype(f32)
    for n in range(ys - 1):
        fin = fin + frecv[n].astype(f32)
    fin_y[...] = fin.astype(bf16)
    out_batch = Batch(out_x)
    for dk, dx in x_order:
        out_batch.send(
            fin_y.at[row(kp[dk]), lane(xp[dx])], fin_pos.at[xl, :, lane(k)],
            x_peer(dk, dx), block_u,
        )
    fin_pos[xl, :, lane(k)] = fin_y[row(k), lane(xl)]

    gg_batch.wait()
    spread_grad = ggpos[...].astype(f32)
    gq_ref[...] = (spread_grad * key_ref[...].astype(f32)).astype(bf16)
    gk_ref[...] = (spread_grad * q_ref[...].astype(f32)).astype(bf16)
    gate_batch.wait()

    weight_sum_hop(4, 1)
    weight_sum_hop(5, 0)
    for c in (0, 1):
        part = gp[chunk[c], lane(z)].astype(f32)
        for long in (0, 1):
            for d, other, hops in ways[long]:
                if other == c:
                    part = part + rsbuf[slots[d, c, hops]].astype(f32)
        gw_ref[chunk[c], :] = (part * scale).astype(bf16)

    tot_batch.wait()
    gres_ref[...] = tot_all[0:MODES, :]
    gskip_ref[...] = tot_all[MODES : MODES + 1, :]
    out_batch.wait()
    final_ref[...] = (fin_pos[0].astype(f32) + fin_pos[1].astype(f32)).astype(bf16)
    for out in sent:
        out.wait()


def store_kernel(*refs):
    count = len(refs) // 2
    for n in range(count):
        refs[count + n][...] = refs[n][...]


def shards(mesh, *args):
    q, key_input, gate, cot, weight, rates, residues, skip = args
    zs, chans = mesh.shape["ctx"] // GROUP, mesh.shape["chan"]
    rows, width = q.shape
    depth = weight.shape[0]
    span = rows * GROUP
    length = rows * mesh.shape["ctx"]
    columns = zs * LANES
    vmem = pl.BlockSpec(memory_space=pltpu.VMEM)
    hbm = pl.BlockSpec(memory_space=pltpu.HBM)
    anywhere = pl.BlockSpec(memory_space=pl.ANY)
    shape = jax.ShapeDtypeStruct
    out_shape = (
        shape((rows, width), bf16),
        shape((rows, width), bf16),
        shape((rows, width), bf16),
        shape((rows, width), bf16),
        shape((depth, LANES), bf16),
        shape((MODES, width), f32),
        shape((1, width), f32),
    )
    outs = pl.pallas_call(
        functools.partial(kernel, zs, chans, length),
        out_shape=out_shape,
        in_specs=[hbm] * 8,
        out_specs=(vmem,) * 7,
        scratch_shapes=[
            pltpu.VMEM((rows, width), bf16),
            pltpu.VMEM((rows, width), bf16),
            pltpu.VMEM((rows, width), bf16),
            pltpu.VMEM((rows, width), bf16),
            pltpu.VMEM((depth, LANES), bf16),
            pltpu.VMEM((MODES, width), f32),
            pltpu.VMEM((MODES, width), f32),
            pltpu.VMEM((1, width), f32),
            pltpu.VMEM((rows, width), bf16),
            pltpu.VMEM((span, columns), bf16),
            pltpu.VMEM((depth, columns), bf16),
            pltpu.VMEM((span, LANES), bf16),
            pltpu.VMEM((span, LANES), bf16),
            pltpu.VMEM((span, LANES), f32),
            pltpu.VMEM((span, LANES), f32),
            pltpu.VMEM((span, LANES), f32),
            pltpu.VMEM((MODES, SUBS, LANES), f32),
            pltpu.VMEM((MODES, SUBS, LANES), f32),
            pltpu.VMEM((zs, MODES, LANES), f32),
            pltpu.VMEM((zs, MODES, LANES), f32),
            pltpu.VMEM((zs, MODES + 8, LANES), f32),
            pltpu.VMEM((span, width), bf16),
            pltpu.VMEM((span, width), f32),
            pltpu.VMEM((3, span, LANES), bf16),
            pltpu.VMEM((3, span, LANES), bf16),
            pltpu.VMEM((span, columns), bf16),
            pltpu.VMEM((chans // PAIR - 1, span, PAIR * LANES), bf16),
            pltpu.VMEM((span, PAIR * LANES), bf16),
            pltpu.VMEM((PAIR, rows, width), bf16),
            pltpu.VMEM((depth, columns), bf16),
            pltpu.VMEM((2 * (zs - 1), depth // 2, LANES), bf16),
            pltpu.VMEM((span, LANES), bf16),
            pltpu.VMEM((rows, width), bf16),
            pltpu.VMEM((span, LANES), bf16),
            pltpu.VMEM((MODES + 8, width), f32),
            pltpu.VMEM((512, 16, LANES), bf16),
            pltpu.SemaphoreType.DMA((32,)),
            pltpu.SemaphoreType.DMA((5,)),
            pltpu.SemaphoreType.DMA((8,)),
        ],
        compiler_params=pltpu.CompilerParams(
            collective_id=0, has_side_effects=True, vmem_limit_bytes=65000 * 1024
        ),
    )(q, key_input, gate, cot, weight, rates.T, residues.T, skip.reshape(1, -1))
    outs = pl.pallas_call(
        store_kernel,
        out_shape=out_shape,
        in_specs=[vmem] * 7,
        out_specs=(vmem,) * 7,
        compiler_params=pltpu.CompilerParams(vmem_limit_bytes=65000 * 1024),
    )(*outs)
    return (*outs[:5], outs[5].T, outs[6].reshape(-1))


def solution(mesh):
    placed = (
        P("ctx", "chan"),
        P("ctx", "chan"),
        P("ctx", "chan"),
        P("ctx", "chan"),
        P("chan", "ctx"),
        P("chan", None),
        P("chan", None),
        P("chan"),
    )
    return jax.shard_map(
        functools.partial(shards, mesh),
        mesh=mesh,
        in_specs=placed,
        out_specs=(
            P("ctx", "chan"),
            P("ctx", "chan"),
            P("ctx", "chan"),
            P("ctx", "chan"),
            P("chan", "ctx"),
            P("chan", None),
            P("chan"),
        ),
        check_vma=False,
    )
```

```python
import functools
import math

import jax
import jax.numpy as jnp
from jax import lax
from jax.experimental import pallas as pl
from jax.experimental.pallas import tpu as pltpu
from jax.sharding import PartitionSpec as P

MESH = pl.DeviceIdType.MESH
f32 = jnp.float32
bf16 = jnp.bfloat16

GROUP = 4
PAIR = 2
LANES = 128
SUBS = 8
MODES = 16


def one_minus_exp(x):
    series = jnp.ones_like(x)
    for n in range(9, 1, -1):
        series = 1.0 - x * (1.0 / n) * series
    return jnp.where(x < 0.5, x * series, 1.0 - jnp.exp(-x))


def kernel(
    zs, chans, length,
    q_hbm, key_hbm, gate_hbm, cot_hbm, w_hbm, rate_hbm, res_hbm, skip_hbm,
    final_hbm, gq_hbm, gk_hbm, gg_hbm, gw_hbm, gres_hbm, gskip_hbm,
    q_ref, key_ref, gate_ref, cot_ref, w_ref, rate_ref, res_ref, skip_ref,
    gat_s, cotall, wall, xg, gateg, x_f, co_f, cg_f, pre_f, pre_b, e_all, b_all, ends_s, l_all,
    mixed_all, og_acc, og_send, og_recv, fp, frecv, fin_y, fin_pos, gp, rsbuf,
    ggrp, ggpos, gates_g, tot_all, sizes,
    final_ref, gq_ref, gk_ref, gg_ref, gw_ref,
    recv_sems, send_sems, load_sems,
):
    rows = q_ref.shape[0]
    span = rows * GROUP
    step_len = span // SUBS
    half = w_ref.shape[0] // 2
    ys = chans // PAIR
    wide = PAIR * LANES
    scale = 1.0 / math.sqrt(length)

    i = lax.axis_index("ctx")
    j = lax.axis_index("chan")
    z = lax.div(i, GROUP)
    k = lax.rem(i, GROUP)
    y = lax.div(j, PAIR)
    xl = lax.rem(j, PAIR)
    k1 = k + 1 - 2 * lax.rem(k, 2)
    k2 = lax.rem(k + 2, GROUP)
    k3 = GROUP - 1 - k
    kp = {0: k, 1: k1, 2: k2, 3: k3}
    xp = {0: xl, 1: PAIR - 1 - xl}

    def zmod(d):
        return lax.rem(z + d + zs, zs)

    def ymod(d):
        return lax.rem(y + d + ys, ys)

    def x_peer(dk, dx):
        return {"ctx": z * GROUP + kp[dk], "chan": y * PAIR + xp[dx]}

    def z_peer(d):
        return {"ctx": zmod(d) * GROUP + k, "chan": j}

    def y_peer(d):
        return {"ctx": i, "chan": ymod(d) * PAIR + xl}

    x_order = [(dk, dx) for dk in (2, 3, 1, 0) for dx in (1, 0) if dk or dx]
    g_order = (2, 3, 1)
    z_order = [zs // 2] + [d for n in range(zs // 2 - 1, 0, -1) for d in (n, -n)]

    def lane(index):
        return pl.ds(pl.multiple_of(index * LANES, LANES), LANES)

    def pair(index):
        return pl.ds(pl.multiple_of(index * wide, wide), wide)

    def row(index):
        return pl.ds(pl.multiple_of(index * rows, rows), rows)

    counts = [0, 0]

    class Batch:
        def __init__(self, lane_class):
            self.recv = recv_sems.at[counts[0]]
            counts[0] += 1
            self.out = lane_class
            self.units = 0

        def send(self, src, dst, peer, units):
            pltpu.make_async_remote_copy(
                src_ref=src, dst_ref=dst, send_sem=self.out.sem, recv_sem=self.recv,
                device_id=peer, device_id_type=MESH,
            ).start()
            self.units += units
            self.out.units += units

        def wait(self):
            part = sizes.at[pl.ds(0, self.units)]
            pltpu.make_async_copy(part, part, self.recv).wait()

    class Outgoing:
        def __init__(self):
            self.sem = send_sems.at[counts[1]]
            counts[1] += 1
            self.units = 0

        def wait(self):
            part = sizes.at[pl.ds(0, self.units)]
            pltpu.make_async_copy(part, part, self.sem).wait()

    block_u = rows // 16
    out_x, out_y, out_z, out_zs, out_s, first_z = (
        Outgoing() for _ in range(6)
    )

    barrier = pltpu.get_barrier_semaphore()
    peers = [x_peer(*d) for d in x_order]
    peers += [z_peer(d) for d in z_order]
    peers += [y_peer(d) for d in range(1, ys)]
    for peer in peers:
        pl.semaphore_signal(barrier, inc=1, device_id=peer, device_id_type=MESH)

    loads = [
        pltpu.make_async_copy(src, dst, load_sems.at[n])
        for n, (src, dst) in enumerate((
            (cot_hbm, cot_ref), (w_hbm, w_ref), (q_hbm, q_ref), (key_hbm, key_ref),
            (gate_hbm, gate_ref), (rate_hbm, rate_ref), (res_hbm, res_ref), (skip_hbm, skip_ref),
        ))
    ]
    for copy in loads:
        copy.start()

    for copy in loads:
        copy.wait()
    rate = rate_ref[:, lane(k)]
    inv_norm = jnp.sqrt(one_minus_exp(2.0 * rate) / one_minus_exp(2.0 * length * rate))
    gain = res_ref[:, lane(k)] * inv_norm
    decay = jnp.exp(-rate)
    decay_sub = jnp.exp(-step_len * rate)
    decay_span = jnp.exp(-span * rate)
    skip_b = jnp.broadcast_to(skip_ref[:, lane(k)], (SUBS, LANES))
    sub = lax.broadcasted_iota(jnp.int32, (SUBS, LANES), 0)

    def spread(table, m):
        return jnp.broadcast_to(table[m : m + 1, :], (SUBS, LANES))

    gat_s[...] = (q_ref[...].astype(f32) * key_ref[...].astype(f32)).astype(bf16)
    pl.semaphore_wait(barrier, len(peers))

    chunk = (pl.ds(0, half), pl.ds(half, half))
    ways = {0: ((1, 0, zs // 2), (-1, 1, zs // 2)), 1: ((1, 1, zs // 2 - 1), (-1, 0, zs // 2 - 1))}
    ring = {}
    chunk_u = half // 16

    def weight_hop(h, long):
        if h > 1:
            ring[h - 1, long].wait()
        if h > ways[long][0][2]:
            return
        ring[h, long] = Batch(first_z if (h, long) == (1, 0) else out_z)
        for d, c, hops in ways[long]:
            block = lane(zmod(-d * (h - 1)))
            src = w_ref.at[chunk[c], :] if h == 1 else wall.at[chunk[c], block]
            ring[h, long].send(src, wall.at[chunk[c], block], z_peer(d), chunk_u)

    y_order = (2, 1, -1)
    signals = Batch(out_x)
    for d in g_order:
        signals.send(gat_s.at[:, lane(kp[d])], xg.at[row(k), :], x_peer(d, 0), block_u)
    cot_a = Batch(out_x)
    for d in g_order:
        cot_a.send(
            cot_ref.at[:, lane(kp[d])], cotall.at[row(k), lane(j)], x_peer(d, 0), block_u
        )
    cot_y = [Batch(out_y) for _ in range(3)]
    for d in y_order:
        cot_y[0].send(cot_ref.at[:, lane(k)], cotall.at[row(k), lane(j)], y_peer(d), block_u)
    weight_hop(1, 0)
    cotall[row(k), lane(j)] = cot_ref[:, lane(k)]
    xg[row(k), :] = gat_s[:, lane(k)]
    gateg[row(k), :] = gate_ref[:, lane(k)]
    wall[:, lane(z)] = w_ref[...]

    decays = [spread(decay, m) for m in range(MODES)]
    gains = [spread(gain, m) for m in range(MODES)]
    zero = jnp.zeros((SUBS, LANES), f32)

    def at_step(t):
        return pl.ds(t, SUBS, stride=step_len)

    def ends(src, backward):
        def body(s, state):
            t = step_len - 1 - s if backward else s
            value = src[at_step(t), :]
            return tuple(decays[m] * state[m] + value for m in range(MODES))

        return lax.fori_loop(0, step_len, body, (zero,) * MODES, unroll=4)

    def prefix(state, pre, backward, all_ref):
        for m in range(MODES):
            factor = spread(decay_sub, m)
            total = state[m]
            for shift in (1, 2, 4):
                moved = pltpu.roll(total, SUBS - shift if backward else shift, 0)
                keep = sub < SUBS - shift if backward else sub >= shift
                total = total + jnp.where(keep, factor * moved, 0.0)
                factor = factor * factor
            moved = pltpu.roll(total, SUBS - 1 if backward else 1, 0)
            pre[m] = jnp.where(sub < SUBS - 1 if backward else sub >= 1, moved, 0.0)
            edge = 0 if backward else SUBS - 1
            ends_s[m : m + 1, :] = total[edge : edge + 1, :]
        all_ref[z] = ends_s[...].astype(bf16)

    def carried(pre, all_ref, backward):
        carry = jnp.zeros((MODES, LANES), f32)
        for n in range(zs):
            other = zs - 1 - n if backward else n
            ahead = z < other if backward else z > other
            carry = jnp.where(ahead, decay_span * carry + all_ref[other].astype(f32), carry)
        steps = (SUBS - 1 - sub if backward else sub).astype(f32)
        return tuple(
            pre[m] + jnp.exp(-step_len * steps * spread(rate, m)) * spread(carry, m)
            for m in range(MODES)
        )

    def tree(terms):
        while len(terms) > 1:
            terms = [a + b for a, b in zip(terms[::2], terms[1::2])]
        return terms[0]

    def sweep(src, out, state, backward):
        def body(s, state):
            t = step_len - 1 - s if backward else s
            value = src[at_step(t), :]
            state = tuple(decays[m] * state[m] + value for m in range(MODES))
            out[at_step(t), :] = (
                tree([gains[m] * state[m] for m in range(MODES)]) + skip_b * value
            )
            return state

        lax.fori_loop(0, step_len, body, state, unroll=4)

    def to_z(ref, units):
        batch = Batch(out_zs)
        for d in z_order:
            batch.send(ref.at[z], ref.at[z], z_peer(d), units)
        return batch

    first_z.wait()
    weight_hop(1, 1)
    cot_b = Batch(out_x)
    for dk in (1, 3, 2, 0):
        cot_b.send(
            cot_ref.at[:, lane(kp[dk])], cotall.at[row(k), lane(j)], x_peer(dk, 1), block_u
        )
    weight_hop(2, 0)
    gates_in = Batch(out_x)
    for d in g_order:
        gates_in.send(gate_ref.at[:, lane(kp[d])], gateg.at[row(k), :], x_peer(d, 0), block_u)
    cot_a.wait()
    for dy in y_order:
        for d in (1, 2, 3):
            piece = (row(kp[d]), lane(j))
            cot_y[1].send(cotall.at[piece], cotall.at[piece], y_peer(dy), block_u)
    signals.wait()
    weight_hop(2, 1)
    x_f[...] = xg[...].astype(f32)
    prefix(ends(x_f, False), pre_f, False, e_all)
    e_batch = to_z(e_all, 1)
    cot_b.wait()
    other = (slice(None), lane(y * PAIR + xp[1]))
    for dy in y_order:
        cot_y[2].send(cotall.at[other], cotall.at[other], y_peer(dy), 4 * block_u)
    weight_hop(3, 0)
    weight_hop(3, 1)
    e_batch.wait()
    start_f = carried(pre_f, e_all, False)
    for m in range(MODES):
        pre_f[m] = start_f[m]
    sweep(x_f, co_f, start_f, False)
    gates_in.wait()
    mixed_all[:, lane(k)] = (gateg[...].astype(f32) * co_f[...]).astype(bf16)
    mix_2 = Batch(out_x)
    mix_2.send(mixed_all.at[:, lane(k)], mixed_all.at[:, lane(k)], x_peer(2, 0), 4 * block_u)
    mix_1 = Batch(out_x)
    mix_1.send(mixed_all.at[:, lane(k)], mixed_all.at[:, lane(k)], x_peer(1, 0), 4 * block_u)
    weight_hop(4, 0)
    mix_2.wait()
    mix_1.send(mixed_all.at[:, lane(k2)], mixed_all.at[:, lane(k2)], x_peer(1, 0), 4 * block_u)
    weight_hop(4, 1)
    weight_hop(5, 0)
    def out_grad_part(d):
        return lax.dot_general(
            cotall[:, pair(ymod(d))], wall[:, pair(ymod(d))], (((1,), (1,)), ((), ())),
            preferred_element_type=f32,
        )

    og_acc[...] = out_grad_part(0)
    for batch in cot_y:
        batch.wait()
    og_acc[...] += out_grad_part(1)
    og_acc[...] += out_grad_part(-1)
    og_acc[...] += out_grad_part(2)
    og_a = Batch(out_x)
    og_send[0] = og_acc[:, lane(k3)].astype(bf16)
    og_a.send(og_send.at[0], og_recv.at[0], x_peer(1, 0), 4 * block_u)
    og_b = Batch(out_x)
    og_send[1] = og_acc[:, lane(k1)].astype(bf16)
    og_b.send(og_send.at[1], og_recv.at[1], x_peer(1, 0), 4 * block_u)

    mix_1.wait()

    for n in range(ys):
        cols = slice(n * wide, (n + 1) * wide)
        fp[:, cols] = jnp.dot(
            mixed_all[...], wall[:, cols], preferred_element_type=f32
        ).astype(bf16)
    fin_batch = Batch(out_y)
    for d in (1, -1, 2):
        fin_batch.send(
            fp.at[:, pair(ymod(d))], frecv.at[{1: 0, -1: 1, 2: 2}[d]], y_peer(d), 8 * block_u
        )

    og_a.wait()
    og_send[2] = (og_acc[:, lane(k2)] + og_recv[0].astype(f32)).astype(bf16)
    og_c = Batch(out_x)
    og_c.send(og_send.at[2], og_recv.at[2], x_peer(2, 0), 4 * block_u)
    for n in range(ys):
        cols = slice(n * wide, (n + 1) * wide)
        gp[:, cols] = lax.dot_general(
            mixed_all[...], cotall[:, cols], (((0,), (0,)), ((), ())),
            preferred_element_type=f32,
        ).astype(bf16)
    sums = {}
    slots = {}
    for h in range(1, zs // 2 + 1):
        for long in (0, 1):
            for d, c, hops in ways[long]:
                if h <= hops:
                    slots[d, c, h] = len(slots)

    def weight_sum_hop(h, long):
        if h > 1:
            sums[h - 1, long].wait()
        if h > ways[long][0][2]:
            return
        sums[h, long] = Batch(out_s)
        for d, c, hops in ways[long]:
            block = lane(zmod(d * (hops - h + 1)))
            if h == 1:
                src = gp.at[chunk[c], block]
            else:
                slot = slots[d, c, h - 1]
                rsbuf[slot] = (
                    rsbuf[slot].astype(f32) + gp[chunk[c], block].astype(f32)
                ).astype(bf16)
                src = rsbuf.at[slot]
            sums[h, long].send(src, rsbuf.at[slots[d, c, h]], z_peer(d), chunk_u)

    weight_sum_hop(1, 0)
    weight_sum_hop(1, 1)
    weight_sum_hop(2, 0)

    weight_sum_hop(2, 1)
    og_b.wait()
    og_c.wait()
    og = og_acc[:, lane(k)] + og_recv[1].astype(f32) + og_recv[2].astype(f32)
    og = og.astype(bf16).astype(f32)
    cg_f[...] = og * gateg[...].astype(f32)
    prefix(ends(cg_f, True), pre_b, True, b_all)
    b_batch = to_z(b_all, 1)
    gates_g[...] = (og * co_f[...]).astype(bf16)
    gate_batch = Batch(out_x)
    for d in g_order:
        gate_batch.send(gates_g.at[row(kp[d]), :], gg_ref.at[:, lane(k)], x_peer(d, 0), block_u)
    gg_ref[:, lane(k)] = gates_g[row(k), :]

    def residue_body(s, carry):
        state, sums_m = carry
        value = x_f[at_step(s), :]
        grad = cg_f[at_step(s), :]
        state = tuple(decays[m] * state[m] + value for m in range(MODES))
        return state, tuple(sums_m[m] + grad * state[m] for m in range(MODES))

    _, mode_sums = lax.fori_loop(
        0, step_len, residue_body,
        (tuple(pre_f[m] for m in range(MODES)), (zero,) * MODES), unroll=4,
    )
    for m in range(MODES):
        l_all[z, m : m + 1, :] = jnp.sum(mode_sums[m], axis=0, keepdims=True)
    l_all[z, MODES : MODES + 8, :] = jnp.broadcast_to(
        jnp.sum(cg_f[...] * x_f[...], axis=0, keepdims=True), (8, LANES)
    )
    l_batch = to_z(l_all, 3)
    weight_sum_hop(3, 0)

    weight_sum_hop(3, 1)
    b_batch.wait()
    sweep(cg_f, co_f, carried(pre_b, b_all, True), True)
    ggrp[...] = co_f[...].astype(bf16)
    gg_batch = Batch(out_x)
    for d in g_order:
        gg_batch.send(ggrp.at[row(kp[d]), :], ggpos.at[:, lane(k)], x_peer(d, 0), block_u)
    ggpos[:, lane(k)] = ggrp[row(k), :]
    weight_sum_hop(4, 0)

    fin_batch.wait()
    fin = fp[:, pair(y)].astype(f32)
    for n in range(ys - 1):
        fin = fin + frecv[n].astype(f32)
    fin_y[...] = fin.astype(bf16)
    out_batch = Batch(out_x)
    for dk, dx in x_order:
        out_batch.send(
            fin_y.at[row(kp[dk]), lane(xp[dx])], fin_pos.at[xl, :, lane(k)],
            x_peer(dk, dx), block_u,
        )
    fin_pos[xl, :, lane(k)] = fin_y[row(k), lane(xl)]

    l_batch.wait()
    total = l_all[0]
    for n in range(1, zs):
        total = total + l_all[n]
    tot_all[0:MODES, lane(k)] = total[0:MODES] * inv_norm * scale
    tot_all[MODES : MODES + 8, lane(k)] = total[MODES : MODES + 8] * scale
    tot_batch = Batch(out_zs)
    for d in g_order:
        tot_batch.send(tot_all.at[:, lane(k)], tot_all.at[:, lane(k)], x_peer(d, 0), 3)
    writes = []

    def write(n, src, dst):
        copy = pltpu.make_async_copy(src, dst, load_sems.at[n])
        copy.start()
        writes.append(copy)

    gg_batch.wait()
    spread_grad = ggpos[...].astype(f32)
    gq_ref[...] = (spread_grad * key_ref[...].astype(f32)).astype(bf16)
    gk_ref[...] = (spread_grad * q_ref[...].astype(f32)).astype(bf16)
    write(1, gq_ref, gq_hbm)
    write(2, gk_ref, gk_hbm)
    gate_batch.wait()
    write(3, gg_ref, gg_hbm)

    weight_sum_hop(4, 1)
    weight_sum_hop(5, 0)
    for c in (0, 1):
        part = gp[chunk[c], lane(z)].astype(f32)
        for long in (0, 1):
            for d, other, hops in ways[long]:
                if other == c:
                    part = part + rsbuf[slots[d, c, hops]].astype(f32)
        gw_ref[chunk[c], :] = (part * scale).astype(bf16)
    write(4, gw_ref, gw_hbm)

    tot_batch.wait()
    write(5, tot_all.at[pl.ds(0, MODES), :], gres_hbm)
    write(6, tot_all.at[pl.ds(MODES, 1), :], gskip_hbm)
    out_batch.wait()
    final_ref[...] = (fin_pos[0].astype(f32) + fin_pos[1].astype(f32)).astype(bf16)
    write(0, final_ref, final_hbm)
    for out in (out_x, out_y, out_z, out_zs, out_s):
        out.wait()
    for copy in writes:
        copy.wait()


def store_kernel(*refs):
    count = (len(refs) - 2) // 3
    srcs, dsts, bufs = refs[:count], refs[count : 2 * count], refs[2 * count : 3 * count]
    in_sems, out_sems = refs[3 * count :]
    reads = [pltpu.make_async_copy(srcs[n], bufs[n], in_sems.at[n]) for n in range(count)]
    writes = [pltpu.make_async_copy(bufs[n], dsts[n], out_sems.at[n]) for n in range(count)]
    for copy in reads:
        copy.start()
    for read, write in zip(reads, writes):
        read.wait()
        write.start()
    for copy in writes:
        copy.wait()


def shards(mesh, *args):
    q, key_input, gate, cot, weight, rates, residues, skip = args
    zs, chans = mesh.shape["ctx"] // GROUP, mesh.shape["chan"]
    rows, width = q.shape
    depth = weight.shape[0]
    span = rows * GROUP
    length = rows * mesh.shape["ctx"]
    columns = zs * LANES
    hbm = pl.BlockSpec(memory_space=pltpu.HBM)
    shape = jax.ShapeDtypeStruct
    out_shape = (
        shape((rows, width), bf16),
        shape((rows, width), bf16),
        shape((rows, width), bf16),
        shape((rows, width), bf16),
        shape((depth, LANES), bf16),
        shape((MODES, width), f32),
        shape((1, width), f32),
    )
    outs = pl.pallas_call(
        functools.partial(kernel, zs, chans, length),
        out_shape=out_shape,
        in_specs=[hbm] * 8,
        out_specs=(hbm,) * 7,
        scratch_shapes=[
            pltpu.VMEM((rows, width), bf16),
            pltpu.VMEM((rows, width), bf16),
            pltpu.VMEM((rows, width), bf16),
            pltpu.VMEM((rows, width), bf16),
            pltpu.VMEM((depth, LANES), bf16),
            pltpu.VMEM((MODES, width), f32),
            pltpu.VMEM((MODES, width), f32),
            pltpu.VMEM((1, width), f32),
            pltpu.VMEM((rows, width), bf16),
            pltpu.VMEM((span, columns), bf16),
            pltpu.VMEM((depth, columns), bf16),
            pltpu.VMEM((span, LANES), bf16),
            pltpu.VMEM((span, LANES), bf16),
            pltpu.VMEM((span, LANES), f32),
            pltpu.VMEM((span, LANES), f32),
            pltpu.VMEM((span, LANES), f32),
            pltpu.VMEM((MODES, SUBS, LANES), f32),
            pltpu.VMEM((MODES, SUBS, LANES), f32),
            pltpu.VMEM((zs, MODES, LANES), bf16),
            pltpu.VMEM((zs, MODES, LANES), bf16),
            pltpu.VMEM((MODES, LANES), f32),
            pltpu.VMEM((zs, MODES + 8, LANES), f32),
            pltpu.VMEM((span, width), bf16),
            pltpu.VMEM((span, width), f32),
            pltpu.VMEM((3, span, LANES), bf16),
            pltpu.VMEM((3, span, LANES), bf16),
            pltpu.VMEM((span, columns), bf16),
            pltpu.VMEM((chans // PAIR - 1, span, PAIR * LANES), bf16),
            pltpu.VMEM((span, PAIR * LANES), bf16),
            pltpu.VMEM((PAIR, rows, width), bf16),
            pltpu.VMEM((depth, columns), bf16),
            pltpu.VMEM((2 * (zs - 1), depth // 2, LANES), bf16),
            pltpu.VMEM((span, LANES), bf16),
            pltpu.VMEM((rows, width), bf16),
            pltpu.VMEM((span, LANES), bf16),
            pltpu.VMEM((MODES + 8, width), f32),
            pltpu.VMEM((512, 16, LANES), bf16),
            *[pltpu.VMEM(a.shape, a.dtype) for a in out_shape[:5]],
            pltpu.SemaphoreType.DMA((36,)),
            pltpu.SemaphoreType.DMA((6,)),
            pltpu.SemaphoreType.DMA((8,)),
        ],
        compiler_params=pltpu.CompilerParams(
            collective_id=0, has_side_effects=True, vmem_limit_bytes=65000 * 1024
        ),
    )(q, key_input, gate, cot, weight, rates.T, residues.T, skip.reshape(1, -1))
    outs = pl.pallas_call(
        store_kernel,
        out_shape=out_shape,
        in_specs=[hbm] * 7,
        out_specs=(hbm,) * 7,
        scratch_shapes=[
            *[pltpu.VMEM(a.shape, a.dtype) for a in out_shape],
            pltpu.SemaphoreType.DMA((7,)),
            pltpu.SemaphoreType.DMA((7,)),
        ],
        compiler_params=pltpu.CompilerParams(vmem_limit_bytes=65000 * 1024),
    )(*outs)
    return (*outs[:5], outs[5].T, outs[6].reshape(-1))


def solution(mesh):
    placed = (
        P("ctx", "chan"),
        P("ctx", "chan"),
        P("ctx", "chan"),
        P("ctx", "chan"),
        P("chan", "ctx"),
        P("chan", None),
        P("chan", None),
        P("chan"),
    )
    return jax.shard_map(
        functools.partial(shards, mesh),
        mesh=mesh,
        in_specs=placed,
        out_specs=(
            P("ctx", "chan"),
            P("ctx", "chan"),
            P("ctx", "chan"),
            P("ctx", "chan"),
            P("chan", "ctx"),
            P("chan", None),
            P("chan"),
        ),
        check_vma=False,
    )
```

```python
import functools
import math

import jax
import jax.numpy as jnp
from jax import lax
from jax.experimental import pallas as pl
from jax.experimental.pallas import tpu as pltpu
from jax.sharding import PartitionSpec as P

MESH = pl.DeviceIdType.MESH
f32 = jnp.float32
bf16 = jnp.bfloat16

GROUP = 4
PAIR = 2
LANES = 128
SUBS = 8
MODES = 16
RECEIVES = 38
SENDS = 6


def one_minus_exp(x):
    series = jnp.ones_like(x)
    for n in range(9, 1, -1):
        series = 1.0 - x * (1.0 / n) * series
    return jnp.where(x < 0.5, x * series, 1.0 - jnp.exp(-x))


def kernel(
    zs, chans, length,
    q_hbm, key_hbm, gate_hbm, cot_hbm, w_hbm, rate_hbm, res_hbm, skip_hbm,
    final_hbm, gq_hbm, gk_hbm, gg_hbm, gw_hbm, gres_hbm, gskip_hbm,
    q_ref, key_ref, gate_ref, cot_ref, w_ref, rate_ref, res_ref, skip_ref,
    gat_s, two_ref, cotall, wall, xg, gateg, x_f, co_f, cg_f, pre_f, pre_b, e_all, b_all, ends_s, l_s, l_all,
    mixed_all, og_acc, og_send, og_recv, fp, frecv, fin_y, fin_pos, gp, rsbuf,
    ggrp, ggpos, gates_g, tot_all, sizes,
    final_ref, gq_ref, gk_ref, gg_ref, gw_ref,
    recv_sems, send_sems, load_sems,
):
    rows = q_ref.shape[0]
    span = rows * GROUP
    step_len = span // SUBS
    half = w_ref.shape[0] // 2
    ys = chans // PAIR
    wide = PAIR * LANES
    scale = 1.0 / math.sqrt(length)

    i = lax.axis_index("ctx")
    j = lax.axis_index("chan")
    z = lax.div(i, GROUP)
    k = lax.rem(i, GROUP)
    y = lax.div(j, PAIR)
    xl = lax.rem(j, PAIR)
    k1 = k + 1 - 2 * lax.rem(k, 2)
    k2 = lax.rem(k + 2, GROUP)
    k3 = GROUP - 1 - k
    kp = {0: k, 1: k1, 2: k2, 3: k3}
    xp = {0: xl, 1: PAIR - 1 - xl}

    def zmod(d):
        return lax.rem(z + d + zs, zs)

    def ymod(d):
        return lax.rem(y + d + ys, ys)

    def x_peer(dk, dx):
        return {"ctx": z * GROUP + kp[dk], "chan": y * PAIR + xp[dx]}

    def z_peer(d):
        return {"ctx": zmod(d) * GROUP + k, "chan": j}

    def y_peer(d):
        return {"ctx": i, "chan": ymod(d) * PAIR + xl}

    x_order = [(dk, dx) for dk in (2, 3, 1, 0) for dx in (1, 0) if dk or dx]
    g_order = (2, 3, 1)
    z_order = [zs // 2] + [d for n in range(zs // 2 - 1, 0, -1) for d in (n, -n)]

    def lane(index):
        return pl.ds(pl.multiple_of(index * LANES, LANES), LANES)

    def pair(index):
        return pl.ds(pl.multiple_of(index * wide, wide), wide)

    def row(index):
        return pl.ds(pl.multiple_of(index * rows, rows), rows)

    counts = [0, 0]

    class Batch:
        def __init__(self, lane_class):
            self.recv = recv_sems.at[counts[0]]
            counts[0] += 1
            self.out = lane_class
            self.units = 0

        def send(self, src, dst, peer, units):
            pltpu.make_async_remote_copy(
                src_ref=src, dst_ref=dst, send_sem=self.out.sem, recv_sem=self.recv,
                device_id=peer, device_id_type=MESH,
            ).start()
            self.units += units
            self.out.units += units

        def wait(self):
            part = sizes.at[pl.ds(0, self.units)]
            pltpu.make_async_copy(part, part, self.recv).wait()

    class Outgoing:
        def __init__(self):
            self.sem = send_sems.at[counts[1]]
            counts[1] += 1
            self.units = 0

        def wait(self):
            part = sizes.at[pl.ds(0, self.units)]
            pltpu.make_async_copy(part, part, self.sem).wait()

    block_u = rows // 16
    out_x, out_y, out_z, out_zs, out_s, first_z = (
        Outgoing() for _ in range(6)
    )

    barrier = pltpu.get_barrier_semaphore()
    peers = [x_peer(*d) for d in x_order]
    peers += [z_peer(d) for d in z_order]
    peers += [y_peer(d) for d in range(1, ys)]
    for peer in peers:
        pl.semaphore_signal(barrier, inc=1, device_id=peer, device_id_type=MESH)

    loads = [
        pltpu.make_async_copy(src, dst, load_sems.at[n])
        for n, (src, dst) in enumerate((
            (cot_hbm, cot_ref), (w_hbm, w_ref), (q_hbm, q_ref), (key_hbm, key_ref),
            (gate_hbm, gate_ref), (rate_hbm, rate_ref), (res_hbm, res_ref), (skip_hbm, skip_ref),
        ))
    ]
    for copy in loads:
        copy.start()

    pl.semaphore_wait(barrier, len(peers))

    chunk = (pl.ds(0, half), pl.ds(half, half))
    ways = {0: ((1, 0, zs // 2), (-1, 1, zs // 2)), 1: ((1, 1, zs // 2 - 1), (-1, 0, zs // 2 - 1))}
    ring = {}
    chunk_u = half // 16

    def weight_hop(h, long):
        if h > 1:
            ring[h - 1, long].wait()
        if h > ways[long][0][2]:
            return
        ring[h, long] = Batch(first_z if (h, long) == (1, 0) else out_z)
        for d, c, hops in ways[long]:
            block = lane(zmod(-d * (h - 1)))
            src = w_hbm.at[chunk[c], :] if h == 1 else wall.at[chunk[c], block]
            ring[h, long].send(src, wall.at[chunk[c], block], z_peer(d), chunk_u)

    y_order = (2, 1, -1)
    cot_y = [Batch(out_y) for _ in range(3)]
    for d in (1, -1):
        cot_y[0].send(cot_hbm.at[:, lane(k)], cotall.at[row(k), lane(j)], y_peer(d), block_u)
    cot_two = Batch(out_y)
    cot_two.send(cot_hbm, two_ref, y_peer(2), 4 * block_u)
    weight_hop(1, 0)
    for copy in loads:
        copy.wait()
    gat_s[...] = (q_ref[...].astype(f32) * key_ref[...].astype(f32)).astype(bf16)
    signals = Batch(out_x)
    for d in g_order:
        signals.send(gat_s.at[:, lane(kp[d])], xg.at[row(k), :], x_peer(d, 0), block_u)
    cot_a = Batch(out_x)
    for d in g_order:
        cot_a.send(
            cot_hbm.at[:, lane(kp[d])], cotall.at[row(k), lane(j)], x_peer(d, 0), block_u
        )
    cotall[row(k), lane(j)] = cot_ref[:, lane(k)]
    xg[row(k), :] = gat_s[:, lane(k)]
    gateg[row(k), :] = gate_ref[:, lane(k)]
    wall[:, lane(z)] = w_ref[...]

    rate = rate_ref[:, lane(k)]
    inv_norm = jnp.sqrt(one_minus_exp(2.0 * rate) / one_minus_exp(2.0 * length * rate))
    gain = res_ref[:, lane(k)] * inv_norm
    decay = jnp.exp(-rate)
    decay_sub = jnp.exp(-step_len * rate)
    decay_span = jnp.exp(-span * rate)
    skip_b = jnp.broadcast_to(skip_ref[:, lane(k)], (SUBS, LANES))
    sub = lax.broadcasted_iota(jnp.int32, (SUBS, LANES), 0)

    def spread(table, m):
        return jnp.broadcast_to(table[m : m + 1, :], (SUBS, LANES))

    decays = [spread(decay, m) for m in range(MODES)]
    gains = [spread(gain, m) for m in range(MODES)]
    zero = jnp.zeros((SUBS, LANES), f32)

    def at_step(t):
        return pl.ds(t, SUBS, stride=step_len)

    def ends(src, backward):
        def body(s, state):
            t = step_len - 1 - s if backward else s
            value = src[at_step(t), :]
            return tuple(decays[m] * state[m] + value for m in range(MODES))

        return lax.fori_loop(0, step_len, body, (zero,) * MODES, unroll=4)

    def prefix(state, pre, backward, all_ref):
        for m in range(MODES):
            factor = spread(decay_sub, m)
            total = state[m]
            for shift in (1, 2, 4):
                moved = pltpu.roll(total, SUBS - shift if backward else shift, 0)
                keep = sub < SUBS - shift if backward else sub >= shift
                total = total + jnp.where(keep, factor * moved, 0.0)
                factor = factor * factor
            moved = pltpu.roll(total, SUBS - 1 if backward else 1, 0)
            pre[m] = jnp.where(sub < SUBS - 1 if backward else sub >= 1, moved, 0.0)
            edge = 0 if backward else SUBS - 1
            ends_s[m : m + 1, :] = total[edge : edge + 1, :]
        all_ref[z] = ends_s[...].astype(bf16)

    def carried(all_ref, backward):
        carry = jnp.zeros((MODES, LANES), f32)
        for n in range(zs):
            other = zs - 1 - n if backward else n
            ahead = z < other if backward else z > other
            carry = jnp.where(ahead, decay_span * carry + all_ref[other].astype(f32), carry)
        steps = (SUBS - 1 - sub if backward else sub).astype(f32)
        return tuple(
            jnp.exp(-step_len * steps * spread(rate, m)) * spread(carry, m)
            for m in range(MODES)
        )

    def tree(terms):
        while len(terms) > 1:
            terms = [a + b for a, b in zip(terms[::2], terms[1::2])]
        return terms[0]

    def sweep(src, out, state, backward):
        def body(s, state):
            t = step_len - 1 - s if backward else s
            value = src[at_step(t), :]
            state = tuple(decays[m] * state[m] + value for m in range(MODES))
            out[at_step(t), :] = (
                tree([gains[m] * state[m] for m in range(MODES)]) + skip_b * value
            )
            return state

        lax.fori_loop(0, step_len, body, state, unroll=4)

    def add_carried(out, state, backward):
        def body(s, state):
            t = step_len - 1 - s if backward else s
            state = tuple(decays[m] * state[m] for m in range(MODES))
            out[at_step(t), :] += tree(list(state))
            return state

        lax.fori_loop(0, step_len, body, tuple(gains[m] * state[m] for m in range(MODES)), unroll=4)

    def to_z(ref, units):
        batch = Batch(out_zs)
        for d in z_order:
            batch.send(ref.at[z], ref.at[z], z_peer(d), units)
        return batch

    first_z.wait()
    weight_hop(1, 1)
    cot_b = Batch(out_x)
    for dk in (1, 3, 2, 0):
        cot_b.send(
            cot_ref.at[:, lane(kp[dk])], cotall.at[row(k), lane(j)], x_peer(dk, 1), block_u
        )
    weight_hop(2, 0)
    gates_in = Batch(out_x)
    for d in g_order:
        gates_in.send(gate_ref.at[:, lane(kp[d])], gateg.at[row(k), :], x_peer(d, 0), block_u)
    signals.wait()
    x_f[...] = xg[...].astype(f32)
    prefix(ends(x_f, False), pre_f, False, e_all)
    e_batch = to_z(e_all, 1)
    cot_a.wait()
    for dy in (1, -1):
        for d in (1, 2, 3):
            piece = (row(kp[d]), lane(j))
            cot_y[1].send(cotall.at[piece], cotall.at[piece], y_peer(dy), block_u)
    weight_hop(2, 1)
    cot_b.wait()
    other = (slice(None), lane(y * PAIR + xp[1]))
    for dy in (1, -1):
        cot_y[2].send(cotall.at[other], cotall.at[other], y_peer(dy), 4 * block_u)
    cot_two.wait()
    cot_spread = Batch(out_x)
    j_two = lane(ymod(2) * PAIR + xl)
    for dk, dx in x_order:
        cot_spread.send(
            two_ref.at[:, lane(kp[dk])], cotall.at[row(k), j_two], x_peer(dk, dx), block_u
        )
    cotall[row(k), j_two] = two_ref[:, lane(k)]
    sweep(x_f, co_f, tuple(pre_f[m] for m in range(MODES)), False)
    weight_hop(3, 0)
    weight_hop(3, 1)
    e_batch.wait()
    start_f = carried(e_all, False)
    add_carried(co_f, start_f, False)
    gates_in.wait()
    mixed_all[:, lane(k)] = (gateg[...].astype(f32) * co_f[...]).astype(bf16)
    mix_2 = Batch(out_x)
    mix_2.send(mixed_all.at[:, lane(k)], mixed_all.at[:, lane(k)], x_peer(2, 0), 4 * block_u)
    mix_1 = Batch(out_x)
    mix_1.send(mixed_all.at[:, lane(k)], mixed_all.at[:, lane(k)], x_peer(1, 0), 4 * block_u)
    weight_hop(4, 0)
    for m in range(MODES):
        pre_f[m] += start_f[m]
    mix_2.wait()
    mix_1.send(mixed_all.at[:, lane(k2)], mixed_all.at[:, lane(k2)], x_peer(1, 0), 4 * block_u)
    weight_hop(4, 1)
    weight_hop(5, 0)
    side = span // 2
    sides = [pl.ds(h * side, side) for h in (0, 1)]

    def out_grad_part(h, d):
        return lax.dot_general(
            cotall[sides[h], pair(ymod(d))], wall[:, pair(ymod(d))], (((1,), (1,)), ((), ())),
            preferred_element_type=f32,
        )

    for h in (0, 1):
        og_acc[sides[h], :] = out_grad_part(h, 0)
    for batch in (*cot_y, cot_spread):
        batch.wait()
    og_a = [Batch(out_x), Batch(out_x)]
    og_b = Batch(out_x)
    for h in (0, 1):
        for d in (1, -1, 2):
            og_acc[sides[h], :] += out_grad_part(h, d)
        og_send[0, sides[h], :] = og_acc[sides[h], lane(k3)].astype(bf16)
        og_a[h].send(
            og_send.at[0, sides[h]], og_recv.at[0, sides[h]], x_peer(1, 0), 2 * block_u
        )
        og_send[1, sides[h], :] = og_acc[sides[h], lane(k1)].astype(bf16)
        og_b.send(
            og_send.at[1, sides[h]], og_recv.at[1, sides[h]], x_peer(1, 0), 2 * block_u
        )

    mix_1.wait()

    far_rows = pl.ds(pl.multiple_of((1 - lax.div(k, 2)) * side, side), side)
    near_rows = pl.ds(pl.multiple_of(lax.div(k, 2) * side, side), side)
    fin_parts = []

    def output_part(part_rows):
        for n in range(ys):
            cols = slice(n * wide, (n + 1) * wide)
            fp[part_rows, cols] = jnp.dot(
                mixed_all[part_rows, :], wall[:, cols], preferred_element_type=f32
            ).astype(bf16)
        batch = Batch(out_y)
        for d in y_order:
            batch.send(
                fp.at[part_rows, pair(ymod(d))],
                frecv.at[{1: 0, -1: 1, 2: 2}[d], part_rows, :], y_peer(d), 4 * block_u,
            )
        fin_parts.append(batch)

    output_part(far_rows)
    def weight_term(d):
        block = lane(zmod(d))
        gp[:, block] = lax.dot_general(
            mixed_all[...], cotall[:, block], (((0,), (0,)), ((), ())),
            preferred_element_type=f32,
        ).astype(bf16)

    sums = {}
    slots = {}
    for h in range(1, zs // 2 + 1):
        for long in (0, 1):
            for d, c, hops in ways[long]:
                if h <= hops:
                    slots[d, c, h] = len(slots)

    def weight_sum_hop(h, long):
        if h > 1:
            sums[h - 1, long].wait()
        if h > ways[long][0][2]:
            return
        sums[h, long] = Batch(out_s)
        for d, c, hops in ways[long]:
            block = lane(zmod(d * (hops - h + 1)))
            if h == 1:
                src = gp.at[chunk[c], block]
            else:
                slot = slots[d, c, h - 1]
                rsbuf[slot] = (
                    rsbuf[slot].astype(f32) + gp[chunk[c], block].astype(f32)
                ).astype(bf16)
                src = rsbuf.at[slot]
            sums[h, long].send(src, rsbuf.at[slots[d, c, h]], z_peer(d), chunk_u)

    weight_term(zs // 2)
    weight_sum_hop(1, 0)
    og_c = Batch(out_x)
    for h in (0, 1):
        og_a[h].wait()
        og_send[2, sides[h], :] = (
            og_acc[sides[h], lane(k2)] + og_recv[0, sides[h], :].astype(f32)
        ).astype(bf16)
        og_c.send(
            og_send.at[2, sides[h]], og_recv.at[2, sides[h]], x_peer(2, 0), 2 * block_u
        )
    output_part(near_rows)
    weight_term(zs // 2 - 1)
    weight_term(1 - zs // 2)
    weight_sum_hop(1, 1)
    for d in range(2 - zs // 2, zs // 2 - 1):
        weight_term(d)
    weight_sum_hop(2, 0)

    og_b.wait()
    og_c.wait()
    og = og_acc[:, lane(k)] + og_recv[1].astype(f32) + og_recv[2].astype(f32)
    og = og.astype(bf16).astype(f32)
    cg_f[...] = og * gateg[...].astype(f32)
    prefix(ends(cg_f, True), pre_b, True, b_all)
    b_batch = to_z(b_all, 1)
    weight_sum_hop(2, 1)
    gates_g[...] = (og * co_f[...]).astype(bf16)
    gate_batch = Batch(out_x)
    for d in g_order:
        gate_batch.send(gates_g.at[row(kp[d]), :], gg_ref.at[:, lane(k)], x_peer(d, 0), block_u)
    gg_ref[:, lane(k)] = gates_g[row(k), :]

    def residue_body(s, carry):
        state, sums_m = carry
        value = x_f[at_step(s), :]
        grad = cg_f[at_step(s), :]
        state = tuple(decays[m] * state[m] + value for m in range(MODES))
        return state, tuple(sums_m[m] + grad * state[m] for m in range(MODES))

    _, mode_sums = lax.fori_loop(
        0, step_len, residue_body,
        (tuple(pre_f[m] for m in range(MODES)), (zero,) * MODES), unroll=4,
    )
    for m in range(MODES):
        l_s[m : m + 1, :] = jnp.sum(mode_sums[m], axis=0, keepdims=True)
    skip_sum = jnp.broadcast_to(
        jnp.sum(cg_f[...] * x_f[...], axis=0, keepdims=True), (SUBS, LANES)
    )
    skip_high = skip_sum.astype(bf16).astype(f32)
    l_s[MODES : MODES + SUBS, :] = skip_high
    l_s[MODES + SUBS : MODES + 2 * SUBS, :] = skip_sum - skip_high
    l_all[z] = l_s[...].astype(bf16)
    weight_sum_hop(3, 0)

    l_batch = to_z(l_all, 2)
    sweep(cg_f, co_f, tuple(pre_b[m] for m in range(MODES)), True)
    out_batch = Batch(out_x)

    def finish(batch, part_rows, order):
        batch.wait()
        fin = fp[part_rows, pair(y)].astype(f32)
        for n in range(ys - 1):
            fin = fin + frecv[n, part_rows, :].astype(f32)
        fin_y[part_rows, :] = fin.astype(bf16)
        for dk, dx in order:
            out_batch.send(
                fin_y.at[row(kp[dk]), lane(xp[dx])], fin_pos.at[xl, :, lane(k)],
                x_peer(dk, dx), block_u,
            )

    finish(fin_parts[0], far_rows, [(dk, dx) for dk in (2, 3) for dx in (1, 0)])
    b_batch.wait()
    add_carried(co_f, carried(b_all, True), True)
    ggrp[...] = co_f[...].astype(bf16)
    gg_batch = Batch(out_x)
    for d in g_order:
        gg_batch.send(ggrp.at[row(kp[d]), :], ggpos.at[:, lane(k)], x_peer(d, 0), block_u)
    ggpos[:, lane(k)] = ggrp[row(k), :]
    weight_sum_hop(3, 1)
    finish(fin_parts[1], near_rows, [(0, 1), (1, 1), (1, 0)])
    fin_pos[xl, :, lane(k)] = fin_y[row(k), lane(xl)]

    weight_sum_hop(4, 0)

    l_batch.wait()
    total = l_all[0].astype(f32)
    for n in range(1, zs):
        total = total + l_all[n].astype(f32)
    tot_all[0:MODES, lane(k)] = total[0:MODES] * inv_norm * scale
    tot_all[MODES : MODES + SUBS, lane(k)] = (
        total[MODES : MODES + SUBS] + total[MODES + SUBS : MODES + 2 * SUBS]
    ) * scale
    tot_batch = Batch(out_zs)
    for d in g_order:
        tot_batch.send(tot_all.at[:, lane(k)], tot_all.at[:, lane(k)], x_peer(d, 0), 3)
    writes = []

    def write(n, src, dst):
        copy = pltpu.make_async_copy(src, dst, load_sems.at[n])
        copy.start()
        writes.append(copy)

    gg_batch.wait()
    spread_grad = ggpos[...].astype(f32)
    gq_ref[...] = (spread_grad * key_ref[...].astype(f32)).astype(bf16)
    gk_ref[...] = (spread_grad * q_ref[...].astype(f32)).astype(bf16)
    write(1, gq_ref, gq_hbm)
    write(2, gk_ref, gk_hbm)
    gate_batch.wait()
    write(3, gg_ref, gg_hbm)

    weight_sum_hop(4, 1)
    weight_sum_hop(5, 0)
    for c in (0, 1):
        part = gp[chunk[c], lane(z)].astype(f32)
        for long in (0, 1):
            for d, other, hops in ways[long]:
                if other == c:
                    part = part + rsbuf[slots[d, c, hops]].astype(f32)
        gw_ref[chunk[c], :] = (part * scale).astype(bf16)
    write(4, gw_ref, gw_hbm)

    tot_batch.wait()
    write(5, tot_all.at[pl.ds(0, MODES), :], gres_hbm)
    write(6, tot_all.at[pl.ds(MODES, 1), :], gskip_hbm)
    out_batch.wait()
    final_ref[...] = (fin_pos[0].astype(f32) + fin_pos[1].astype(f32)).astype(bf16)
    write(0, final_ref, final_hbm)
    for out in (out_x, out_y, out_z, out_zs, out_s):
        out.wait()
    for copy in writes:
        copy.wait()
    assert counts == [RECEIVES, SENDS], counts


def store_kernel(*refs):
    count = (len(refs) - 2) // 3
    srcs, dsts, bufs = refs[:count], refs[count : 2 * count], refs[2 * count : 3 * count]
    in_sems, out_sems = refs[3 * count :]
    reads = [pltpu.make_async_copy(srcs[n], bufs[n], in_sems.at[n]) for n in range(count)]
    writes = [pltpu.make_async_copy(bufs[n], dsts[n], out_sems.at[n]) for n in range(count)]
    for copy in reads:
        copy.start()
    for read, write in zip(reads, writes):
        read.wait()
        write.start()
    for copy in writes:
        copy.wait()


def shards(mesh, *args):
    q, key_input, gate, cot, weight, rates, residues, skip = args
    zs, chans = mesh.shape["ctx"] // GROUP, mesh.shape["chan"]
    rows, width = q.shape
    depth = weight.shape[0]
    span = rows * GROUP
    length = rows * mesh.shape["ctx"]
    columns = zs * LANES
    hbm = pl.BlockSpec(memory_space=pltpu.HBM)
    shape = jax.ShapeDtypeStruct
    out_shape = (
        shape((rows, width), bf16),
        shape((rows, width), bf16),
        shape((rows, width), bf16),
        shape((rows, width), bf16),
        shape((depth, LANES), bf16),
        shape((MODES, width), f32),
        shape((1, width), f32),
    )
    outs = pl.pallas_call(
        functools.partial(kernel, zs, chans, length),
        out_shape=out_shape,
        in_specs=[hbm] * 8,
        out_specs=(hbm,) * 7,
        scratch_shapes=[
            pltpu.VMEM((rows, width), bf16),
            pltpu.VMEM((rows, width), bf16),
            pltpu.VMEM((rows, width), bf16),
            pltpu.VMEM((rows, width), bf16),
            pltpu.VMEM((depth, LANES), bf16),
            pltpu.VMEM((MODES, width), f32),
            pltpu.VMEM((MODES, width), f32),
            pltpu.VMEM((1, width), f32),
            pltpu.VMEM((rows, width), bf16),
            pltpu.VMEM((rows, width), bf16),
            pltpu.VMEM((span, columns), bf16),
            pltpu.VMEM((depth, columns), bf16),
            pltpu.VMEM((span, LANES), bf16),
            pltpu.VMEM((span, LANES), bf16),
            pltpu.VMEM((span, LANES), f32),
            pltpu.VMEM((span, LANES), f32),
            pltpu.VMEM((span, LANES), f32),
            pltpu.VMEM((MODES, SUBS, LANES), f32),
            pltpu.VMEM((MODES, SUBS, LANES), f32),
            pltpu.VMEM((zs, MODES, LANES), bf16),
            pltpu.VMEM((zs, MODES, LANES), bf16),
            pltpu.VMEM((MODES, LANES), f32),
            pltpu.VMEM((MODES + 2 * SUBS, LANES), f32),
            pltpu.VMEM((zs, MODES + 2 * SUBS, LANES), bf16),
            pltpu.VMEM((span, width), bf16),
            pltpu.VMEM((span, width), f32),
            pltpu.VMEM((3, span, LANES), bf16),
            pltpu.VMEM((3, span, LANES), bf16),
            pltpu.VMEM((span, columns), bf16),
            pltpu.VMEM((chans // PAIR - 1, span, PAIR * LANES), bf16),
            pltpu.VMEM((span, PAIR * LANES), bf16),
            pltpu.VMEM((PAIR, rows, width), bf16),
            pltpu.VMEM((depth, columns), bf16),
            pltpu.VMEM((2 * (zs - 1), depth // 2, LANES), bf16),
            pltpu.VMEM((span, LANES), bf16),
            pltpu.VMEM((rows, width), bf16),
            pltpu.VMEM((span, LANES), bf16),
            pltpu.VMEM((MODES + 8, width), f32),
            pltpu.VMEM((512, 16, LANES), bf16),
            *[pltpu.VMEM(a.shape, a.dtype) for a in out_shape[:5]],
            pltpu.SemaphoreType.DMA((RECEIVES,)),
            pltpu.SemaphoreType.DMA((SENDS,)),
            pltpu.SemaphoreType.DMA((8,)),
        ],
        compiler_params=pltpu.CompilerParams(
            collective_id=0, has_side_effects=True, vmem_limit_bytes=65000 * 1024
        ),
    )(q, key_input, gate, cot, weight, rates.T, residues.T, skip.reshape(1, -1))
    outs = pl.pallas_call(
        store_kernel,
        out_shape=out_shape,
        in_specs=[hbm] * 7,
        out_specs=(hbm,) * 7,
        scratch_shapes=[
            *[pltpu.VMEM(a.shape, a.dtype) for a in out_shape],
            pltpu.SemaphoreType.DMA((7,)),
            pltpu.SemaphoreType.DMA((7,)),
        ],
        compiler_params=pltpu.CompilerParams(vmem_limit_bytes=65000 * 1024),
    )(*outs)
    return (*outs[:5], outs[5].T, outs[6].reshape(-1))


def solution(mesh):
    placed = (
        P("ctx", "chan"),
        P("ctx", "chan"),
        P("ctx", "chan"),
        P("ctx", "chan"),
        P("chan", "ctx"),
        P("chan", None),
        P("chan", None),
        P("chan"),
    )
    return jax.shard_map(
        functools.partial(shards, mesh),
        mesh=mesh,
        in_specs=placed,
        out_specs=(
            P("ctx", "chan"),
            P("ctx", "chan"),
            P("ctx", "chan"),
            P("ctx", "chan"),
            P("chan", "ctx"),
            P("chan", None),
            P("chan"),
        ),
        check_vma=False,
    )
```

```python
import functools
import math

import jax
import jax.numpy as jnp
from jax import lax
from jax.experimental import pallas as pl
from jax.experimental.pallas import tpu as pltpu
from jax.sharding import PartitionSpec as P

MESH = pl.DeviceIdType.MESH
f32 = jnp.float32
bf16 = jnp.bfloat16

GROUP = 4
PAIR = 2
LANES = 128
SUBS = 8
MODES = 16
RECEIVES = 39
SENDS = 7


def one_minus_exp(x):
    series = jnp.ones_like(x)
    for n in range(9, 1, -1):
        series = 1.0 - x * (1.0 / n) * series
    return jnp.where(x < 0.5, x * series, 1.0 - jnp.exp(-x))


def kernel(
    zs, chans, length,
    q_hbm, key_hbm, gate_hbm, cot_hbm, w_hbm, rate_hbm, res_hbm, skip_hbm,
    final_hbm, gq_hbm, gk_hbm, gg_hbm, gw_hbm, gres_hbm, gskip_hbm,
    q_ref, key_ref, gate_ref, cot_ref, w_ref, rate_ref, res_ref, skip_ref,
    gat_s, two_ref, cotall, wall, xg, gateg, x_f, co_f, cg_f, pre_f, pre_b, e_all, b_all, ends_s, l_s, l_all, skip_all, sizes_one,
    mixed_all, og_acc, og_send, og_recv, fp, frecv, fin_y, fin_pos, gp, rsbuf,
    ggrp, ggpos, gates_g, tot_all, sizes,
    final_ref, gq_ref, gk_ref, gg_ref, gw_ref,
    recv_sems, send_sems, load_sems,
):
    rows = q_ref.shape[0]
    span = rows * GROUP
    step_len = span // SUBS
    half = w_ref.shape[0] // 2
    ys = chans // PAIR
    wide = PAIR * LANES
    scale = 1.0 / math.sqrt(length)

    i = lax.axis_index("ctx")
    j = lax.axis_index("chan")
    z = lax.div(i, GROUP)
    k = lax.rem(i, GROUP)
    y = lax.div(j, PAIR)
    xl = lax.rem(j, PAIR)
    k1 = k + 1 - 2 * lax.rem(k, 2)
    k2 = lax.rem(k + 2, GROUP)
    k3 = GROUP - 1 - k
    kp = {0: k, 1: k1, 2: k2, 3: k3}
    xp = {0: xl, 1: PAIR - 1 - xl}

    def zmod(d):
        return lax.rem(z + d + zs, zs)

    def ymod(d):
        return lax.rem(y + d + ys, ys)

    def x_peer(dk, dx):
        return {"ctx": z * GROUP + kp[dk], "chan": y * PAIR + xp[dx]}

    def z_peer(d):
        return {"ctx": zmod(d) * GROUP + k, "chan": j}

    def y_peer(d):
        return {"ctx": i, "chan": ymod(d) * PAIR + xl}

    x_order = [(dk, dx) for dk in (2, 3, 1, 0) for dx in (1, 0) if dk or dx]
    g_order = (2, 3, 1)
    z_order = [zs // 2] + [d for n in range(zs // 2 - 1, 0, -1) for d in (n, -n)]

    def lane(index):
        return pl.ds(pl.multiple_of(index * LANES, LANES), LANES)

    def pair(index):
        return pl.ds(pl.multiple_of(index * wide, wide), wide)

    def row(index):
        return pl.ds(pl.multiple_of(index * rows, rows), rows)

    counts = [0, 0]

    class Batch:
        def __init__(self, lane_class):
            self.recv = recv_sems.at[counts[0]]
            counts[0] += 1
            self.out = lane_class
            self.units = 0

        def send(self, src, dst, peer, units):
            pltpu.make_async_remote_copy(
                src_ref=src, dst_ref=dst, send_sem=self.out.sem, recv_sem=self.recv,
                device_id=peer, device_id_type=MESH,
            ).start()
            self.units += units
            self.out.units += units

        def wait(self):
            part = self.out.sizes.at[pl.ds(0, self.units)]
            pltpu.make_async_copy(part, part, self.recv).wait()

    class Outgoing:
        def __init__(self, size_ref=sizes):
            self.sizes = size_ref
            self.sem = send_sems.at[counts[1]]
            counts[1] += 1
            self.units = 0

        def wait(self):
            part = self.sizes.at[pl.ds(0, self.units)]
            pltpu.make_async_copy(part, part, self.sem).wait()

    block_u = rows // 16
    out_x, out_y, out_z, out_zs, out_s, first_z = (
        Outgoing() for _ in range(6)
    )
    out_one = Outgoing(sizes_one)

    barrier = pltpu.get_barrier_semaphore()
    peers = [x_peer(*d) for d in x_order]
    peers += [z_peer(d) for d in z_order]
    peers += [y_peer(d) for d in range(1, ys)]
    for peer in peers:
        pl.semaphore_signal(barrier, inc=1, device_id=peer, device_id_type=MESH)

    loads = [
        pltpu.make_async_copy(src, dst, load_sems.at[n])
        for n, (src, dst) in enumerate((
            (cot_hbm, cot_ref), (w_hbm, w_ref), (q_hbm, q_ref), (key_hbm, key_ref),
            (gate_hbm, gate_ref), (rate_hbm, rate_ref), (res_hbm, res_ref), (skip_hbm, skip_ref),
        ))
    ]
    for copy in loads:
        copy.start()

    pl.semaphore_wait(barrier, len(peers))

    chunk = (pl.ds(0, half), pl.ds(half, half))
    ways = {0: ((1, 0, zs // 2), (-1, 1, zs // 2)), 1: ((1, 1, zs // 2 - 1), (-1, 0, zs // 2 - 1))}
    ring = {}
    chunk_u = half // 16

    def weight_hop(h, long):
        if h > 1:
            ring[h - 1, long].wait()
        if h > ways[long][0][2]:
            return
        ring[h, long] = Batch(first_z if (h, long) == (1, 0) else out_z)
        for d, c, hops in ways[long]:
            block = lane(zmod(-d * (h - 1)))
            src = w_hbm.at[chunk[c], :] if h == 1 else wall.at[chunk[c], block]
            ring[h, long].send(src, wall.at[chunk[c], block], z_peer(d), chunk_u)

    y_order = (2, 1, -1)
    cot_y = [Batch(out_y) for _ in range(3)]
    for d in (1, -1):
        cot_y[0].send(cot_hbm.at[:, lane(k)], cotall.at[row(k), lane(j)], y_peer(d), block_u)
    cot_two = Batch(out_y)
    cot_two.send(cot_hbm, two_ref, y_peer(2), 4 * block_u)
    weight_hop(1, 0)
    for copy in loads:
        copy.wait()
    gat_s[...] = (q_ref[...].astype(f32) * key_ref[...].astype(f32)).astype(bf16)
    signals = Batch(out_x)
    for d in g_order:
        signals.send(gat_s.at[:, lane(kp[d])], xg.at[row(k), :], x_peer(d, 0), block_u)
    cot_a = Batch(out_x)
    for d in g_order:
        cot_a.send(
            cot_hbm.at[:, lane(kp[d])], cotall.at[row(k), lane(j)], x_peer(d, 0), block_u
        )
    cotall[row(k), lane(j)] = cot_ref[:, lane(k)]
    xg[row(k), :] = gat_s[:, lane(k)]
    gateg[row(k), :] = gate_ref[:, lane(k)]
    wall[:, lane(z)] = w_ref[...]

    rate = rate_ref[:, lane(k)]
    inv_norm = jnp.sqrt(one_minus_exp(2.0 * rate) / one_minus_exp(2.0 * length * rate))
    gain = res_ref[:, lane(k)] * inv_norm
    decay = jnp.exp(-rate)
    decay_sub = jnp.exp(-step_len * rate)
    decay_span = jnp.exp(-span * rate)
    skip_b = jnp.broadcast_to(skip_ref[:, lane(k)], (SUBS, LANES))
    sub = lax.broadcasted_iota(jnp.int32, (SUBS, LANES), 0)

    def spread(table, m):
        return jnp.broadcast_to(table[m : m + 1, :], (SUBS, LANES))

    decays = [spread(decay, m) for m in range(MODES)]
    gains = [spread(gain, m) for m in range(MODES)]
    zero = jnp.zeros((SUBS, LANES), f32)

    def at_step(t):
        return pl.ds(t, SUBS, stride=step_len)

    def ends(src, backward):
        def body(s, state):
            t = step_len - 1 - s if backward else s
            value = src[at_step(t), :]
            return tuple(decays[m] * state[m] + value for m in range(MODES))

        return lax.fori_loop(0, step_len, body, (zero,) * MODES, unroll=4)

    def prefix(state, pre, backward, all_ref):
        for m in range(MODES):
            factor = spread(decay_sub, m)
            total = state[m]
            for shift in (1, 2, 4):
                moved = pltpu.roll(total, SUBS - shift if backward else shift, 0)
                keep = sub < SUBS - shift if backward else sub >= shift
                total = total + jnp.where(keep, factor * moved, 0.0)
                factor = factor * factor
            moved = pltpu.roll(total, SUBS - 1 if backward else 1, 0)
            pre[m] = jnp.where(sub < SUBS - 1 if backward else sub >= 1, moved, 0.0)
            edge = 0 if backward else SUBS - 1
            ends_s[m : m + 1, :] = total[edge : edge + 1, :]
        all_ref[z] = ends_s[...].astype(bf16)

    def carried(all_ref, backward):
        carry = jnp.zeros((MODES, LANES), f32)
        for n in range(zs):
            other = zs - 1 - n if backward else n
            ahead = z < other if backward else z > other
            carry = jnp.where(ahead, decay_span * carry + all_ref[other].astype(f32), carry)
        steps = (SUBS - 1 - sub if backward else sub).astype(f32)
        return tuple(
            jnp.exp(-step_len * steps * spread(rate, m)) * spread(carry, m)
            for m in range(MODES)
        )

    def tree(terms):
        while len(terms) > 1:
            terms = [a + b for a, b in zip(terms[::2], terms[1::2])]
        return terms[0]

    def sweep(src, out, state, backward):
        def body(s, state):
            t = step_len - 1 - s if backward else s
            value = src[at_step(t), :]
            state = tuple(decays[m] * state[m] + value for m in range(MODES))
            out[at_step(t), :] = (
                tree([gains[m] * state[m] for m in range(MODES)]) + skip_b * value
            )
            return state

        lax.fori_loop(0, step_len, body, state, unroll=4)

    def add_carried(out, state, backward):
        def body(s, state):
            t = step_len - 1 - s if backward else s
            state = tuple(decays[m] * state[m] for m in range(MODES))
            out[at_step(t), :] += tree(list(state))
            return state

        lax.fori_loop(0, step_len, body, tuple(gains[m] * state[m] for m in range(MODES)), unroll=4)

    def to_z(ref, units):
        batch = Batch(out_zs)
        for d in z_order:
            batch.send(ref.at[z], ref.at[z], z_peer(d), units)
        return batch

    first_z.wait()
    weight_hop(1, 1)
    cot_b = Batch(out_x)
    for dk in (1, 3, 2, 0):
        cot_b.send(
            cot_ref.at[:, lane(kp[dk])], cotall.at[row(k), lane(j)], x_peer(dk, 1), block_u
        )
    weight_hop(2, 0)
    gates_in = Batch(out_x)
    for d in g_order:
        gates_in.send(gate_ref.at[:, lane(kp[d])], gateg.at[row(k), :], x_peer(d, 0), block_u)
    signals.wait()
    x_f[...] = xg[...].astype(f32)
    prefix(ends(x_f, False), pre_f, False, e_all)
    e_batch = to_z(e_all, 1)
    cot_a.wait()
    for dy in (1, -1):
        for d in (1, 2, 3):
            piece = (row(kp[d]), lane(j))
            cot_y[1].send(cotall.at[piece], cotall.at[piece], y_peer(dy), block_u)
    weight_hop(2, 1)
    cot_b.wait()
    other = (slice(None), lane(y * PAIR + xp[1]))
    for dy in (1, -1):
        cot_y[2].send(cotall.at[other], cotall.at[other], y_peer(dy), 4 * block_u)
    cot_two.wait()
    cot_spread = Batch(out_x)
    j_two = lane(ymod(2) * PAIR + xl)
    for dk, dx in x_order:
        cot_spread.send(
            two_ref.at[:, lane(kp[dk])], cotall.at[row(k), j_two], x_peer(dk, dx), block_u
        )
    cotall[row(k), j_two] = two_ref[:, lane(k)]
    weight_hop(3, 0)
    sweep(x_f, co_f, tuple(pre_f[m] for m in range(MODES)), False)
    e_batch.wait()
    start_f = carried(e_all, False)
    add_carried(co_f, start_f, False)
    gates_in.wait()
    mixed_all[:, lane(k)] = (gateg[...].astype(f32) * co_f[...]).astype(bf16)
    mix_2 = Batch(out_x)
    mix_2.send(mixed_all.at[:, lane(k)], mixed_all.at[:, lane(k)], x_peer(2, 0), 4 * block_u)
    mix_1 = Batch(out_x)
    mix_1.send(mixed_all.at[:, lane(k)], mixed_all.at[:, lane(k)], x_peer(1, 0), 4 * block_u)
    weight_hop(3, 1)
    weight_hop(4, 0)
    for m in range(MODES):
        pre_f[m] += start_f[m]
    mix_2.wait()
    mix_1.send(mixed_all.at[:, lane(k2)], mixed_all.at[:, lane(k2)], x_peer(1, 0), 4 * block_u)
    weight_hop(4, 1)
    weight_hop(5, 0)
    side = span // 2
    sides = [pl.ds(h * side, side) for h in (0, 1)]

    def out_grad_part(h, d):
        return lax.dot_general(
            cotall[sides[h], pair(ymod(d))], wall[:, pair(ymod(d))], (((1,), (1,)), ((), ())),
            preferred_element_type=f32,
        )

    for h in (0, 1):
        og_acc[sides[h], :] = out_grad_part(h, 0)
    for batch in (*cot_y, cot_spread):
        batch.wait()
    og_a = [Batch(out_x), Batch(out_x)]
    og_b = Batch(out_x)
    for h in (0, 1):
        for d in (1, -1, 2):
            og_acc[sides[h], :] += out_grad_part(h, d)
        og_send[0, sides[h], :] = og_acc[sides[h], lane(k3)].astype(bf16)
        og_a[h].send(
            og_send.at[0, sides[h]], og_recv.at[0, sides[h]], x_peer(1, 0), 2 * block_u
        )
        og_send[1, sides[h], :] = og_acc[sides[h], lane(k1)].astype(bf16)
        og_b.send(
            og_send.at[1, sides[h]], og_recv.at[1, sides[h]], x_peer(1, 0), 2 * block_u
        )

    mix_1.wait()

    far_rows = pl.ds(pl.multiple_of((1 - lax.div(k, 2)) * side, side), side)
    near_rows = pl.ds(pl.multiple_of(lax.div(k, 2) * side, side), side)
    fin_parts = []

    def output_part(part_rows):
        for n in range(ys):
            cols = slice(n * wide, (n + 1) * wide)
            fp[part_rows, cols] = jnp.dot(
                mixed_all[part_rows, :], wall[:, cols], preferred_element_type=f32
            ).astype(bf16)
        batch = Batch(out_y)
        for d in y_order:
            batch.send(
                fp.at[part_rows, pair(ymod(d))],
                frecv.at[{1: 0, -1: 1, 2: 2}[d], part_rows, :], y_peer(d), 4 * block_u,
            )
        fin_parts.append(batch)

    def weight_term(d):
        block = lane(zmod(d))
        gp[:, block] = lax.dot_general(
            mixed_all[...], cotall[:, block], (((0,), (0,)), ((), ())),
            preferred_element_type=f32,
        ).astype(bf16)

    sums = {}
    slots = {}
    for h in range(1, zs // 2 + 1):
        for long in (0, 1):
            for d, c, hops in ways[long]:
                if h <= hops:
                    slots[d, c, h] = len(slots)

    def weight_sum_hop(h, long):
        if h > 1:
            sums[h - 1, long].wait()
        if h > ways[long][0][2]:
            return
        sums[h, long] = Batch(out_s)
        for d, c, hops in ways[long]:
            block = lane(zmod(d * (hops - h + 1)))
            if h == 1:
                src = gp.at[chunk[c], block]
            else:
                slot = slots[d, c, h - 1]
                rsbuf[slot] = (
                    rsbuf[slot].astype(f32) + gp[chunk[c], block].astype(f32)
                ).astype(bf16)
                src = rsbuf.at[slot]
            sums[h, long].send(src, rsbuf.at[slots[d, c, h]], z_peer(d), chunk_u)

    weight_term(zs // 2)
    weight_sum_hop(1, 0)
    output_part(far_rows)
    og_c = Batch(out_x)
    for h in (0, 1):
        og_a[h].wait()
        og_send[2, sides[h], :] = (
            og_acc[sides[h], lane(k2)] + og_recv[0, sides[h], :].astype(f32)
        ).astype(bf16)
        og_c.send(
            og_send.at[2, sides[h]], og_recv.at[2, sides[h]], x_peer(2, 0), 2 * block_u
        )
    output_part(near_rows)
    weight_term(zs // 2 - 1)
    weight_term(1 - zs // 2)
    weight_sum_hop(1, 1)
    for d in range(2 - zs // 2, zs // 2 - 1):
        weight_term(d)
    weight_sum_hop(2, 0)

    og_b.wait()
    og_c.wait()
    og = og_acc[:, lane(k)] + og_recv[1].astype(f32) + og_recv[2].astype(f32)
    og = og.astype(bf16).astype(f32)
    cg_f[...] = og * gateg[...].astype(f32)
    prefix(ends(cg_f, True), pre_b, True, b_all)
    b_batch = to_z(b_all, 1)
    weight_sum_hop(2, 1)
    gates_g[...] = (og * co_f[...]).astype(bf16)
    gate_batch = Batch(out_x)
    for d in g_order:
        gate_batch.send(gates_g.at[row(kp[d]), :], gg_ref.at[:, lane(k)], x_peer(d, 0), block_u)
    gg_ref[:, lane(k)] = gates_g[row(k), :]

    def residue_body(s, carry):
        state, sums_m = carry
        value = x_f[at_step(s), :]
        grad = cg_f[at_step(s), :]
        state = tuple(decays[m] * state[m] + value for m in range(MODES))
        return state, tuple(sums_m[m] + grad * state[m] for m in range(MODES))

    _, mode_sums = lax.fori_loop(
        0, step_len, residue_body,
        (tuple(pre_f[m] for m in range(MODES)), (zero,) * MODES), unroll=4,
    )
    for m in range(MODES):
        l_s[m : m + 1, :] = jnp.sum(mode_sums[m], axis=0, keepdims=True)
    l_all[z] = l_s[...].astype(bf16)
    skip_all[z] = jnp.sum(cg_f[...] * x_f[...], axis=0, keepdims=True)
    l_batch = to_z(l_all, 1)
    skip_batch = Batch(out_one)
    for d in z_order:
        skip_batch.send(skip_all.at[z], skip_all.at[z], z_peer(d), 1)
    weight_sum_hop(3, 0)

    sweep(cg_f, co_f, tuple(pre_b[m] for m in range(MODES)), True)
    out_batch = Batch(out_x)

    def finish(batch, part_rows, order):
        batch.wait()
        fin = fp[part_rows, pair(y)].astype(f32)
        for n in range(ys - 1):
            fin = fin + frecv[n, part_rows, :].astype(f32)
        fin_y[part_rows, :] = fin.astype(bf16)
        for dk, dx in order:
            out_batch.send(
                fin_y.at[row(kp[dk]), lane(xp[dx])], fin_pos.at[xl, :, lane(k)],
                x_peer(dk, dx), block_u,
            )

    finish(fin_parts[0], far_rows, [(dk, dx) for dk in (2, 3) for dx in (1, 0)])
    b_batch.wait()
    add_carried(co_f, carried(b_all, True), True)
    ggrp[...] = co_f[...].astype(bf16)
    gg_batch = Batch(out_x)
    for d in g_order:
        gg_batch.send(ggrp.at[row(kp[d]), :], ggpos.at[:, lane(k)], x_peer(d, 0), block_u)
    ggpos[:, lane(k)] = ggrp[row(k), :]
    weight_sum_hop(3, 1)
    l_batch.wait()
    skip_batch.wait()
    total = l_all[0].astype(f32)
    for n in range(1, zs):
        total = total + l_all[n].astype(f32)
    tot_all[0:MODES, lane(k)] = total[0:MODES] * inv_norm * scale
    total = skip_all[0]
    for n in range(1, zs):
        total = total + skip_all[n]
    tot_all[MODES : MODES + SUBS, lane(k)] = spread(total, 0) * scale
    tot_batch = Batch(out_zs)
    for d in g_order:
        tot_batch.send(tot_all.at[:, lane(k)], tot_all.at[:, lane(k)], x_peer(d, 0), 3)
    finish(fin_parts[1], near_rows, [(0, 1), (1, 1), (1, 0)])
    fin_pos[xl, :, lane(k)] = fin_y[row(k), lane(xl)]

    weight_sum_hop(4, 0)

    writes = []

    def write(n, src, dst):
        copy = pltpu.make_async_copy(src, dst, load_sems.at[n])
        copy.start()
        writes.append(copy)

    gg_batch.wait()
    spread_grad = ggpos[...].astype(f32)
    gq_ref[...] = (spread_grad * key_ref[...].astype(f32)).astype(bf16)
    gk_ref[...] = (spread_grad * q_ref[...].astype(f32)).astype(bf16)
    write(1, gq_ref, gq_hbm)
    write(2, gk_ref, gk_hbm)
    gate_batch.wait()
    write(3, gg_ref, gg_hbm)

    weight_sum_hop(4, 1)
    weight_sum_hop(5, 0)
    for c in (0, 1):
        part = gp[chunk[c], lane(z)].astype(f32)
        for long in (0, 1):
            for d, other, hops in ways[long]:
                if other == c:
                    part = part + rsbuf[slots[d, c, hops]].astype(f32)
        gw_ref[chunk[c], :] = (part * scale).astype(bf16)
    write(4, gw_ref, gw_hbm)

    tot_batch.wait()
    write(5, tot_all.at[pl.ds(0, MODES), :], gres_hbm)
    write(6, tot_all.at[pl.ds(MODES, 1), :], gskip_hbm)
    out_batch.wait()
    final_ref[...] = (fin_pos[0].astype(f32) + fin_pos[1].astype(f32)).astype(bf16)
    write(0, final_ref, final_hbm)
    for out in (out_x, out_y, out_z, out_zs, out_s, out_one):
        out.wait()
    for copy in writes:
        copy.wait()
    assert counts == [RECEIVES, SENDS], counts


def store_kernel(*refs):
    count = (len(refs) - 2) // 3
    srcs, dsts, bufs = refs[:count], refs[count : 2 * count], refs[2 * count : 3 * count]
    in_sems, out_sems = refs[3 * count :]
    reads = [pltpu.make_async_copy(srcs[n], bufs[n], in_sems.at[n]) for n in range(count)]
    writes = [pltpu.make_async_copy(bufs[n], dsts[n], out_sems.at[n]) for n in range(count)]
    for copy in reads:
        copy.start()
    for read, write in zip(reads, writes):
        read.wait()
        write.start()
    for copy in writes:
        copy.wait()


def shards(mesh, *args):
    q, key_input, gate, cot, weight, rates, residues, skip = args
    zs, chans = mesh.shape["ctx"] // GROUP, mesh.shape["chan"]
    rows, width = q.shape
    depth = weight.shape[0]
    span = rows * GROUP
    length = rows * mesh.shape["ctx"]
    columns = zs * LANES
    hbm = pl.BlockSpec(memory_space=pltpu.HBM)
    shape = jax.ShapeDtypeStruct
    out_shape = (
        shape((rows, width), bf16),
        shape((rows, width), bf16),
        shape((rows, width), bf16),
        shape((rows, width), bf16),
        shape((depth, LANES), bf16),
        shape((MODES, width), f32),
        shape((1, width), f32),
    )
    outs = pl.pallas_call(
        functools.partial(kernel, zs, chans, length),
        out_shape=out_shape,
        in_specs=[hbm] * 8,
        out_specs=(hbm,) * 7,
        scratch_shapes=[
            pltpu.VMEM((rows, width), bf16),
            pltpu.VMEM((rows, width), bf16),
            pltpu.VMEM((rows, width), bf16),
            pltpu.VMEM((rows, width), bf16),
            pltpu.VMEM((depth, LANES), bf16),
            pltpu.VMEM((MODES, width), f32),
            pltpu.VMEM((MODES, width), f32),
            pltpu.VMEM((1, width), f32),
            pltpu.VMEM((rows, width), bf16),
            pltpu.VMEM((rows, width), bf16),
            pltpu.VMEM((span, columns), bf16),
            pltpu.VMEM((depth, columns), bf16),
            pltpu.VMEM((span, LANES), bf16),
            pltpu.VMEM((span, LANES), bf16),
            pltpu.VMEM((span, LANES), f32),
            pltpu.VMEM((span, LANES), f32),
            pltpu.VMEM((span, LANES), f32),
            pltpu.VMEM((MODES, SUBS, LANES), f32),
            pltpu.VMEM((MODES, SUBS, LANES), f32),
            pltpu.VMEM((zs, MODES, LANES), bf16),
            pltpu.VMEM((zs, MODES, LANES), bf16),
            pltpu.VMEM((MODES, LANES), f32),
            pltpu.VMEM((MODES, LANES), f32),
            pltpu.VMEM((zs, MODES, LANES), bf16),
            pltpu.VMEM((zs, 1, LANES), f32),
            pltpu.VMEM((zs, 1, LANES), f32),
            pltpu.VMEM((span, width), bf16),
            pltpu.VMEM((span, width), f32),
            pltpu.VMEM((3, span, LANES), bf16),
            pltpu.VMEM((3, span, LANES), bf16),
            pltpu.VMEM((span, columns), bf16),
            pltpu.VMEM((chans // PAIR - 1, span, PAIR * LANES), bf16),
            pltpu.VMEM((span, PAIR * LANES), bf16),
            pltpu.VMEM((PAIR, rows, width), bf16),
            pltpu.VMEM((depth, columns), bf16),
            pltpu.VMEM((2 * (zs - 1), depth // 2, LANES), bf16),
            pltpu.VMEM((span, LANES), bf16),
            pltpu.VMEM((rows, width), bf16),
            pltpu.VMEM((span, LANES), bf16),
            pltpu.VMEM((MODES + 8, width), f32),
            pltpu.VMEM((512, 16, LANES), bf16),
            *[pltpu.VMEM(a.shape, a.dtype) for a in out_shape[:5]],
            pltpu.SemaphoreType.DMA((RECEIVES,)),
            pltpu.SemaphoreType.DMA((SENDS,)),
            pltpu.SemaphoreType.DMA((8,)),
        ],
        compiler_params=pltpu.CompilerParams(
            collective_id=0, has_side_effects=True, vmem_limit_bytes=65000 * 1024
        ),
    )(q, key_input, gate, cot, weight, rates.T, residues.T, skip.reshape(1, -1))
    outs = pl.pallas_call(
        store_kernel,
        out_shape=out_shape,
        in_specs=[hbm] * 7,
        out_specs=(hbm,) * 7,
        scratch_shapes=[
            *[pltpu.VMEM(a.shape, a.dtype) for a in out_shape],
            pltpu.SemaphoreType.DMA((7,)),
            pltpu.SemaphoreType.DMA((7,)),
        ],
        compiler_params=pltpu.CompilerParams(vmem_limit_bytes=65000 * 1024),
    )(*outs)
    return (*outs[:5], outs[5].T, outs[6].reshape(-1))


def solution(mesh):
    placed = (
        P("ctx", "chan"),
        P("ctx", "chan"),
        P("ctx", "chan"),
        P("ctx", "chan"),
        P("chan", "ctx"),
        P("chan", None),
        P("chan", None),
        P("chan"),
    )
    return jax.shard_map(
        functools.partial(shards, mesh),
        mesh=mesh,
        in_specs=placed,
        out_specs=(
            P("ctx", "chan"),
            P("ctx", "chan"),
            P("ctx", "chan"),
            P("ctx", "chan"),
            P("chan", "ctx"),
            P("chan", None),
            P("chan"),
        ),
        check_vma=False,
    )
```

```python
import functools
import math

import jax
import jax.numpy as jnp
from jax import lax
from jax.experimental import pallas as pl
from jax.experimental.pallas import tpu as pltpu
from jax.sharding import PartitionSpec as P

MESH = pl.DeviceIdType.MESH
f32 = jnp.float32
bf16 = jnp.bfloat16

GROUP = 4
PAIR = 2
LANES = 128
SUBS = 8
MODES = 16
RECEIVES = 53
SENDS = 7


def one_minus_exp(x):
    series = jnp.ones_like(x)
    for n in range(9, 1, -1):
        series = 1.0 - x * (1.0 / n) * series
    return jnp.where(x < 0.5, x * series, 1.0 - jnp.exp(-x))


def kernel(
    zs, chans, length,
    q_hbm, key_hbm, gate_hbm, cot_hbm, w_hbm, rate_hbm, res_hbm, skip_hbm,
    final_hbm, gq_hbm, gk_hbm, gg_hbm, gw_hbm, gres_hbm, gskip_hbm,
    q_ref, key_ref, gate_ref, cot_ref, w_ref, rate_ref, res_ref, skip_ref,
    gat_s, two_ref, cotall, wall, xg, gateg, x_f, co_f, cg_f, pre_f, pre_b, e_all, b_all, ends_s, l_s, l_all, skip_all, sizes_one,
    mixed_all, og_acc, og_send, og_recv, fp, frecv, fin_y, fin_pos, gp, rsbuf,
    ggrp, ggpos, gates_g, tot_all, sizes,
    final_ref, gq_ref, gk_ref, gg_ref, gw_ref,
    recv_sems, send_sems, load_sems,
):
    rows = q_ref.shape[0]
    span = rows * GROUP
    step_len = span // SUBS
    half = w_ref.shape[0] // 2
    ys = chans // PAIR
    wide = PAIR * LANES
    scale = 1.0 / math.sqrt(length)

    i = lax.axis_index("ctx")
    j = lax.axis_index("chan")
    z = lax.div(i, GROUP)
    k = lax.rem(i, GROUP)
    y = lax.div(j, PAIR)
    xl = lax.rem(j, PAIR)
    k1 = k + 1 - 2 * lax.rem(k, 2)
    k2 = lax.rem(k + 2, GROUP)
    k3 = GROUP - 1 - k
    kp = {0: k, 1: k1, 2: k2, 3: k3}
    xp = {0: xl, 1: PAIR - 1 - xl}

    def zmod(d):
        return lax.rem(z + d + zs, zs)

    def ymod(d):
        return lax.rem(y + d + ys, ys)

    def x_peer(dk, dx):
        return {"ctx": z * GROUP + kp[dk], "chan": y * PAIR + xp[dx]}

    def z_peer(d):
        return {"ctx": zmod(d) * GROUP + k, "chan": j}

    def y_peer(d):
        return {"ctx": i, "chan": ymod(d) * PAIR + xl}

    x_order = [(dk, dx) for dk in (2, 3, 1, 0) for dx in (1, 0) if dk or dx]
    g_order = (2, 3, 1)
    z_order = [zs // 2] + [d for n in range(zs // 2 - 1, 0, -1) for d in (n, -n)]

    def lane(index):
        return pl.ds(pl.multiple_of(index * LANES, LANES), LANES)

    def pair(index):
        return pl.ds(pl.multiple_of(index * wide, wide), wide)

    def row(index):
        return pl.ds(pl.multiple_of(index * rows, rows), rows)

    counts = [0, 0]

    class Batch:
        def __init__(self, lane_class):
            self.recv = recv_sems.at[counts[0]]
            counts[0] += 1
            self.out = lane_class
            self.units = 0

        def send(self, src, dst, peer, units):
            pltpu.make_async_remote_copy(
                src_ref=src, dst_ref=dst, send_sem=self.out.sem, recv_sem=self.recv,
                device_id=peer, device_id_type=MESH,
            ).start()
            self.units += units
            self.out.units += units

        def wait(self):
            part = self.out.sizes.at[pl.ds(0, self.units)]
            pltpu.make_async_copy(part, part, self.recv).wait()

    class Outgoing:
        def __init__(self, size_ref=sizes):
            self.sizes = size_ref
            self.sem = send_sems.at[counts[1]]
            counts[1] += 1
            self.units = 0

        def wait(self):
            part = self.sizes.at[pl.ds(0, self.units)]
            pltpu.make_async_copy(part, part, self.sem).wait()

    block_u = rows // 16
    out_x, out_y, out_z, out_zs, out_s, first_z = (
        Outgoing() for _ in range(6)
    )
    out_one = Outgoing(sizes_one)

    barrier = pltpu.get_barrier_semaphore()
    peers = [x_peer(*d) for d in x_order]
    peers += [z_peer(d) for d in z_order]
    peers += [y_peer(d) for d in range(1, ys)]
    for peer in peers:
        pl.semaphore_signal(barrier, inc=1, device_id=peer, device_id_type=MESH)

    loads = [
        pltpu.make_async_copy(src, dst, load_sems.at[n])
        for n, (src, dst) in enumerate((
            (cot_hbm, cot_ref), (w_hbm, w_ref), (q_hbm, q_ref), (key_hbm, key_ref),
            (gate_hbm, gate_ref), (rate_hbm, rate_ref), (res_hbm, res_ref), (skip_hbm, skip_ref),
        ))
    ]
    for copy in loads:
        copy.start()

    pl.semaphore_wait(barrier, len(peers))

    chunk = (pl.ds(0, half), pl.ds(half, half))
    ways = {0: ((1, 0, zs // 2), (-1, 1, zs // 2)), 1: ((1, 1, zs // 2 - 1), (-1, 0, zs // 2 - 1))}
    ring = {}
    chunk_u = half // 16

    def quarter(c, q):
        return pl.ds(c * half + q * (half // 2), half // 2)

    def weight_hop(h, long):
        for q in (0, 1):
            if h > 1:
                ring[h - 1, long, q].wait()
            if h > ways[long][0][2]:
                continue
            ring[h, long, q] = Batch(first_z if (h, long) == (1, 0) else out_z)
            for d, c, hops in ways[long]:
                spot = (quarter(c, q), lane(zmod(-d * (h - 1))))
                src = w_hbm.at[spot[0], :] if h == 1 else wall.at[spot]
                ring[h, long, q].send(src, wall.at[spot], z_peer(d), chunk_u // 2)

    y_order = (2, 1, -1)
    cot_y = [Batch(out_y) for _ in range(3)]
    for d in (1, -1):
        cot_y[0].send(cot_hbm.at[:, lane(k)], cotall.at[row(k), lane(j)], y_peer(d), block_u)
    cot_two = Batch(out_y)
    cot_two.send(cot_hbm, two_ref, y_peer(2), 4 * block_u)
    weight_hop(1, 0)
    for copy in loads:
        copy.wait()
    gat_s[...] = (q_ref[...].astype(f32) * key_ref[...].astype(f32)).astype(bf16)
    signals = Batch(out_x)
    for d in g_order:
        signals.send(gat_s.at[:, lane(kp[d])], xg.at[row(k), :], x_peer(d, 0), block_u)
    cot_a = Batch(out_x)
    for d in g_order:
        cot_a.send(
            cot_hbm.at[:, lane(kp[d])], cotall.at[row(k), lane(j)], x_peer(d, 0), block_u
        )
    cotall[row(k), lane(j)] = cot_ref[:, lane(k)]
    xg[row(k), :] = gat_s[:, lane(k)]
    gateg[row(k), :] = gate_ref[:, lane(k)]
    wall[:, lane(z)] = w_ref[...]

    rate = rate_ref[:, lane(k)]
    inv_norm = jnp.sqrt(one_minus_exp(2.0 * rate) / one_minus_exp(2.0 * length * rate))
    gain = res_ref[:, lane(k)] * inv_norm
    decay = jnp.exp(-rate)
    decay_sub = jnp.exp(-step_len * rate)
    decay_span = jnp.exp(-span * rate)
    skip_b = jnp.broadcast_to(skip_ref[:, lane(k)], (SUBS, LANES))
    sub = lax.broadcasted_iota(jnp.int32, (SUBS, LANES), 0)

    def spread(table, m):
        return jnp.broadcast_to(table[m : m + 1, :], (SUBS, LANES))

    decays = [spread(decay, m) for m in range(MODES)]
    gains = [spread(gain, m) for m in range(MODES)]
    zero = jnp.zeros((SUBS, LANES), f32)

    def at_step(t):
        return pl.ds(t, SUBS, stride=step_len)

    def ends(src, backward):
        def body(s, state):
            t = step_len - 1 - s if backward else s
            value = src[at_step(t), :]
            return tuple(decays[m] * state[m] + value for m in range(MODES))

        return lax.fori_loop(0, step_len, body, (zero,) * MODES, unroll=4)

    def prefix(state, pre, backward, all_ref):
        for m in range(MODES):
            factor = spread(decay_sub, m)
            total = state[m]
            for shift in (1, 2, 4):
                moved = pltpu.roll(total, SUBS - shift if backward else shift, 0)
                keep = sub < SUBS - shift if backward else sub >= shift
                total = total + jnp.where(keep, factor * moved, 0.0)
                factor = factor * factor
            moved = pltpu.roll(total, SUBS - 1 if backward else 1, 0)
            pre[m] = jnp.where(sub < SUBS - 1 if backward else sub >= 1, moved, 0.0)
            edge = 0 if backward else SUBS - 1
            ends_s[m : m + 1, :] = total[edge : edge + 1, :]
        all_ref[z] = ends_s[...].astype(bf16)

    def carried(all_ref, backward):
        carry = jnp.zeros((MODES, LANES), f32)
        for n in range(zs):
            other = zs - 1 - n if backward else n
            ahead = z < other if backward else z > other
            carry = jnp.where(ahead, decay_span * carry + all_ref[other].astype(f32), carry)
        steps = (SUBS - 1 - sub if backward else sub).astype(f32)
        return tuple(
            jnp.exp(-step_len * steps * spread(rate, m)) * spread(carry, m)
            for m in range(MODES)
        )

    def tree(terms):
        while len(terms) > 1:
            terms = [a + b for a, b in zip(terms[::2], terms[1::2])]
        return terms[0]

    def sweep(src, out, state, backward):
        def body(s, state):
            t = step_len - 1 - s if backward else s
            value = src[at_step(t), :]
            state = tuple(decays[m] * state[m] + value for m in range(MODES))
            out[at_step(t), :] = (
                tree([gains[m] * state[m] for m in range(MODES)]) + skip_b * value
            )
            return state

        lax.fori_loop(0, step_len, body, state, unroll=4)

    def add_carried(out, state, backward):
        def body(s, state):
            t = step_len - 1 - s if backward else s
            state = tuple(decays[m] * state[m] for m in range(MODES))
            out[at_step(t), :] += tree(list(state))
            return state

        lax.fori_loop(0, step_len, body, tuple(gains[m] * state[m] for m in range(MODES)), unroll=4)

    def to_z(ref, units):
        batch = Batch(out_zs)
        for d in z_order:
            batch.send(ref.at[z], ref.at[z], z_peer(d), units)
        return batch

    first_z.wait()
    weight_hop(1, 1)
    cot_b = Batch(out_x)
    for dk in (1, 3, 2, 0):
        cot_b.send(
            cot_ref.at[:, lane(kp[dk])], cotall.at[row(k), lane(j)], x_peer(dk, 1), block_u
        )
    weight_hop(2, 0)
    gates_in = Batch(out_x)
    for d in g_order:
        gates_in.send(gate_ref.at[:, lane(kp[d])], gateg.at[row(k), :], x_peer(d, 0), block_u)
    signals.wait()
    x_f[...] = xg[...].astype(f32)
    prefix(ends(x_f, False), pre_f, False, e_all)
    e_batch = to_z(e_all, 1)
    cot_a.wait()
    for dy in (1, -1):
        for d in (1, 2, 3):
            piece = (row(kp[d]), lane(j))
            cot_y[1].send(cotall.at[piece], cotall.at[piece], y_peer(dy), block_u)
    weight_hop(2, 1)
    cot_two.wait()
    cot_spread = Batch(out_x)
    j_two = lane(ymod(2) * PAIR + xl)
    for dk, dx in x_order:
        cot_spread.send(
            two_ref.at[:, lane(kp[dk])], cotall.at[row(k), j_two], x_peer(dk, dx), block_u
        )
    cotall[row(k), j_two] = two_ref[:, lane(k)]
    cot_b.wait()
    other = (slice(None), lane(y * PAIR + xp[1]))
    for dy in (1, -1):
        cot_y[2].send(cotall.at[other], cotall.at[other], y_peer(dy), 4 * block_u)
    weight_hop(3, 0)
    sweep(x_f, co_f, tuple(pre_f[m] for m in range(MODES)), False)
    e_batch.wait()
    start_f = carried(e_all, False)
    add_carried(co_f, start_f, False)
    gates_in.wait()
    mixed_all[:, lane(k)] = (gateg[...].astype(f32) * co_f[...]).astype(bf16)
    mix_2 = Batch(out_x)
    mix_2.send(mixed_all.at[:, lane(k)], mixed_all.at[:, lane(k)], x_peer(2, 0), 4 * block_u)
    mix_1 = Batch(out_x)
    mix_1.send(mixed_all.at[:, lane(k)], mixed_all.at[:, lane(k)], x_peer(1, 0), 4 * block_u)
    weight_hop(3, 1)
    weight_hop(4, 0)
    for m in range(MODES):
        pre_f[m] += start_f[m]
    mix_2.wait()
    mix_1.send(mixed_all.at[:, lane(k2)], mixed_all.at[:, lane(k2)], x_peer(1, 0), 4 * block_u)
    weight_hop(4, 1)
    weight_hop(5, 0)
    side = span // 2
    sides = [pl.ds(h * side, side) for h in (0, 1)]

    def out_grad_part(h, d):
        return lax.dot_general(
            cotall[sides[h], pair(ymod(d))], wall[:, pair(ymod(d))], (((1,), (1,)), ((), ())),
            preferred_element_type=f32,
        )

    for h in (0, 1):
        og_acc[sides[h], :] = out_grad_part(h, 0)
    for batch in (*cot_y, cot_spread):
        batch.wait()
    og_a = [Batch(out_x), Batch(out_x)]
    og_b = Batch(out_x)
    for h in (0, 1):
        for d in (1, -1, 2):
            og_acc[sides[h], :] += out_grad_part(h, d)
        og_send[0, sides[h], :] = og_acc[sides[h], lane(k3)].astype(bf16)
        og_a[h].send(
            og_send.at[0, sides[h]], og_recv.at[0, sides[h]], x_peer(1, 0), 2 * block_u
        )
        og_send[1, sides[h], :] = og_acc[sides[h], lane(k1)].astype(bf16)
        og_b.send(
            og_send.at[1, sides[h]], og_recv.at[1, sides[h]], x_peer(1, 0), 2 * block_u
        )

    mix_1.wait()

    far_rows = pl.ds(pl.multiple_of((1 - lax.div(k, 2)) * side, side), side)
    near_rows = pl.ds(pl.multiple_of(lax.div(k, 2) * side, side), side)
    fin_parts = []

    def output_part(part_rows):
        for n in range(ys):
            cols = slice(n * wide, (n + 1) * wide)
            fp[part_rows, cols] = jnp.dot(
                mixed_all[part_rows, :], wall[:, cols], preferred_element_type=f32
            ).astype(bf16)
        batch = Batch(out_y)
        for d in y_order:
            batch.send(
                fp.at[part_rows, pair(ymod(d))],
                frecv.at[{1: 0, -1: 1, 2: 2}[d], part_rows, :], y_peer(d), 4 * block_u,
            )
        fin_parts.append(batch)

    output_part(far_rows)
    def weight_term(d):
        block = lane(zmod(d))
        gp[:, block] = lax.dot_general(
            mixed_all[...], cotall[:, block], (((0,), (0,)), ((), ())),
            preferred_element_type=f32,
        ).astype(bf16)

    sums = {}
    slots = {}
    for h in range(1, zs // 2 + 1):
        for long in (0, 1):
            for d, c, hops in ways[long]:
                if h <= hops:
                    slots[d, c, h] = len(slots)

    def weight_sum_hop(h, long):
        for q in (0, 1):
            if h > 1:
                sums[h - 1, long, q].wait()
            if h > ways[long][0][2]:
                continue
            sums[h, long, q] = Batch(out_s)
            part = pl.ds(q * (half // 2), half // 2)
            for d, c, hops in ways[long]:
                block = lane(zmod(d * (hops - h + 1)))
                if h == 1:
                    src = gp.at[quarter(c, q), block]
                else:
                    slot = slots[d, c, h - 1]
                    rsbuf[slot, part, :] = (
                        rsbuf[slot, part, :].astype(f32) + gp[quarter(c, q), block].astype(f32)
                    ).astype(bf16)
                    src = rsbuf.at[slot, part]
                sums[h, long, q].send(
                    src, rsbuf.at[slots[d, c, h], part], z_peer(d), chunk_u // 2
                )

    weight_term(zs // 2)
    weight_sum_hop(1, 0)
    og_c = Batch(out_x)
    for h in (0, 1):
        og_a[h].wait()
        og_send[2, sides[h], :] = (
            og_acc[sides[h], lane(k2)] + og_recv[0, sides[h], :].astype(f32)
        ).astype(bf16)
        og_c.send(
            og_send.at[2, sides[h]], og_recv.at[2, sides[h]], x_peer(2, 0), 2 * block_u
        )
    output_part(near_rows)
    weight_term(zs // 2 - 1)
    weight_term(1 - zs // 2)
    weight_sum_hop(1, 1)
    for d in range(2 - zs // 2, zs // 2 - 1):
        weight_term(d)
    weight_sum_hop(2, 0)

    og_b.wait()
    og_c.wait()
    og = og_acc[:, lane(k)] + og_recv[1].astype(f32) + og_recv[2].astype(f32)
    og = og.astype(bf16).astype(f32)
    cg_f[...] = og * gateg[...].astype(f32)
    prefix(ends(cg_f, True), pre_b, True, b_all)
    b_batch = to_z(b_all, 1)
    weight_sum_hop(2, 1)
    gates_g[...] = (og * co_f[...]).astype(bf16)
    gate_batch = Batch(out_x)
    for d in g_order:
        gate_batch.send(gates_g.at[row(kp[d]), :], gg_ref.at[:, lane(k)], x_peer(d, 0), block_u)
    gg_ref[:, lane(k)] = gates_g[row(k), :]

    def residue_body(s, carry):
        state, sums_m = carry
        value = x_f[at_step(s), :]
        grad = cg_f[at_step(s), :]
        state = tuple(decays[m] * state[m] + value for m in range(MODES))
        return state, tuple(sums_m[m] + grad * state[m] for m in range(MODES))

    _, mode_sums = lax.fori_loop(
        0, step_len, residue_body,
        (tuple(pre_f[m] for m in range(MODES)), (zero,) * MODES), unroll=4,
    )
    for m in range(MODES):
        l_s[m : m + 1, :] = jnp.sum(mode_sums[m], axis=0, keepdims=True)
    l_all[z] = l_s[...].astype(bf16)
    skip_all[z] = jnp.sum(cg_f[...] * x_f[...], axis=0, keepdims=True)
    l_batch = to_z(l_all, 1)
    skip_batch = Batch(out_one)
    for d in z_order:
        skip_batch.send(skip_all.at[z], skip_all.at[z], z_peer(d), 1)
    weight_sum_hop(3, 0)

    sweep(cg_f, co_f, tuple(pre_b[m] for m in range(MODES)), True)
    out_batch = Batch(out_x)

    def finish(batch, part_rows, order):
        batch.wait()
        fin = fp[part_rows, pair(y)].astype(f32)
        for n in range(ys - 1):
            fin = fin + frecv[n, part_rows, :].astype(f32)
        fin_y[part_rows, :] = fin.astype(bf16)
        for dk, dx in order:
            out_batch.send(
                fin_y.at[row(kp[dk]), lane(xp[dx])], fin_pos.at[xl, :, lane(k)],
                x_peer(dk, dx), block_u,
            )

    finish(fin_parts[0], far_rows, [(dk, dx) for dk in (2, 3) for dx in (1, 0)])
    b_batch.wait()
    add_carried(co_f, carried(b_all, True), True)
    ggrp[...] = co_f[...].astype(bf16)
    gg_batch = Batch(out_x)
    for d in g_order:
        gg_batch.send(ggrp.at[row(kp[d]), :], ggpos.at[:, lane(k)], x_peer(d, 0), block_u)
    ggpos[:, lane(k)] = ggrp[row(k), :]
    weight_sum_hop(3, 1)
    l_batch.wait()
    skip_batch.wait()
    total = l_all[0].astype(f32)
    for n in range(1, zs):
        total = total + l_all[n].astype(f32)
    tot_all[0:MODES, lane(k)] = total[0:MODES] * inv_norm * scale
    total = skip_all[0]
    for n in range(1, zs):
        total = total + skip_all[n]
    tot_all[MODES : MODES + SUBS, lane(k)] = spread(total, 0) * scale
    tot_batch = Batch(out_zs)
    for d in g_order:
        tot_batch.send(tot_all.at[:, lane(k)], tot_all.at[:, lane(k)], x_peer(d, 0), 3)
    finish(fin_parts[1], near_rows, [(0, 1), (1, 1), (1, 0)])
    fin_pos[xl, :, lane(k)] = fin_y[row(k), lane(xl)]

    weight_sum_hop(4, 0)

    writes = []

    def write(n, src, dst):
        copy = pltpu.make_async_copy(src, dst, load_sems.at[n])
        copy.start()
        writes.append(copy)

    gg_batch.wait()
    spread_grad = ggpos[...].astype(f32)
    gq_ref[...] = (spread_grad * key_ref[...].astype(f32)).astype(bf16)
    gk_ref[...] = (spread_grad * q_ref[...].astype(f32)).astype(bf16)
    write(1, gq_ref, gq_hbm)
    write(2, gk_ref, gk_hbm)
    gate_batch.wait()
    write(3, gg_ref, gg_hbm)

    weight_sum_hop(4, 1)
    weight_sum_hop(5, 0)
    for c in (0, 1):
        part = gp[chunk[c], lane(z)].astype(f32)
        for long in (0, 1):
            for d, other, hops in ways[long]:
                if other == c:
                    part = part + rsbuf[slots[d, c, hops]].astype(f32)
        gw_ref[chunk[c], :] = (part * scale).astype(bf16)
    write(4, gw_ref, gw_hbm)

    tot_batch.wait()
    write(5, tot_all.at[pl.ds(0, MODES), :], gres_hbm)
    write(6, tot_all.at[pl.ds(MODES, 1), :], gskip_hbm)
    out_batch.wait()
    final_ref[...] = (fin_pos[0].astype(f32) + fin_pos[1].astype(f32)).astype(bf16)
    write(0, final_ref, final_hbm)
    for out in (out_x, out_y, out_z, out_zs, out_s, out_one):
        out.wait()
    for copy in writes:
        copy.wait()
    assert counts == [RECEIVES, SENDS], counts


def store_kernel(*refs):
    count = (len(refs) - 2) // 3
    srcs, dsts, bufs = refs[:count], refs[count : 2 * count], refs[2 * count : 3 * count]
    in_sems, out_sems = refs[3 * count :]
    reads = [pltpu.make_async_copy(srcs[n], bufs[n], in_sems.at[n]) for n in range(count)]
    writes = [pltpu.make_async_copy(bufs[n], dsts[n], out_sems.at[n]) for n in range(count)]
    for copy in reads:
        copy.start()
    for read, write in zip(reads, writes):
        read.wait()
        write.start()
    for copy in writes:
        copy.wait()


def shards(mesh, *args):
    q, key_input, gate, cot, weight, rates, residues, skip = args
    zs, chans = mesh.shape["ctx"] // GROUP, mesh.shape["chan"]
    rows, width = q.shape
    depth = weight.shape[0]
    span = rows * GROUP
    length = rows * mesh.shape["ctx"]
    columns = zs * LANES
    hbm = pl.BlockSpec(memory_space=pltpu.HBM)
    shape = jax.ShapeDtypeStruct
    out_shape = (
        shape((rows, width), bf16),
        shape((rows, width), bf16),
        shape((rows, width), bf16),
        shape((rows, width), bf16),
        shape((depth, LANES), bf16),
        shape((MODES, width), f32),
        shape((1, width), f32),
    )
    outs = pl.pallas_call(
        functools.partial(kernel, zs, chans, length),
        out_shape=out_shape,
        in_specs=[hbm] * 8,
        out_specs=(hbm,) * 7,
        scratch_shapes=[
            pltpu.VMEM((rows, width), bf16),
            pltpu.VMEM((rows, width), bf16),
            pltpu.VMEM((rows, width), bf16),
            pltpu.VMEM((rows, width), bf16),
            pltpu.VMEM((depth, LANES), bf16),
            pltpu.VMEM((MODES, width), f32),
            pltpu.VMEM((MODES, width), f32),
            pltpu.VMEM((1, width), f32),
            pltpu.VMEM((rows, width), bf16),
            pltpu.VMEM((rows, width), bf16),
            pltpu.VMEM((span, columns), bf16),
            pltpu.VMEM((depth, columns), bf16),
            pltpu.VMEM((span, LANES), bf16),
            pltpu.VMEM((span, LANES), bf16),
            pltpu.VMEM((span, LANES), f32),
            pltpu.VMEM((span, LANES), f32),
            pltpu.VMEM((span, LANES), f32),
            pltpu.VMEM((MODES, SUBS, LANES), f32),
            pltpu.VMEM((MODES, SUBS, LANES), f32),
            pltpu.VMEM((zs, MODES, LANES), bf16),
            pltpu.VMEM((zs, MODES, LANES), bf16),
            pltpu.VMEM((MODES, LANES), f32),
            pltpu.VMEM((MODES, LANES), f32),
            pltpu.VMEM((zs, MODES, LANES), bf16),
            pltpu.VMEM((zs, 1, LANES), f32),
            pltpu.VMEM((zs, 1, LANES), f32),
            pltpu.VMEM((span, width), bf16),
            pltpu.VMEM((span, width), f32),
            pltpu.VMEM((3, span, LANES), bf16),
            pltpu.VMEM((3, span, LANES), bf16),
            pltpu.VMEM((span, columns), bf16),
            pltpu.VMEM((chans // PAIR - 1, span, PAIR * LANES), bf16),
            pltpu.VMEM((span, PAIR * LANES), bf16),
            pltpu.VMEM((PAIR, rows, width), bf16),
            pltpu.VMEM((depth, columns), bf16),
            pltpu.VMEM((2 * (zs - 1), depth // 2, LANES), bf16),
            pltpu.VMEM((span, LANES), bf16),
            pltpu.VMEM((rows, width), bf16),
            pltpu.VMEM((span, LANES), bf16),
            pltpu.VMEM((MODES + 8, width), f32),
            pltpu.VMEM((512, 16, LANES), bf16),
            *[pltpu.VMEM(a.shape, a.dtype) for a in out_shape[:5]],
            pltpu.SemaphoreType.DMA((RECEIVES,)),
            pltpu.SemaphoreType.DMA((SENDS,)),
            pltpu.SemaphoreType.DMA((8,)),
        ],
        compiler_params=pltpu.CompilerParams(
            collective_id=0, has_side_effects=True, vmem_limit_bytes=65000 * 1024
        ),
    )(q, key_input, gate, cot, weight, rates.T, residues.T, skip.reshape(1, -1))
    outs = pl.pallas_call(
        store_kernel,
        out_shape=out_shape,
        in_specs=[hbm] * 7,
        out_specs=(hbm,) * 7,
        scratch_shapes=[
            *[pltpu.VMEM(a.shape, a.dtype) for a in out_shape],
            pltpu.SemaphoreType.DMA((7,)),
            pltpu.SemaphoreType.DMA((7,)),
        ],
        compiler_params=pltpu.CompilerParams(vmem_limit_bytes=65000 * 1024),
    )(*outs)
    return (*outs[:5], outs[5].T, outs[6].reshape(-1))


def solution(mesh):
    placed = (
        P("ctx", "chan"),
        P("ctx", "chan"),
        P("ctx", "chan"),
        P("ctx", "chan"),
        P("chan", "ctx"),
        P("chan", None),
        P("chan", None),
        P("chan"),
    )
    return jax.shard_map(
        functools.partial(shards, mesh),
        mesh=mesh,
        in_specs=placed,
        out_specs=(
            P("ctx", "chan"),
            P("ctx", "chan"),
            P("ctx", "chan"),
            P("ctx", "chan"),
            P("chan", "ctx"),
            P("chan", None),
            P("chan"),
        ),
        check_vma=False,
    )
```

```python
import functools
import math

import jax
import jax.numpy as jnp
from jax import lax
from jax.experimental import pallas as pl
from jax.experimental.pallas import tpu as pltpu
from jax.sharding import PartitionSpec as P

MESH = pl.DeviceIdType.MESH
f32 = jnp.float32
bf16 = jnp.bfloat16

GROUP = 4
PAIR = 2
LANES = 128
SUBS = 8
MODES = 16
RECEIVES = 53
SENDS = 7


def one_minus_exp(x):
    series = jnp.ones_like(x)
    for n in range(9, 1, -1):
        series = 1.0 - x * (1.0 / n) * series
    return jnp.where(x < 0.5, x * series, 1.0 - jnp.exp(-x))


def kernel(
    zs, chans, length,
    q_hbm, key_hbm, gate_hbm, cot_hbm, w_hbm, rate_hbm, res_hbm, skip_hbm,
    final_hbm, gq_hbm, gk_hbm, gg_hbm, gw_hbm, gres_hbm, gskip_hbm,
    q_ref, key_ref, gate_ref, cot_ref, w_ref, rate_ref, res_ref, skip_ref,
    gat_s, two_ref, cotall, wall, xg, gateg, x_f, co_f, cg_f, pre_f, pre_b, e_all, b_all, ends_s, l_s, l_all, skip_all, sizes_one,
    mixed_all, og_acc, og_send, og_recv, fp, frecv, fin_y, fin_pos, gp, rsbuf,
    ggrp, ggpos, gates_g, tot_all, sizes,
    final_ref, gq_ref, gk_ref, gg_ref, gw_ref,
    recv_sems, send_sems, load_sems,
):
    rows = q_ref.shape[0]
    span = rows * GROUP
    step_len = span // SUBS
    half = w_ref.shape[0] // 2
    ys = chans // PAIR
    wide = PAIR * LANES
    scale = 1.0 / math.sqrt(length)

    i = lax.axis_index("ctx")
    j = lax.axis_index("chan")
    z = lax.div(i, GROUP)
    k = lax.rem(i, GROUP)
    y = lax.div(j, PAIR)
    xl = lax.rem(j, PAIR)
    k1 = k + 1 - 2 * lax.rem(k, 2)
    k2 = lax.rem(k + 2, GROUP)
    k3 = GROUP - 1 - k
    kp = {0: k, 1: k1, 2: k2, 3: k3}
    xp = {0: xl, 1: PAIR - 1 - xl}

    def zmod(d):
        return lax.rem(z + d + zs, zs)

    def ymod(d):
        return lax.rem(y + d + ys, ys)

    def x_peer(dk, dx):
        return {"ctx": z * GROUP + kp[dk], "chan": y * PAIR + xp[dx]}

    def z_peer(d):
        return {"ctx": zmod(d) * GROUP + k, "chan": j}

    def y_peer(d):
        return {"ctx": i, "chan": ymod(d) * PAIR + xl}

    x_order = [(dk, dx) for dk in (2, 3, 1, 0) for dx in (1, 0) if dk or dx]
    g_order = (2, 3, 1)
    z_order = [zs // 2] + [d for n in range(zs // 2 - 1, 0, -1) for d in (n, -n)]

    def lane(index):
        return pl.ds(pl.multiple_of(index * LANES, LANES), LANES)

    def pair(index):
        return pl.ds(pl.multiple_of(index * wide, wide), wide)

    def row(index):
        return pl.ds(pl.multiple_of(index * rows, rows), rows)

    counts = [0, 0]

    class Batch:
        def __init__(self, lane_class):
            self.recv = recv_sems.at[counts[0]]
            counts[0] += 1
            self.out = lane_class
            self.units = 0

        def send(self, src, dst, peer, units):
            pltpu.make_async_remote_copy(
                src_ref=src, dst_ref=dst, send_sem=self.out.sem, recv_sem=self.recv,
                device_id=peer, device_id_type=MESH,
            ).start()
            self.units += units
            self.out.units += units

        def wait(self):
            part = self.out.sizes.at[pl.ds(0, self.units)]
            pltpu.make_async_copy(part, part, self.recv).wait()

    class Outgoing:
        def __init__(self, size_ref=sizes):
            self.sizes = size_ref
            self.sem = send_sems.at[counts[1]]
            counts[1] += 1
            self.units = 0

        def wait(self):
            part = self.sizes.at[pl.ds(0, self.units)]
            pltpu.make_async_copy(part, part, self.sem).wait()

    block_u = rows // 16
    out_x, out_y, out_z, out_zs, out_s, first_z = (
        Outgoing() for _ in range(6)
    )
    out_one = Outgoing(sizes_one)

    barrier = pltpu.get_barrier_semaphore()
    peers = [x_peer(*d) for d in x_order]
    peers += [z_peer(d) for d in z_order]
    peers += [y_peer(d) for d in range(1, ys)]
    for peer in peers:
        pl.semaphore_signal(barrier, inc=1, device_id=peer, device_id_type=MESH)

    loads = [
        pltpu.make_async_copy(src, dst, load_sems.at[n])
        for n, (src, dst) in enumerate((
            (cot_hbm, cot_ref), (w_hbm, w_ref), (q_hbm, q_ref), (key_hbm, key_ref),
            (gate_hbm, gate_ref), (rate_hbm, rate_ref), (res_hbm, res_ref), (skip_hbm, skip_ref),
        ))
    ]
    for copy in loads:
        copy.start()

    pl.semaphore_wait(barrier, len(peers))

    chunk = (pl.ds(0, half), pl.ds(half, half))
    ways = {0: ((1, 0, zs // 2), (-1, 1, zs // 2)), 1: ((1, 1, zs // 2 - 1), (-1, 0, zs // 2 - 1))}
    ring = {}
    chunk_u = half // 16

    def quarter(c, q):
        return pl.ds(c * half + q * (half // 2), half // 2)

    def weight_hop(h, long):
        for q in (0, 1):
            if h > 1:
                ring[h - 1, long, q].wait()
            if h > ways[long][0][2]:
                continue
            ring[h, long, q] = Batch(first_z if (h, long) == (1, 0) else out_z)
            for d, c, hops in ways[long]:
                spot = (quarter(c, q), lane(zmod(-d * (h - 1))))
                src = w_hbm.at[spot[0], :] if h == 1 else wall.at[spot]
                ring[h, long, q].send(src, wall.at[spot], z_peer(d), chunk_u // 2)

    y_order = (2, 1, -1)
    cot_y = [Batch(out_y) for _ in range(3)]
    for d in (1, -1):
        cot_y[0].send(cot_hbm.at[:, lane(k)], cotall.at[row(k), lane(j)], y_peer(d), block_u)
    cot_two = Batch(out_y)
    cot_two.send(cot_hbm, two_ref, y_peer(2), 4 * block_u)
    weight_hop(1, 0)
    for copy in loads:
        copy.wait()
    gat_s[...] = (q_ref[...].astype(f32) * key_ref[...].astype(f32)).astype(bf16)
    signals = Batch(out_x)
    for d in g_order:
        signals.send(gat_s.at[:, lane(kp[d])], xg.at[row(k), :], x_peer(d, 0), block_u)
    cot_a = Batch(out_x)
    for d in g_order:
        cot_a.send(
            cot_hbm.at[:, lane(kp[d])], cotall.at[row(k), lane(j)], x_peer(d, 0), block_u
        )
    cotall[row(k), lane(j)] = cot_ref[:, lane(k)]
    xg[row(k), :] = gat_s[:, lane(k)]
    gateg[row(k), :] = gate_ref[:, lane(k)]
    wall[:, lane(z)] = w_ref[...]

    rate = rate_ref[:, lane(k)]
    inv_norm = jnp.sqrt(one_minus_exp(2.0 * rate) / one_minus_exp(2.0 * length * rate))
    gain = res_ref[:, lane(k)] * inv_norm
    decay = jnp.exp(-rate)
    decay_sub = jnp.exp(-step_len * rate)
    decay_span = jnp.exp(-span * rate)
    skip_b = jnp.broadcast_to(skip_ref[:, lane(k)], (SUBS, LANES))
    sub = lax.broadcasted_iota(jnp.int32, (SUBS, LANES), 0)

    def spread(table, m):
        return jnp.broadcast_to(table[m : m + 1, :], (SUBS, LANES))

    decays = [spread(decay, m) for m in range(MODES)]
    gains = [spread(gain, m) for m in range(MODES)]
    zero = jnp.zeros((SUBS, LANES), f32)

    def at_step(t):
        return pl.ds(t, SUBS, stride=step_len)

    def ends(src, backward):
        def body(s, state):
            t = step_len - 1 - s if backward else s
            value = src[at_step(t), :]
            return tuple(decays[m] * state[m] + value for m in range(MODES))

        return lax.fori_loop(0, step_len, body, (zero,) * MODES, unroll=8)

    def prefix(state, pre, backward, all_ref):
        for m in range(MODES):
            factor = spread(decay_sub, m)
            total = state[m]
            for shift in (1, 2, 4):
                moved = pltpu.roll(total, SUBS - shift if backward else shift, 0)
                keep = sub < SUBS - shift if backward else sub >= shift
                total = total + jnp.where(keep, factor * moved, 0.0)
                factor = factor * factor
            moved = pltpu.roll(total, SUBS - 1 if backward else 1, 0)
            pre[m] = jnp.where(sub < SUBS - 1 if backward else sub >= 1, moved, 0.0)
            edge = 0 if backward else SUBS - 1
            ends_s[m : m + 1, :] = total[edge : edge + 1, :]
        all_ref[z] = ends_s[...].astype(bf16)

    def carried(all_ref, backward):
        carry = jnp.zeros((MODES, LANES), f32)
        for n in range(zs):
            other = zs - 1 - n if backward else n
            ahead = z < other if backward else z > other
            carry = jnp.where(ahead, decay_span * carry + all_ref[other].astype(f32), carry)
        steps = (SUBS - 1 - sub if backward else sub).astype(f32)
        return tuple(
            jnp.exp(-step_len * steps * spread(rate, m)) * spread(carry, m)
            for m in range(MODES)
        )

    def tree(terms):
        while len(terms) > 1:
            terms = [a + b for a, b in zip(terms[::2], terms[1::2])]
        return terms[0]

    def sweep(src, out, state, backward):
        def body(s, state):
            t = step_len - 1 - s if backward else s
            value = src[at_step(t), :]
            state = tuple(decays[m] * state[m] + value for m in range(MODES))
            out[at_step(t), :] = (
                tree([gains[m] * state[m] for m in range(MODES)]) + skip_b * value
            )
            return state

        lax.fori_loop(0, step_len, body, state, unroll=8)

    def add_carried(out, state, backward):
        def body(s, state):
            t = step_len - 1 - s if backward else s
            state = tuple(decays[m] * state[m] for m in range(MODES))
            out[at_step(t), :] += tree(list(state))
            return state

        lax.fori_loop(0, step_len, body, tuple(gains[m] * state[m] for m in range(MODES)), unroll=8)

    def to_z(ref, units):
        batch = Batch(out_zs)
        for d in z_order:
            batch.send(ref.at[z], ref.at[z], z_peer(d), units)
        return batch

    first_z.wait()
    weight_hop(1, 1)
    cot_b = Batch(out_x)
    for dk in (1, 3, 2, 0):
        cot_b.send(
            cot_ref.at[:, lane(kp[dk])], cotall.at[row(k), lane(j)], x_peer(dk, 1), block_u
        )
    weight_hop(2, 0)
    gates_in = Batch(out_x)
    for d in g_order:
        gates_in.send(gate_ref.at[:, lane(kp[d])], gateg.at[row(k), :], x_peer(d, 0), block_u)
    signals.wait()
    x_f[...] = xg[...].astype(f32)
    prefix(ends(x_f, False), pre_f, False, e_all)
    e_batch = to_z(e_all, 1)
    cot_a.wait()
    for dy in (1, -1):
        for d in (1, 2, 3):
            piece = (row(kp[d]), lane(j))
            cot_y[1].send(cotall.at[piece], cotall.at[piece], y_peer(dy), block_u)
    weight_hop(2, 1)
    cot_two.wait()
    cot_spread = Batch(out_x)
    j_two = lane(ymod(2) * PAIR + xl)
    for dk, dx in x_order:
        cot_spread.send(
            two_ref.at[:, lane(kp[dk])], cotall.at[row(k), j_two], x_peer(dk, dx), block_u
        )
    cotall[row(k), j_two] = two_ref[:, lane(k)]
    cot_b.wait()
    other = (slice(None), lane(y * PAIR + xp[1]))
    for dy in (1, -1):
        cot_y[2].send(cotall.at[other], cotall.at[other], y_peer(dy), 4 * block_u)
    weight_hop(3, 0)
    sweep(x_f, co_f, tuple(pre_f[m] for m in range(MODES)), False)
    e_batch.wait()
    start_f = carried(e_all, False)
    add_carried(co_f, start_f, False)
    gates_in.wait()
    mixed_all[:, lane(k)] = (gateg[...].astype(f32) * co_f[...]).astype(bf16)
    mix_2 = Batch(out_x)
    mix_2.send(mixed_all.at[:, lane(k)], mixed_all.at[:, lane(k)], x_peer(2, 0), 4 * block_u)
    mix_1 = Batch(out_x)
    mix_1.send(mixed_all.at[:, lane(k)], mixed_all.at[:, lane(k)], x_peer(1, 0), 4 * block_u)
    weight_hop(3, 1)
    weight_hop(4, 0)
    for m in range(MODES):
        pre_f[m] += start_f[m]
    side = span // 2
    sides = [pl.ds(h * side, side) for h in (0, 1)]

    def add_out_grad(h, steps):
        for d in steps:
            block = lane(zmod(d))
            part = lax.dot_general(
                cotall[sides[h], block], wall[:, block], (((1,), (1,)), ((), ())),
                preferred_element_type=f32,
            )
            if d == 0:
                og_acc[sides[h], :] = part
            else:
                og_acc[sides[h], :] += part

    for batch in (*cot_y, cot_spread):
        batch.wait()
    for h in (0, 1):
        add_out_grad(h, (0, 1, -1, 2, -2))
    mix_2.wait()
    mix_1.send(mixed_all.at[:, lane(k2)], mixed_all.at[:, lane(k2)], x_peer(1, 0), 4 * block_u)
    weight_hop(4, 1)
    weight_hop(5, 0)
    og_a = [Batch(out_x), Batch(out_x)]
    og_b = Batch(out_x)
    for h in (0, 1):
        add_out_grad(h, (zs // 2 - 1, 1 - zs // 2, zs // 2))
        og_send[0, sides[h], :] = og_acc[sides[h], lane(k3)].astype(bf16)
        og_a[h].send(
            og_send.at[0, sides[h]], og_recv.at[0, sides[h]], x_peer(1, 0), 2 * block_u
        )
        og_send[1, sides[h], :] = og_acc[sides[h], lane(k1)].astype(bf16)
        og_b.send(
            og_send.at[1, sides[h]], og_recv.at[1, sides[h]], x_peer(1, 0), 2 * block_u
        )

    mix_1.wait()

    far_rows = pl.ds(pl.multiple_of((1 - lax.div(k, 2)) * side, side), side)
    near_rows = pl.ds(pl.multiple_of(lax.div(k, 2) * side, side), side)
    fin_parts = []

    def output_part(part_rows):
        for n in range(ys):
            cols = slice(n * wide, (n + 1) * wide)
            fp[part_rows, cols] = jnp.dot(
                mixed_all[part_rows, :], wall[:, cols], preferred_element_type=f32
            ).astype(bf16)
        batch = Batch(out_y)
        for d in y_order:
            batch.send(
                fp.at[part_rows, pair(ymod(d))],
                frecv.at[{1: 0, -1: 1, 2: 2}[d], part_rows, :], y_peer(d), 4 * block_u,
            )
        fin_parts.append(batch)

    output_part(far_rows)
    def weight_term(d):
        block = lane(zmod(d))
        gp[:, block] = lax.dot_general(
            mixed_all[...], cotall[:, block], (((0,), (0,)), ((), ())),
            preferred_element_type=f32,
        ).astype(bf16)

    sums = {}
    slots = {}
    for h in range(1, zs // 2 + 1):
        for long in (0, 1):
            for d, c, hops in ways[long]:
                if h <= hops:
                    slots[d, c, h] = len(slots)

    def weight_sum_hop(h, long):
        for q in (0, 1):
            if h > 1:
                sums[h - 1, long, q].wait()
            if h > ways[long][0][2]:
                continue
            sums[h, long, q] = Batch(out_s)
            part = pl.ds(q * (half // 2), half // 2)
            for d, c, hops in ways[long]:
                block = lane(zmod(d * (hops - h + 1)))
                if h == 1:
                    src = gp.at[quarter(c, q), block]
                else:
                    slot = slots[d, c, h - 1]
                    rsbuf[slot, part, :] = (
                        rsbuf[slot, part, :].astype(f32) + gp[quarter(c, q), block].astype(f32)
                    ).astype(bf16)
                    src = rsbuf.at[slot, part]
                sums[h, long, q].send(
                    src, rsbuf.at[slots[d, c, h], part], z_peer(d), chunk_u // 2
                )

    weight_term(zs // 2)
    weight_sum_hop(1, 0)
    og_c = Batch(out_x)
    for h in (0, 1):
        og_a[h].wait()
        og_send[2, sides[h], :] = (
            og_acc[sides[h], lane(k2)] + og_recv[0, sides[h], :].astype(f32)
        ).astype(bf16)
        og_c.send(
            og_send.at[2, sides[h]], og_recv.at[2, sides[h]], x_peer(2, 0), 2 * block_u
        )
    weight_term(zs // 2 - 1)
    weight_term(1 - zs // 2)
    weight_sum_hop(1, 1)
    output_part(near_rows)
    for d in range(2 - zs // 2, zs // 2 - 1):
        weight_term(d)
    weight_sum_hop(2, 0)

    og_b.wait()
    og_c.wait()
    og = og_acc[:, lane(k)] + og_recv[1].astype(f32) + og_recv[2].astype(f32)
    og = og.astype(bf16).astype(f32)
    cg_f[...] = og * gateg[...].astype(f32)
    prefix(ends(cg_f, True), pre_b, True, b_all)
    b_batch = to_z(b_all, 1)
    weight_sum_hop(2, 1)
    gates_g[...] = (og * co_f[...]).astype(bf16)
    gate_batch = Batch(out_x)
    for d in g_order:
        gate_batch.send(gates_g.at[row(kp[d]), :], gg_ref.at[:, lane(k)], x_peer(d, 0), block_u)
    gg_ref[:, lane(k)] = gates_g[row(k), :]

    def residue_body(s, carry):
        state, sums_m = carry
        value = x_f[at_step(s), :]
        grad = cg_f[at_step(s), :]
        state = tuple(decays[m] * state[m] + value for m in range(MODES))
        return state, tuple(sums_m[m] + grad * state[m] for m in range(MODES))

    _, mode_sums = lax.fori_loop(
        0, step_len, residue_body,
        (tuple(pre_f[m] for m in range(MODES)), (zero,) * MODES), unroll=8,
    )
    for m in range(MODES):
        l_s[m : m + 1, :] = jnp.sum(mode_sums[m], axis=0, keepdims=True)
    l_all[z] = l_s[...].astype(bf16)
    skip_all[z] = jnp.sum(cg_f[...] * x_f[...], axis=0, keepdims=True)
    l_batch = to_z(l_all, 1)
    skip_batch = Batch(out_one)
    for d in z_order:
        skip_batch.send(skip_all.at[z], skip_all.at[z], z_peer(d), 1)
    weight_sum_hop(3, 0)

    sweep(cg_f, co_f, tuple(pre_b[m] for m in range(MODES)), True)
    out_batch = Batch(out_x)

    def finish(batch, part_rows, order):
        batch.wait()
        fin = fp[part_rows, pair(y)].astype(f32)
        for n in range(ys - 1):
            fin = fin + frecv[n, part_rows, :].astype(f32)
        fin_y[part_rows, :] = fin.astype(bf16)
        for dk, dx in order:
            out_batch.send(
                fin_y.at[row(kp[dk]), lane(xp[dx])], fin_pos.at[xl, :, lane(k)],
                x_peer(dk, dx), block_u,
            )

    finish(fin_parts[0], far_rows, [(dk, dx) for dk in (2, 3) for dx in (1, 0)])
    b_batch.wait()
    add_carried(co_f, carried(b_all, True), True)
    ggrp[...] = co_f[...].astype(bf16)
    gg_batch = Batch(out_x)
    for d in g_order:
        gg_batch.send(ggrp.at[row(kp[d]), :], ggpos.at[:, lane(k)], x_peer(d, 0), block_u)
    ggpos[:, lane(k)] = ggrp[row(k), :]
    weight_sum_hop(3, 1)
    weight_sum_hop(4, 0)

    l_batch.wait()
    skip_batch.wait()
    total = l_all[0].astype(f32)
    for n in range(1, zs):
        total = total + l_all[n].astype(f32)
    tot_all[0:MODES, lane(k)] = total[0:MODES] * inv_norm * scale
    total = skip_all[0]
    for n in range(1, zs):
        total = total + skip_all[n]
    tot_all[MODES : MODES + SUBS, lane(k)] = spread(total, 0) * scale
    tot_batch = Batch(out_zs)
    for d in g_order:
        tot_batch.send(tot_all.at[:, lane(k)], tot_all.at[:, lane(k)], x_peer(d, 0), 3)
    finish(fin_parts[1], near_rows, [(0, 1), (1, 1), (1, 0)])
    fin_pos[xl, :, lane(k)] = fin_y[row(k), lane(xl)]

    writes = []

    def write(n, src, dst):
        copy = pltpu.make_async_copy(src, dst, load_sems.at[n])
        copy.start()
        writes.append(copy)

    gg_batch.wait()
    spread_grad = ggpos[...].astype(f32)
    gq_ref[...] = (spread_grad * key_ref[...].astype(f32)).astype(bf16)
    gk_ref[...] = (spread_grad * q_ref[...].astype(f32)).astype(bf16)
    write(1, gq_ref, gq_hbm)
    write(2, gk_ref, gk_hbm)
    gate_batch.wait()
    write(3, gg_ref, gg_hbm)

    weight_sum_hop(4, 1)
    weight_sum_hop(5, 0)
    for c in (0, 1):
        part = gp[chunk[c], lane(z)].astype(f32)
        for long in (0, 1):
            for d, other, hops in ways[long]:
                if other == c:
                    part = part + rsbuf[slots[d, c, hops]].astype(f32)
        gw_ref[chunk[c], :] = (part * scale).astype(bf16)
    write(4, gw_ref, gw_hbm)

    tot_batch.wait()
    write(5, tot_all.at[pl.ds(0, MODES), :], gres_hbm)
    write(6, tot_all.at[pl.ds(MODES, 1), :], gskip_hbm)
    out_batch.wait()
    final_ref[...] = (fin_pos[0].astype(f32) + fin_pos[1].astype(f32)).astype(bf16)
    write(0, final_ref, final_hbm)
    for out in (out_x, out_y, out_z, out_zs, out_s, out_one):
        out.wait()
    for copy in writes:
        copy.wait()
    assert counts == [RECEIVES, SENDS], counts


def store_kernel(*refs):
    count = (len(refs) - 2) // 3
    srcs, dsts, bufs = refs[:count], refs[count : 2 * count], refs[2 * count : 3 * count]
    in_sems, out_sems = refs[3 * count :]
    reads = [pltpu.make_async_copy(srcs[n], bufs[n], in_sems.at[n]) for n in range(count)]
    writes = [pltpu.make_async_copy(bufs[n], dsts[n], out_sems.at[n]) for n in range(count)]
    for copy in reads:
        copy.start()
    for read, write in zip(reads, writes):
        read.wait()
        write.start()
    for copy in writes:
        copy.wait()


def shards(mesh, *args):
    q, key_input, gate, cot, weight, rates, residues, skip = args
    zs, chans = mesh.shape["ctx"] // GROUP, mesh.shape["chan"]
    rows, width = q.shape
    depth = weight.shape[0]
    span = rows * GROUP
    length = rows * mesh.shape["ctx"]
    columns = zs * LANES
    hbm = pl.BlockSpec(memory_space=pltpu.HBM)
    shape = jax.ShapeDtypeStruct
    out_shape = (
        shape((rows, width), bf16),
        shape((rows, width), bf16),
        shape((rows, width), bf16),
        shape((rows, width), bf16),
        shape((depth, LANES), bf16),
        shape((MODES, width), f32),
        shape((1, width), f32),
    )
    outs = pl.pallas_call(
        functools.partial(kernel, zs, chans, length),
        out_shape=out_shape,
        in_specs=[hbm] * 8,
        out_specs=(hbm,) * 7,
        scratch_shapes=[
            pltpu.VMEM((rows, width), bf16),
            pltpu.VMEM((rows, width), bf16),
            pltpu.VMEM((rows, width), bf16),
            pltpu.VMEM((rows, width), bf16),
            pltpu.VMEM((depth, LANES), bf16),
            pltpu.VMEM((MODES, width), f32),
            pltpu.VMEM((MODES, width), f32),
            pltpu.VMEM((1, width), f32),
            pltpu.VMEM((rows, width), bf16),
            pltpu.VMEM((rows, width), bf16),
            pltpu.VMEM((span, columns), bf16),
            pltpu.VMEM((depth, columns), bf16),
            pltpu.VMEM((span, LANES), bf16),
            pltpu.VMEM((span, LANES), bf16),
            pltpu.VMEM((span, LANES), f32),
            pltpu.VMEM((span, LANES), f32),
            pltpu.VMEM((span, LANES), f32),
            pltpu.VMEM((MODES, SUBS, LANES), f32),
            pltpu.VMEM((MODES, SUBS, LANES), f32),
            pltpu.VMEM((zs, MODES, LANES), bf16),
            pltpu.VMEM((zs, MODES, LANES), bf16),
            pltpu.VMEM((MODES, LANES), f32),
            pltpu.VMEM((MODES, LANES), f32),
            pltpu.VMEM((zs, MODES, LANES), bf16),
            pltpu.VMEM((zs, 1, LANES), f32),
            pltpu.VMEM((zs, 1, LANES), f32),
            pltpu.VMEM((span, width), bf16),
            pltpu.VMEM((span, width), f32),
            pltpu.VMEM((3, span, LANES), bf16),
            pltpu.VMEM((3, span, LANES), bf16),
            pltpu.VMEM((span, columns), bf16),
            pltpu.VMEM((chans // PAIR - 1, span, PAIR * LANES), bf16),
            pltpu.VMEM((span, PAIR * LANES), bf16),
            pltpu.VMEM((PAIR, rows, width), bf16),
            pltpu.VMEM((depth, columns), bf16),
            pltpu.VMEM((2 * (zs - 1), depth // 2, LANES), bf16),
            pltpu.VMEM((span, LANES), bf16),
            pltpu.VMEM((rows, width), bf16),
            pltpu.VMEM((span, LANES), bf16),
            pltpu.VMEM((MODES + 8, width), f32),
            pltpu.VMEM((512, 16, LANES), bf16),
            *[pltpu.VMEM(a.shape, a.dtype) for a in out_shape[:5]],
            pltpu.SemaphoreType.DMA((RECEIVES,)),
            pltpu.SemaphoreType.DMA((SENDS,)),
            pltpu.SemaphoreType.DMA((8,)),
        ],
        compiler_params=pltpu.CompilerParams(
            collective_id=0, has_side_effects=True, vmem_limit_bytes=65000 * 1024
        ),
    )(q, key_input, gate, cot, weight, rates.T, residues.T, skip.reshape(1, -1))
    outs = pl.pallas_call(
        store_kernel,
        out_shape=out_shape,
        in_specs=[hbm] * 7,
        out_specs=(hbm,) * 7,
        scratch_shapes=[
            *[pltpu.VMEM(a.shape, a.dtype) for a in out_shape],
            pltpu.SemaphoreType.DMA((7,)),
            pltpu.SemaphoreType.DMA((7,)),
        ],
        compiler_params=pltpu.CompilerParams(vmem_limit_bytes=65000 * 1024),
    )(*outs)
    return (*outs[:5], outs[5].T, outs[6].reshape(-1))


def solution(mesh):
    placed = (
        P("ctx", "chan"),
        P("ctx", "chan"),
        P("ctx", "chan"),
        P("ctx", "chan"),
        P("chan", "ctx"),
        P("chan", None),
        P("chan", None),
        P("chan"),
    )
    return jax.shard_map(
        functools.partial(shards, mesh),
        mesh=mesh,
        in_specs=placed,
        out_specs=(
            P("ctx", "chan"),
            P("ctx", "chan"),
            P("ctx", "chan"),
            P("ctx", "chan"),
            P("chan", "ctx"),
            P("chan", None),
            P("chan"),
        ),
        check_vma=False,
    )
```

```python
import functools
import math

import jax
import jax.numpy as jnp
from jax import lax
from jax.experimental import pallas as pl
from jax.experimental.pallas import tpu as pltpu
from jax.sharding import PartitionSpec as P

MESH = pl.DeviceIdType.MESH
f32 = jnp.float32
bf16 = jnp.bfloat16

GROUP = 4
PAIR = 2
LANES = 128
SUBS = 8
MODES = 16
RECEIVES = 52
SENDS = 7


def one_minus_exp(x):
    series = jnp.ones_like(x)
    for n in range(9, 1, -1):
        series = 1.0 - x * (1.0 / n) * series
    return jnp.where(x < 0.5, x * series, 1.0 - jnp.exp(-x))


def kernel(
    zs, chans, length,
    q_hbm, key_hbm, gate_hbm, cot_hbm, w_hbm, rate_hbm, res_hbm, skip_hbm,
    final_hbm, gq_hbm, gk_hbm, gg_hbm, gw_hbm, gres_hbm, gskip_hbm,
    q_ref, key_ref, gate_ref, cot_ref, w_ref, rate_ref, res_ref, skip_ref,
    gat_s, two_ref, cotall, wall, xg, gateg, x_f, co_f, cg_f, pre_f, pre_b, e_all, b_all, ends_s, l_s, l_all, skip_all, sizes_one,
    mixed_all, og_acc, og_send, og_recv, fp, frecv, fin_y, fin_pos, gp, rsbuf,
    ggrp, ggpos, gates_g, tot_all, sizes,
    final_ref, gq_ref, gk_ref, gg_ref, gw_ref,
    recv_sems, send_sems, load_sems,
):
    rows = q_ref.shape[0]
    span = rows * GROUP
    step_len = span // SUBS
    half = w_ref.shape[0] // 2
    ys = chans // PAIR
    wide = PAIR * LANES
    scale = 1.0 / math.sqrt(length)

    i = lax.axis_index("ctx")
    j = lax.axis_index("chan")
    z = lax.div(i, GROUP)
    k = lax.rem(i, GROUP)
    y = lax.div(j, PAIR)
    xl = lax.rem(j, PAIR)
    k1 = k + 1 - 2 * lax.rem(k, 2)
    k2 = lax.rem(k + 2, GROUP)
    k3 = GROUP - 1 - k
    kp = {0: k, 1: k1, 2: k2, 3: k3}
    xp = {0: xl, 1: PAIR - 1 - xl}

    def zmod(d):
        return lax.rem(z + d + zs, zs)

    def ymod(d):
        return lax.rem(y + d + ys, ys)

    def x_peer(dk, dx):
        return {"ctx": z * GROUP + kp[dk], "chan": y * PAIR + xp[dx]}

    def z_peer(d):
        return {"ctx": zmod(d) * GROUP + k, "chan": j}

    def y_peer(d):
        return {"ctx": i, "chan": ymod(d) * PAIR + xl}

    x_order = [(dk, dx) for dk in (2, 3, 1, 0) for dx in (1, 0) if dk or dx]
    g_order = (2, 3, 1)
    z_order = [zs // 2] + [d for n in range(zs // 2 - 1, 0, -1) for d in (n, -n)]

    def lane(index):
        return pl.ds(pl.multiple_of(index * LANES, LANES), LANES)

    def pair(index):
        return pl.ds(pl.multiple_of(index * wide, wide), wide)

    def row(index):
        return pl.ds(pl.multiple_of(index * rows, rows), rows)

    counts = [0, 0]

    class Batch:
        def __init__(self, lane_class):
            self.recv = recv_sems.at[counts[0]]
            counts[0] += 1
            self.out = lane_class
            self.units = 0

        def send(self, src, dst, peer, units):
            pltpu.make_async_remote_copy(
                src_ref=src, dst_ref=dst, send_sem=self.out.sem, recv_sem=self.recv,
                device_id=peer, device_id_type=MESH,
            ).start()
            self.units += units
            self.out.units += units

        def wait(self):
            part = self.out.sizes.at[pl.ds(0, self.units)]
            pltpu.make_async_copy(part, part, self.recv).wait()

    class Outgoing:
        def __init__(self, size_ref=sizes):
            self.sizes = size_ref
            self.sem = send_sems.at[counts[1]]
            counts[1] += 1
            self.units = 0

        def wait(self):
            part = self.sizes.at[pl.ds(0, self.units)]
            pltpu.make_async_copy(part, part, self.sem).wait()

    block_u = rows // 16
    out_x, out_y, out_z, out_zs, out_s, first_z = (
        Outgoing() for _ in range(6)
    )
    out_one = Outgoing(sizes_one)

    barrier = pltpu.get_barrier_semaphore()
    peers = [x_peer(*d) for d in x_order]
    peers += [z_peer(d) for d in z_order]
    peers += [y_peer(d) for d in range(1, ys)]
    for peer in peers:
        pl.semaphore_signal(barrier, inc=1, device_id=peer, device_id_type=MESH)

    loads = [
        pltpu.make_async_copy(src, dst, load_sems.at[n])
        for n, (src, dst) in enumerate((
            (cot_hbm, cot_ref), (w_hbm, w_ref), (q_hbm, q_ref), (key_hbm, key_ref),
            (gate_hbm, gate_ref), (rate_hbm, rate_ref), (res_hbm, res_ref), (skip_hbm, skip_ref),
        ))
    ]
    for copy in loads:
        copy.start()

    pl.semaphore_wait(barrier, len(peers))

    chunk = (pl.ds(0, half), pl.ds(half, half))
    ways = {0: ((1, 0, zs // 2), (-1, 1, zs // 2)), 1: ((1, 1, zs // 2 - 1), (-1, 0, zs // 2 - 1))}
    ring = {}
    chunk_u = half // 16

    def quarter(c, q):
        return pl.ds(c * half + q * (half // 2), half // 2)

    def weight_hop(h, long):
        for q in (0, 1):
            if h > 1:
                ring[h - 1, long, q].wait()
            if h > ways[long][0][2]:
                continue
            ring[h, long, q] = Batch(first_z if (h, long) == (1, 0) else out_z)
            for d, c, hops in ways[long]:
                spot = (quarter(c, q), lane(zmod(-d * (h - 1))))
                src = w_hbm.at[spot[0], :] if h == 1 else wall.at[spot]
                ring[h, long, q].send(src, wall.at[spot], z_peer(d), chunk_u // 2)

    y_order = (2, 1, -1)
    cot_y = [Batch(out_y) for _ in range(3)]
    for d in (1, -1):
        cot_y[0].send(cot_hbm.at[:, lane(k)], cotall.at[row(k), lane(j)], y_peer(d), block_u)
    cot_two = Batch(out_y)
    cot_two.send(cot_hbm, two_ref, y_peer(2), 4 * block_u)
    weight_hop(1, 0)
    for copy in loads:
        copy.wait()
    gat_s[...] = (q_ref[...].astype(f32) * key_ref[...].astype(f32)).astype(bf16)
    signals = Batch(out_x)
    for d in g_order:
        signals.send(gat_s.at[:, lane(kp[d])], xg.at[row(k), :], x_peer(d, 0), block_u)
    cot_a = Batch(out_x)
    for d in g_order:
        cot_a.send(
            cot_hbm.at[:, lane(kp[d])], cotall.at[row(k), lane(j)], x_peer(d, 0), block_u
        )
    cotall[row(k), lane(j)] = cot_ref[:, lane(k)]
    xg[row(k), :] = gat_s[:, lane(k)]
    gateg[row(k), :] = gate_ref[:, lane(k)]
    wall[:, lane(z)] = w_ref[...]

    rate = rate_ref[:, lane(k)]
    inv_norm = jnp.sqrt(one_minus_exp(2.0 * rate) / one_minus_exp(2.0 * length * rate))
    gain = res_ref[:, lane(k)] * inv_norm
    decay = jnp.exp(-rate)
    decay_sub = jnp.exp(-step_len * rate)
    decay_span = jnp.exp(-span * rate)
    skip_b = jnp.broadcast_to(skip_ref[:, lane(k)], (SUBS, LANES))
    sub = lax.broadcasted_iota(jnp.int32, (SUBS, LANES), 0)

    def spread(table, m):
        return jnp.broadcast_to(table[m : m + 1, :], (SUBS, LANES))

    decays = [spread(decay, m) for m in range(MODES)]
    gains = [spread(gain, m) for m in range(MODES)]
    zero = jnp.zeros((SUBS, LANES), f32)

    def at_step(t):
        return pl.ds(t, SUBS, stride=step_len)

    def ends(src, backward):
        def body(s, state):
            t = step_len - 1 - s if backward else s
            value = src[at_step(t), :]
            return tuple(decays[m] * state[m] + value for m in range(MODES))

        return lax.fori_loop(0, step_len, body, (zero,) * MODES, unroll=8)

    def prefix(state, pre, backward, all_ref):
        for m in range(MODES):
            factor = spread(decay_sub, m)
            total = state[m]
            for shift in (1, 2, 4):
                moved = pltpu.roll(total, SUBS - shift if backward else shift, 0)
                keep = sub < SUBS - shift if backward else sub >= shift
                total = total + jnp.where(keep, factor * moved, 0.0)
                factor = factor * factor
            moved = pltpu.roll(total, SUBS - 1 if backward else 1, 0)
            pre[m] = jnp.where(sub < SUBS - 1 if backward else sub >= 1, moved, 0.0)
            edge = 0 if backward else SUBS - 1
            ends_s[m : m + 1, :] = total[edge : edge + 1, :]
        all_ref[z] = ends_s[...].astype(bf16)

    def carried(all_ref, backward):
        carry = jnp.zeros((MODES, LANES), f32)
        for n in range(zs):
            other = zs - 1 - n if backward else n
            ahead = z < other if backward else z > other
            carry = jnp.where(ahead, decay_span * carry + all_ref[other].astype(f32), carry)
        steps = (SUBS - 1 - sub if backward else sub).astype(f32)
        return tuple(
            jnp.exp(-step_len * steps * spread(rate, m)) * spread(carry, m)
            for m in range(MODES)
        )

    def tree(terms):
        while len(terms) > 1:
            terms = [a + b for a, b in zip(terms[::2], terms[1::2])]
        return terms[0]

    def sweep(src, out, state, backward):
        def body(s, state):
            t = step_len - 1 - s if backward else s
            value = src[at_step(t), :]
            state = tuple(decays[m] * state[m] + value for m in range(MODES))
            out[at_step(t), :] = (
                tree([gains[m] * state[m] for m in range(MODES)]) + skip_b * value
            )
            return state

        lax.fori_loop(0, step_len, body, state, unroll=8)

    def add_carried(out, state, backward):
        def body(s, state):
            t = step_len - 1 - s if backward else s
            state = tuple(decays[m] * state[m] for m in range(MODES))
            out[at_step(t), :] += tree(list(state))
            return state

        lax.fori_loop(0, step_len, body, tuple(gains[m] * state[m] for m in range(MODES)), unroll=8)

    def to_z(ref, units):
        batch = Batch(out_zs)
        for d in z_order:
            batch.send(ref.at[z], ref.at[z], z_peer(d), units)
        return batch

    first_z.wait()
    weight_hop(1, 1)
    cot_b = Batch(out_x)
    for dk in (1, 3, 2, 0):
        cot_b.send(
            cot_ref.at[:, lane(kp[dk])], cotall.at[row(k), lane(j)], x_peer(dk, 1), block_u
        )
    weight_hop(2, 0)
    gates_in = Batch(out_x)
    for d in g_order:
        gates_in.send(gate_ref.at[:, lane(kp[d])], gateg.at[row(k), :], x_peer(d, 0), block_u)
    signals.wait()
    x_f[...] = xg[...].astype(f32)
    prefix(ends(x_f, False), pre_f, False, e_all)
    e_batch = to_z(e_all, 1)
    cot_a.wait()
    for dy in (1, -1):
        for d in (1, 2, 3):
            piece = (row(kp[d]), lane(j))
            cot_y[1].send(cotall.at[piece], cotall.at[piece], y_peer(dy), block_u)
    weight_hop(2, 1)
    cot_two.wait()
    cot_spread = Batch(out_x)
    j_two = lane(ymod(2) * PAIR + xl)
    for dk, dx in x_order:
        cot_spread.send(
            two_ref.at[:, lane(kp[dk])], cotall.at[row(k), j_two], x_peer(dk, dx), block_u
        )
    cotall[row(k), j_two] = two_ref[:, lane(k)]
    cot_b.wait()
    other = (slice(None), lane(y * PAIR + xp[1]))
    for dy in (1, -1):
        cot_y[2].send(cotall.at[other], cotall.at[other], y_peer(dy), 4 * block_u)
    weight_hop(3, 0)
    sweep(x_f, co_f, tuple(pre_f[m] for m in range(MODES)), False)
    e_batch.wait()
    start_f = carried(e_all, False)
    add_carried(co_f, start_f, False)
    gates_in.wait()
    mixed_all[:, lane(k)] = (gateg[...].astype(f32) * co_f[...]).astype(bf16)
    mix_2 = Batch(out_x)
    mix_2.send(mixed_all.at[:, lane(k)], mixed_all.at[:, lane(k)], x_peer(2, 0), 4 * block_u)
    mix_1 = Batch(out_x)
    mix_1.send(mixed_all.at[:, lane(k)], mixed_all.at[:, lane(k)], x_peer(1, 0), 4 * block_u)
    weight_hop(3, 1)
    weight_hop(4, 0)
    for m in range(MODES):
        pre_f[m] += start_f[m]
    side = span // 2
    sides = [pl.ds(h * side, side) for h in (0, 1)]

    def add_out_grad(h, steps):
        for d in steps:
            block = lane(zmod(d))
            part = lax.dot_general(
                cotall[sides[h], block], wall[:, block], (((1,), (1,)), ((), ())),
                preferred_element_type=f32,
            )
            if d == 0:
                og_acc[sides[h], :] = part
            else:
                og_acc[sides[h], :] += part

    for batch in (*cot_y, cot_spread):
        batch.wait()
    for h in (0, 1):
        add_out_grad(h, (0, 1, -1, 2, -2))
    mix_2.wait()
    mix_1.send(mixed_all.at[:, lane(k2)], mixed_all.at[:, lane(k2)], x_peer(1, 0), 4 * block_u)
    weight_hop(4, 1)
    weight_hop(5, 0)
    og_a = [Batch(out_x), Batch(out_x)]
    og_b = Batch(out_x)
    for h in (0, 1):
        add_out_grad(h, (zs // 2 - 1, 1 - zs // 2, zs // 2))
        og_send[0, sides[h], :] = og_acc[sides[h], lane(k3)].astype(bf16)
        og_a[h].send(
            og_send.at[0, sides[h]], og_recv.at[0, sides[h]], x_peer(1, 0), 2 * block_u
        )
        og_send[1, sides[h], :] = og_acc[sides[h], lane(k1)].astype(bf16)
        og_b.send(
            og_send.at[1, sides[h]], og_recv.at[1, sides[h]], x_peer(1, 0), 2 * block_u
        )

    mix_1.wait()

    far_rows = pl.ds(pl.multiple_of((1 - lax.div(k, 2)) * side, side), side)
    near_rows = pl.ds(pl.multiple_of(lax.div(k, 2) * side, side), side)
    fin_parts = []

    def output_part(part_rows):
        for n in range(ys):
            cols = slice(n * wide, (n + 1) * wide)
            fp[part_rows, cols] = jnp.dot(
                mixed_all[part_rows, :], wall[:, cols], preferred_element_type=f32
            ).astype(bf16)
        batch = Batch(out_y)
        for d in y_order:
            batch.send(
                fp.at[part_rows, pair(ymod(d))],
                frecv.at[{1: 0, -1: 1, 2: 2}[d], part_rows, :], y_peer(d), 4 * block_u,
            )
        fin_parts.append(batch)

    output_part(far_rows)
    def weight_term(d):
        block = lane(zmod(d))
        gp[:, block] = lax.dot_general(
            mixed_all[...], cotall[:, block], (((0,), (0,)), ((), ())),
            preferred_element_type=f32,
        ).astype(bf16)

    sums = {}
    slots = {}
    for h in range(1, zs // 2 + 1):
        for long in (0, 1):
            for d, c, hops in ways[long]:
                if h <= hops:
                    slots[d, c, h] = len(slots)

    def weight_sum_hop(h, long):
        for q in (0, 1):
            if h > 1:
                sums[h - 1, long, q].wait()
            if h > ways[long][0][2]:
                continue
            sums[h, long, q] = Batch(out_s)
            part = pl.ds(q * (half // 2), half // 2)
            for d, c, hops in ways[long]:
                block = lane(zmod(d * (hops - h + 1)))
                if h == 1:
                    src = gp.at[quarter(c, q), block]
                else:
                    slot = slots[d, c, h - 1]
                    rsbuf[slot, part, :] = (
                        rsbuf[slot, part, :].astype(f32) + gp[quarter(c, q), block].astype(f32)
                    ).astype(bf16)
                    src = rsbuf.at[slot, part]
                sums[h, long, q].send(
                    src, rsbuf.at[slots[d, c, h], part], z_peer(d), chunk_u // 2
                )

    weight_term(zs // 2)
    weight_sum_hop(1, 0)
    for h in (0, 1):
        og_a[h].wait()
        og_send[2, sides[h], :] = (
            og_acc[sides[h], lane(k2)] + og_recv[0, sides[h], :].astype(f32)
        ).astype(bf16)
        og_b.send(
            og_send.at[2, sides[h]], og_recv.at[2, sides[h]], x_peer(2, 0), 2 * block_u
        )
    weight_term(zs // 2 - 1)
    weight_term(1 - zs // 2)
    weight_sum_hop(1, 1)
    output_part(near_rows)
    for d in range(2 - zs // 2, zs // 2 - 1):
        weight_term(d)
    weight_sum_hop(2, 0)

    og_b.wait()
    og = og_acc[:, lane(k)] + og_recv[1].astype(f32) + og_recv[2].astype(f32)
    og = og.astype(bf16).astype(f32)
    cg_f[...] = og * gateg[...].astype(f32)
    prefix(ends(cg_f, True), pre_b, True, b_all)
    b_batch = to_z(b_all, 1)
    weight_sum_hop(2, 1)
    gates_g[...] = (og * co_f[...]).astype(bf16)
    gg_batch = Batch(out_x)
    for d in g_order:
        gg_batch.send(gates_g.at[row(kp[d]), :], gg_ref.at[:, lane(k)], x_peer(d, 0), block_u)
    gg_ref[:, lane(k)] = gates_g[row(k), :]

    def residue_body(s, carry):
        state, sums_m = carry
        value = x_f[at_step(s), :]
        grad = cg_f[at_step(s), :]
        state = tuple(decays[m] * state[m] + value for m in range(MODES))
        return state, tuple(sums_m[m] + grad * state[m] for m in range(MODES))

    _, mode_sums = lax.fori_loop(
        0, step_len, residue_body,
        (tuple(pre_f[m] for m in range(MODES)), (zero,) * MODES), unroll=8,
    )
    for m in range(MODES):
        l_s[m : m + 1, :] = jnp.sum(mode_sums[m], axis=0, keepdims=True)
    l_all[z] = l_s[...].astype(bf16)
    skip_all[z] = jnp.sum(cg_f[...] * x_f[...], axis=0, keepdims=True)
    l_batch = to_z(l_all, 1)
    skip_batch = Batch(out_one)
    for d in z_order:
        skip_batch.send(skip_all.at[z], skip_all.at[z], z_peer(d), 1)
    weight_sum_hop(3, 0)

    sweep(cg_f, co_f, tuple(pre_b[m] for m in range(MODES)), True)
    out_far, out_near = Batch(out_x), Batch(out_x)

    def finish(batch, part_rows, order, out_batch):
        batch.wait()
        fin = fp[part_rows, pair(y)].astype(f32)
        for n in range(ys - 1):
            fin = fin + frecv[n, part_rows, :].astype(f32)
        fin_y[part_rows, :] = fin.astype(bf16)
        for dk, dx in order:
            out_batch.send(
                fin_y.at[row(kp[dk]), lane(xp[dx])], fin_pos.at[xl, :, lane(k)],
                x_peer(dk, dx), block_u,
            )

    finish(fin_parts[0], far_rows, [(dk, dx) for dk in (2, 3) for dx in (1, 0)], out_far)
    b_batch.wait()
    add_carried(co_f, carried(b_all, True), True)
    ggrp[...] = co_f[...].astype(bf16)
    for d in g_order:
        gg_batch.send(ggrp.at[row(kp[d]), :], ggpos.at[:, lane(k)], x_peer(d, 0), block_u)
    ggpos[:, lane(k)] = ggrp[row(k), :]
    weight_sum_hop(3, 1)
    weight_sum_hop(4, 0)

    l_batch.wait()
    skip_batch.wait()
    total = l_all[0].astype(f32)
    for n in range(1, zs):
        total = total + l_all[n].astype(f32)
    tot_all[0:MODES, lane(k)] = total[0:MODES] * inv_norm * scale
    total = skip_all[0]
    for n in range(1, zs):
        total = total + skip_all[n]
    tot_all[MODES : MODES + SUBS, lane(k)] = spread(total, 0) * scale
    tot_batch = Batch(out_zs)
    for d in g_order:
        tot_batch.send(tot_all.at[:, lane(k)], tot_all.at[:, lane(k)], x_peer(d, 0), 3)
    finish(fin_parts[1], near_rows, [(0, 1), (1, 1), (1, 0)], out_near)
    fin_pos[xl, :, lane(k)] = fin_y[row(k), lane(xl)]

    writes = []

    def write(n, src, dst):
        copy = pltpu.make_async_copy(src, dst, load_sems.at[n])
        copy.start()
        writes.append(copy)

    gg_batch.wait()
    spread_grad = ggpos[...].astype(f32)
    gq_ref[...] = (spread_grad * key_ref[...].astype(f32)).astype(bf16)
    gk_ref[...] = (spread_grad * q_ref[...].astype(f32)).astype(bf16)
    write(1, gq_ref, gq_hbm)
    write(2, gk_ref, gk_hbm)
    write(3, gg_ref, gg_hbm)

    weight_sum_hop(4, 1)
    weight_sum_hop(5, 0)
    for c in (0, 1):
        part = gp[chunk[c], lane(z)].astype(f32)
        for long in (0, 1):
            for d, other, hops in ways[long]:
                if other == c:
                    part = part + rsbuf[slots[d, c, hops]].astype(f32)
        gw_ref[chunk[c], :] = (part * scale).astype(bf16)
    write(4, gw_ref, gw_hbm)

    tot_batch.wait()
    write(5, tot_all.at[pl.ds(0, MODES), :], gres_hbm)
    write(6, tot_all.at[pl.ds(MODES, 1), :], gskip_hbm)
    def write_output(n, batch, block):
        batch.wait()
        spot = (slice(None), pair(block))
        final_ref[spot] = (
            fin_pos[0, :, pair(block)].astype(f32) + fin_pos[1, :, pair(block)].astype(f32)
        ).astype(bf16)
        write(n, final_ref.at[spot], final_hbm.at[spot])

    write_output(7, out_far, 1 - lax.div(k, 2))
    write_output(0, out_near, lax.div(k, 2))
    for out in (out_x, out_y, out_z, out_zs, out_s, out_one):
        out.wait()
    for copy in writes:
        copy.wait()
    assert counts == [RECEIVES, SENDS], counts


def store_kernel(*refs):
    count = (len(refs) - 2) // 3
    srcs, dsts, bufs = refs[:count], refs[count : 2 * count], refs[2 * count : 3 * count]
    in_sems, out_sems = refs[3 * count :]
    reads = [pltpu.make_async_copy(srcs[n], bufs[n], in_sems.at[n]) for n in range(count)]
    writes = [pltpu.make_async_copy(bufs[n], dsts[n], out_sems.at[n]) for n in range(count)]
    for copy in reads:
        copy.start()
    for read, write in zip(reads, writes):
        read.wait()
        write.start()
    for copy in writes:
        copy.wait()


def shards(mesh, *args):
    q, key_input, gate, cot, weight, rates, residues, skip = args
    zs, chans = mesh.shape["ctx"] // GROUP, mesh.shape["chan"]
    rows, width = q.shape
    depth = weight.shape[0]
    span = rows * GROUP
    length = rows * mesh.shape["ctx"]
    columns = zs * LANES
    hbm = pl.BlockSpec(memory_space=pltpu.HBM)
    shape = jax.ShapeDtypeStruct
    out_shape = (
        shape((rows, width), bf16),
        shape((rows, width), bf16),
        shape((rows, width), bf16),
        shape((rows, width), bf16),
        shape((depth, LANES), bf16),
        shape((MODES, width), f32),
        shape((1, width), f32),
    )
    outs = pl.pallas_call(
        functools.partial(kernel, zs, chans, length),
        out_shape=out_shape,
        in_specs=[hbm] * 8,
        out_specs=(hbm,) * 7,
        scratch_shapes=[
            pltpu.VMEM((rows, width), bf16),
            pltpu.VMEM((rows, width), bf16),
            pltpu.VMEM((rows, width), bf16),
            pltpu.VMEM((rows, width), bf16),
            pltpu.VMEM((depth, LANES), bf16),
            pltpu.VMEM((MODES, width), f32),
            pltpu.VMEM((MODES, width), f32),
            pltpu.VMEM((1, width), f32),
            pltpu.VMEM((rows, width), bf16),
            pltpu.VMEM((rows, width), bf16),
            pltpu.VMEM((span, columns), bf16),
            pltpu.VMEM((depth, columns), bf16),
            pltpu.VMEM((span, LANES), bf16),
            pltpu.VMEM((span, LANES), bf16),
            pltpu.VMEM((span, LANES), f32),
            pltpu.VMEM((span, LANES), f32),
            pltpu.VMEM((span, LANES), f32),
            pltpu.VMEM((MODES, SUBS, LANES), f32),
            pltpu.VMEM((MODES, SUBS, LANES), f32),
            pltpu.VMEM((zs, MODES, LANES), bf16),
            pltpu.VMEM((zs, MODES, LANES), bf16),
            pltpu.VMEM((MODES, LANES), f32),
            pltpu.VMEM((MODES, LANES), f32),
            pltpu.VMEM((zs, MODES, LANES), bf16),
            pltpu.VMEM((zs, 1, LANES), f32),
            pltpu.VMEM((zs, 1, LANES), f32),
            pltpu.VMEM((span, width), bf16),
            pltpu.VMEM((span, width), f32),
            pltpu.VMEM((3, span, LANES), bf16),
            pltpu.VMEM((3, span, LANES), bf16),
            pltpu.VMEM((span, columns), bf16),
            pltpu.VMEM((chans // PAIR - 1, span, PAIR * LANES), bf16),
            pltpu.VMEM((span, PAIR * LANES), bf16),
            pltpu.VMEM((PAIR, rows, width), bf16),
            pltpu.VMEM((depth, columns), bf16),
            pltpu.VMEM((2 * (zs - 1), depth // 2, LANES), bf16),
            pltpu.VMEM((span, LANES), bf16),
            pltpu.VMEM((rows, width), bf16),
            pltpu.VMEM((span, LANES), bf16),
            pltpu.VMEM((MODES + 8, width), f32),
            pltpu.VMEM((512, 16, LANES), bf16),
            *[pltpu.VMEM(a.shape, a.dtype) for a in out_shape[:5]],
            pltpu.SemaphoreType.DMA((RECEIVES,)),
            pltpu.SemaphoreType.DMA((SENDS,)),
            pltpu.SemaphoreType.DMA((8,)),
        ],
        compiler_params=pltpu.CompilerParams(
            collective_id=0, has_side_effects=True, vmem_limit_bytes=65000 * 1024
        ),
    )(q, key_input, gate, cot, weight, rates.T, residues.T, skip.reshape(1, -1))
    outs = pl.pallas_call(
        store_kernel,
        out_shape=out_shape,
        in_specs=[hbm] * 7,
        out_specs=(hbm,) * 7,
        scratch_shapes=[
            *[pltpu.VMEM(a.shape, a.dtype) for a in out_shape],
            pltpu.SemaphoreType.DMA((7,)),
            pltpu.SemaphoreType.DMA((7,)),
        ],
        compiler_params=pltpu.CompilerParams(vmem_limit_bytes=65000 * 1024),
    )(*outs)
    return (*outs[:5], outs[5].T, outs[6].reshape(-1))


def solution(mesh):
    placed = (
        P("ctx", "chan"),
        P("ctx", "chan"),
        P("ctx", "chan"),
        P("ctx", "chan"),
        P("chan", "ctx"),
        P("chan", None),
        P("chan", None),
        P("chan"),
    )
    return jax.shard_map(
        functools.partial(shards, mesh),
        mesh=mesh,
        in_specs=placed,
        out_specs=(
            P("ctx", "chan"),
            P("ctx", "chan"),
            P("ctx", "chan"),
            P("ctx", "chan"),
            P("chan", "ctx"),
            P("chan", None),
            P("chan"),
        ),
        check_vma=False,
    )
```

```python
import functools
import math

import jax
import jax.numpy as jnp
from jax import lax
from jax.experimental import pallas as pl
from jax.experimental.pallas import tpu as pltpu
from jax.sharding import PartitionSpec as P

MESH = pl.DeviceIdType.MESH
f32 = jnp.float32
bf16 = jnp.bfloat16

GROUP = 4
PAIR = 2
LANES = 128
SUBS = 8
MODES = 16
RECEIVES = 53
SENDS = 7


def one_minus_exp(x):
    series = jnp.ones_like(x)
    for n in range(9, 1, -1):
        series = 1.0 - x * (1.0 / n) * series
    return jnp.where(x < 0.5, x * series, 1.0 - jnp.exp(-x))


def kernel(
    zs, chans, length,
    q_hbm, key_hbm, gate_hbm, cot_hbm, w_hbm, rate_hbm, res_hbm, skip_hbm,
    final_hbm, gq_hbm, gk_hbm, gg_hbm, gw_hbm, gres_hbm, gskip_hbm,
    q_ref, key_ref, gate_ref, cot_ref, w_ref, rate_ref, res_ref, skip_ref,
    gat_s, two_ref, cotall, wall, xg, gateg, x_f, co_f, cg_f, pre_f, pre_b, e_all, b_all, ends_s, l_s, l_all, skip_all, sizes_one,
    mixed_all, og_acc, og_send, og_recv, fp, frecv, fin_y, fin_pos, gp, rsbuf,
    ggrp, ggpos, gates_g, tot_all, sizes,
    final_ref, gq_ref, gk_ref, gg_ref, gw_ref,
    recv_sems, send_sems, load_sems,
):
    rows = q_ref.shape[0]
    span = rows * GROUP
    step_len = span // SUBS
    half = w_ref.shape[0] // 2
    ys = chans // PAIR
    wide = PAIR * LANES
    scale = 1.0 / math.sqrt(length)

    i = lax.axis_index("ctx")
    j = lax.axis_index("chan")
    z = lax.div(i, GROUP)
    k = lax.rem(i, GROUP)
    y = lax.div(j, PAIR)
    xl = lax.rem(j, PAIR)
    k1 = k + 1 - 2 * lax.rem(k, 2)
    k2 = lax.rem(k + 2, GROUP)
    k3 = GROUP - 1 - k
    kp = {0: k, 1: k1, 2: k2, 3: k3}
    xp = {0: xl, 1: PAIR - 1 - xl}

    def zmod(d):
        return lax.rem(z + d + zs, zs)

    def ymod(d):
        return lax.rem(y + d + ys, ys)

    def x_peer(dk, dx):
        return {"ctx": z * GROUP + kp[dk], "chan": y * PAIR + xp[dx]}

    def z_peer(d):
        return {"ctx": zmod(d) * GROUP + k, "chan": j}

    def y_peer(d):
        return {"ctx": i, "chan": ymod(d) * PAIR + xl}

    x_order = [(dk, dx) for dk in (2, 3, 1, 0) for dx in (1, 0) if dk or dx]
    g_order = (2, 3, 1)
    z_order = [zs // 2] + [d for n in range(zs // 2 - 1, 0, -1) for d in (n, -n)]

    def lane(index):
        return pl.ds(pl.multiple_of(index * LANES, LANES), LANES)

    def pair(index):
        return pl.ds(pl.multiple_of(index * wide, wide), wide)

    def row(index):
        return pl.ds(pl.multiple_of(index * rows, rows), rows)

    counts = [0, 0]

    class Batch:
        def __init__(self, lane_class):
            self.recv = recv_sems.at[counts[0]]
            counts[0] += 1
            self.out = lane_class
            self.units = 0

        def send(self, src, dst, peer, units):
            pltpu.make_async_remote_copy(
                src_ref=src, dst_ref=dst, send_sem=self.out.sem, recv_sem=self.recv,
                device_id=peer, device_id_type=MESH,
            ).start()
            self.units += units
            self.out.units += units

        def wait(self):
            part = self.out.sizes.at[pl.ds(0, self.units)]
            pltpu.make_async_copy(part, part, self.recv).wait()

    class Outgoing:
        def __init__(self, size_ref=sizes):
            self.sizes = size_ref
            self.sem = send_sems.at[counts[1]]
            counts[1] += 1
            self.units = 0

        def wait(self):
            part = self.sizes.at[pl.ds(0, self.units)]
            pltpu.make_async_copy(part, part, self.sem).wait()

    block_u = rows // 16
    out_x, out_y, out_z, out_zs, out_s, first_z = (
        Outgoing() for _ in range(6)
    )
    out_one = Outgoing(sizes_one)

    barrier = pltpu.get_barrier_semaphore()
    peers = [x_peer(*d) for d in x_order]
    peers += [z_peer(d) for d in z_order]
    peers += [y_peer(d) for d in range(1, ys)]
    for peer in peers:
        pl.semaphore_signal(barrier, inc=1, device_id=peer, device_id_type=MESH)

    loads = [
        pltpu.make_async_copy(src, dst, load_sems.at[n])
        for n, (src, dst) in enumerate((
            (q_hbm, q_ref), (key_hbm, key_ref), (cot_hbm, cot_ref), (w_hbm, w_ref),
            (gate_hbm, gate_ref), (rate_hbm, rate_ref), (res_hbm, res_ref), (skip_hbm, skip_ref),
        ))
    ]
    for copy in loads:
        copy.start()

    pl.semaphore_wait(barrier, len(peers))

    chunk = (pl.ds(0, half), pl.ds(half, half))
    ways = {0: ((1, 0, zs // 2), (-1, 1, zs // 2)), 1: ((1, 1, zs // 2 - 1), (-1, 0, zs // 2 - 1))}
    ring = {}
    chunk_u = half // 16

    def quarter(c, q):
        return pl.ds(c * half + q * (half // 2), half // 2)

    def weight_hop(h, long):
        for q in (0, 1):
            if h > 1:
                ring[h - 1, long, q].wait()
            if h > ways[long][0][2]:
                continue
            ring[h, long, q] = Batch(first_z if (h, long) == (1, 0) else out_z)
            for d, c, hops in ways[long]:
                spot = (quarter(c, q), lane(zmod(-d * (h - 1))))
                src = w_hbm.at[spot[0], :] if h == 1 else wall.at[spot]
                ring[h, long, q].send(src, wall.at[spot], z_peer(d), chunk_u // 2)

    y_order = (2, 1, -1)
    cot_y = [Batch(out_y) for _ in range(3)]
    for d in (1, -1):
        cot_y[0].send(cot_hbm.at[:, lane(k)], cotall.at[row(k), lane(j)], y_peer(d), block_u)
    cot_two = Batch(out_y)
    cot_two.send(cot_hbm, two_ref, y_peer(2), 4 * block_u)
    weight_hop(1, 0)
    for copy in loads[:2]:
        copy.wait()
    gat_s[...] = (q_ref[...].astype(f32) * key_ref[...].astype(f32)).astype(bf16)
    signals = Batch(out_x)
    for d in g_order:
        signals.send(gat_s.at[:, lane(kp[d])], xg.at[row(k), :], x_peer(d, 0), block_u)
    cot_a = Batch(out_x)
    for d in g_order:
        cot_a.send(
            cot_hbm.at[:, lane(kp[d])], cotall.at[row(k), lane(j)], x_peer(d, 0), block_u
        )
    for copy in loads[2:]:
        copy.wait()
    cotall[row(k), lane(j)] = cot_ref[:, lane(k)]
    xg[row(k), :] = gat_s[:, lane(k)]
    gateg[row(k), :] = gate_ref[:, lane(k)]
    wall[:, lane(z)] = w_ref[...]

    rate = rate_ref[:, lane(k)]
    inv_norm = jnp.sqrt(one_minus_exp(2.0 * rate) / one_minus_exp(2.0 * length * rate))
    gain = res_ref[:, lane(k)] * inv_norm
    decay = jnp.exp(-rate)
    decay_sub = jnp.exp(-step_len * rate)
    decay_span = jnp.exp(-span * rate)
    skip_b = jnp.broadcast_to(skip_ref[:, lane(k)], (SUBS, LANES))
    sub = lax.broadcasted_iota(jnp.int32, (SUBS, LANES), 0)

    def spread(table, m):
        return jnp.broadcast_to(table[m : m + 1, :], (SUBS, LANES))

    decays = [spread(decay, m) for m in range(MODES)]
    gains = [spread(gain, m) for m in range(MODES)]
    zero = jnp.zeros((SUBS, LANES), f32)

    def at_step(t):
        return pl.ds(t, SUBS, stride=step_len)

    def ends(src, backward):
        def body(s, state):
            t = step_len - 1 - s if backward else s
            value = src[at_step(t), :]
            return tuple(decays[m] * state[m] + value for m in range(MODES))

        return lax.fori_loop(0, step_len, body, (zero,) * MODES, unroll=8)

    def prefix(state, pre, backward, all_ref):
        for m in range(MODES):
            factor = spread(decay_sub, m)
            total = state[m]
            for shift in (1, 2, 4):
                moved = pltpu.roll(total, SUBS - shift if backward else shift, 0)
                keep = sub < SUBS - shift if backward else sub >= shift
                total = total + jnp.where(keep, factor * moved, 0.0)
                factor = factor * factor
            moved = pltpu.roll(total, SUBS - 1 if backward else 1, 0)
            pre[m] = jnp.where(sub < SUBS - 1 if backward else sub >= 1, moved, 0.0)
            edge = 0 if backward else SUBS - 1
            ends_s[m : m + 1, :] = total[edge : edge + 1, :]
        all_ref[z] = ends_s[...].astype(bf16)

    def carried(all_ref, backward):
        carry = jnp.zeros((MODES, LANES), f32)
        for n in range(zs):
            other = zs - 1 - n if backward else n
            ahead = z < other if backward else z > other
            carry = jnp.where(ahead, decay_span * carry + all_ref[other].astype(f32), carry)
        steps = (SUBS - 1 - sub if backward else sub).astype(f32)
        return tuple(
            jnp.exp(-step_len * steps * spread(rate, m)) * spread(carry, m)
            for m in range(MODES)
        )

    def tree(terms):
        while len(terms) > 1:
            terms = [a + b for a, b in zip(terms[::2], terms[1::2])]
        return terms[0]

    def sweep(src, out, state, backward):
        def body(s, state):
            t = step_len - 1 - s if backward else s
            value = src[at_step(t), :]
            state = tuple(decays[m] * state[m] + value for m in range(MODES))
            out[at_step(t), :] = (
                tree([gains[m] * state[m] for m in range(MODES)]) + skip_b * value
            )
            return state

        lax.fori_loop(0, step_len, body, state, unroll=8)

    def add_carried(out, state, backward):
        def body(s, state):
            t = step_len - 1 - s if backward else s
            state = tuple(decays[m] * state[m] for m in range(MODES))
            out[at_step(t), :] += tree(list(state))
            return state

        lax.fori_loop(0, step_len, body, tuple(gains[m] * state[m] for m in range(MODES)), unroll=8)

    def to_z(ref, units):
        batch = Batch(out_zs)
        for d in z_order:
            batch.send(ref.at[z], ref.at[z], z_peer(d), units)
        return batch

    first_z.wait()
    weight_hop(1, 1)
    cot_b = Batch(out_x)
    for dk in (1, 3, 2, 0):
        cot_b.send(
            cot_ref.at[:, lane(kp[dk])], cotall.at[row(k), lane(j)], x_peer(dk, 1), block_u
        )
    weight_hop(2, 0)
    gates_in = Batch(out_x)
    for d in g_order:
        gates_in.send(gate_ref.at[:, lane(kp[d])], gateg.at[row(k), :], x_peer(d, 0), block_u)
    signals.wait()
    x_f[...] = xg[...].astype(f32)
    prefix(ends(x_f, False), pre_f, False, e_all)
    e_batch = to_z(e_all, 1)
    cot_a.wait()
    for dy in (1, -1):
        for d in (1, 2, 3):
            piece = (row(kp[d]), lane(j))
            cot_y[1].send(cotall.at[piece], cotall.at[piece], y_peer(dy), block_u)
    weight_hop(2, 1)
    cot_two.wait()
    cot_spread = Batch(out_x)
    j_two = lane(ymod(2) * PAIR + xl)
    for dk, dx in x_order:
        cot_spread.send(
            two_ref.at[:, lane(kp[dk])], cotall.at[row(k), j_two], x_peer(dk, dx), block_u
        )
    cotall[row(k), j_two] = two_ref[:, lane(k)]
    cot_b.wait()
    other = (slice(None), lane(y * PAIR + xp[1]))
    for dy in (1, -1):
        cot_y[2].send(cotall.at[other], cotall.at[other], y_peer(dy), 4 * block_u)
    weight_hop(3, 0)
    sweep(x_f, co_f, tuple(pre_f[m] for m in range(MODES)), False)
    e_batch.wait()
    start_f = carried(e_all, False)
    add_carried(co_f, start_f, False)
    gates_in.wait()
    mixed_all[:, lane(k)] = (gateg[...].astype(f32) * co_f[...]).astype(bf16)
    mix_2 = Batch(out_x)
    mix_2.send(mixed_all.at[:, lane(k)], mixed_all.at[:, lane(k)], x_peer(2, 0), 4 * block_u)
    mix_1 = Batch(out_x)
    mix_1.send(mixed_all.at[:, lane(k)], mixed_all.at[:, lane(k)], x_peer(1, 0), 4 * block_u)
    weight_hop(3, 1)
    weight_hop(4, 0)
    for m in range(MODES):
        pre_f[m] += start_f[m]
    side = span // 2
    sides = [pl.ds(h * side, side) for h in (0, 1)]

    def add_out_grad(h, steps):
        for d in steps:
            block = lane(zmod(d))
            part = lax.dot_general(
                cotall[sides[h], block], wall[:, block], (((1,), (1,)), ((), ())),
                preferred_element_type=f32,
            )
            if d == 0:
                og_acc[sides[h], :] = part
            else:
                og_acc[sides[h], :] += part

    for batch in (*cot_y, cot_spread):
        batch.wait()
    for h in (0, 1):
        add_out_grad(h, (0, 1, -1, 2, -2))
    mix_2.wait()
    mix_1.send(mixed_all.at[:, lane(k2)], mixed_all.at[:, lane(k2)], x_peer(1, 0), 4 * block_u)
    weight_hop(4, 1)
    weight_hop(5, 0)
    og_a = [Batch(out_x), Batch(out_x)]
    og_b = Batch(out_x)
    for h in (0, 1):
        add_out_grad(h, (zs // 2 - 1, 1 - zs // 2, zs // 2))
        og_send[0, sides[h], :] = og_acc[sides[h], lane(k3)].astype(bf16)
        og_a[h].send(
            og_send.at[0, sides[h]], og_recv.at[0, sides[h]], x_peer(1, 0), 2 * block_u
        )
        og_send[1, sides[h], :] = og_acc[sides[h], lane(k1)].astype(bf16)
        og_b.send(
            og_send.at[1, sides[h]], og_recv.at[1, sides[h]], x_peer(1, 0), 2 * block_u
        )

    mix_1.wait()

    far_rows = pl.ds(pl.multiple_of((1 - lax.div(k, 2)) * side, side), side)
    near_rows = pl.ds(pl.multiple_of(lax.div(k, 2) * side, side), side)
    fin_parts = []

    def output_part(part_rows):
        for n in range(ys):
            cols = slice(n * wide, (n + 1) * wide)
            fp[part_rows, cols] = jnp.dot(
                mixed_all[part_rows, :], wall[:, cols], preferred_element_type=f32
            ).astype(bf16)
        batch = Batch(out_y)
        for d in y_order:
            batch.send(
                fp.at[part_rows, pair(ymod(d))],
                frecv.at[{1: 0, -1: 1, 2: 2}[d], part_rows, :], y_peer(d), 4 * block_u,
            )
        fin_parts.append(batch)

    output_part(far_rows)
    def weight_term(d):
        block = lane(zmod(d))
        gp[:, block] = lax.dot_general(
            mixed_all[...], cotall[:, block], (((0,), (0,)), ((), ())),
            preferred_element_type=f32,
        ).astype(bf16)

    sums = {}
    slots = {}
    for h in range(1, zs // 2 + 1):
        for long in (0, 1):
            for d, c, hops in ways[long]:
                if h <= hops:
                    slots[d, c, h] = len(slots)

    def weight_sum_hop(h, long):
        for q in (0, 1):
            if h > 1:
                sums[h - 1, long, q].wait()
            if h > ways[long][0][2]:
                continue
            sums[h, long, q] = Batch(out_s)
            part = pl.ds(q * (half // 2), half // 2)
            for d, c, hops in ways[long]:
                block = lane(zmod(d * (hops - h + 1)))
                if h == 1:
                    src = gp.at[quarter(c, q), block]
                else:
                    slot = slots[d, c, h - 1]
                    rsbuf[slot, part, :] = (
                        rsbuf[slot, part, :].astype(f32) + gp[quarter(c, q), block].astype(f32)
                    ).astype(bf16)
                    src = rsbuf.at[slot, part]
                sums[h, long, q].send(
                    src, rsbuf.at[slots[d, c, h], part], z_peer(d), chunk_u // 2
                )

    weight_term(zs // 2)
    weight_sum_hop(1, 0)
    og_c = Batch(out_x)
    for h in (0, 1):
        og_a[h].wait()
        og_send[2, sides[h], :] = (
            og_acc[sides[h], lane(k2)] + og_recv[0, sides[h], :].astype(f32)
        ).astype(bf16)
        og_c.send(
            og_send.at[2, sides[h]], og_recv.at[2, sides[h]], x_peer(2, 0), 2 * block_u
        )
    weight_term(zs // 2 - 1)
    weight_term(1 - zs // 2)
    weight_sum_hop(1, 1)
    output_part(near_rows)
    for d in range(2 - zs // 2, zs // 2 - 1):
        weight_term(d)
    weight_sum_hop(2, 0)

    og_b.wait()
    og_c.wait()
    og = og_acc[:, lane(k)] + og_recv[1].astype(f32) + og_recv[2].astype(f32)
    og = og.astype(bf16).astype(f32)
    cg_f[...] = og * gateg[...].astype(f32)
    prefix(ends(cg_f, True), pre_b, True, b_all)
    b_batch = to_z(b_all, 1)
    weight_sum_hop(2, 1)
    gates_g[...] = (og * co_f[...]).astype(bf16)
    gate_batch = Batch(out_x)
    for d in g_order:
        gate_batch.send(gates_g.at[row(kp[d]), :], gg_ref.at[:, lane(k)], x_peer(d, 0), block_u)
    gg_ref[:, lane(k)] = gates_g[row(k), :]

    def residue_body(s, carry):
        state, sums_m = carry
        value = x_f[at_step(s), :]
        grad = cg_f[at_step(s), :]
        state = tuple(decays[m] * state[m] + value for m in range(MODES))
        return state, tuple(sums_m[m] + grad * state[m] for m in range(MODES))

    _, mode_sums = lax.fori_loop(
        0, step_len, residue_body,
        (tuple(pre_f[m] for m in range(MODES)), (zero,) * MODES), unroll=8,
    )
    for m in range(MODES):
        l_s[m : m + 1, :] = jnp.sum(mode_sums[m], axis=0, keepdims=True)
    l_all[z] = l_s[...].astype(bf16)
    skip_all[z] = jnp.sum(cg_f[...] * x_f[...], axis=0, keepdims=True)
    l_batch = to_z(l_all, 1)
    skip_batch = Batch(out_one)
    for d in z_order:
        skip_batch.send(skip_all.at[z], skip_all.at[z], z_peer(d), 1)
    weight_sum_hop(3, 0)

    sweep(cg_f, co_f, tuple(pre_b[m] for m in range(MODES)), True)
    out_batch = Batch(out_x)

    def finish(batch, part_rows, order):
        batch.wait()
        fin = fp[part_rows, pair(y)].astype(f32)
        for n in range(ys - 1):
            fin = fin + frecv[n, part_rows, :].astype(f32)
        fin_y[part_rows, :] = fin.astype(bf16)
        for dk, dx in order:
            out_batch.send(
                fin_y.at[row(kp[dk]), lane(xp[dx])], fin_pos.at[xl, :, lane(k)],
                x_peer(dk, dx), block_u,
            )

    finish(fin_parts[0], far_rows, [(dk, dx) for dk in (2, 3) for dx in (1, 0)])
    b_batch.wait()
    add_carried(co_f, carried(b_all, True), True)
    ggrp[...] = co_f[...].astype(bf16)
    gg_batch = Batch(out_x)
    for d in g_order:
        gg_batch.send(ggrp.at[row(kp[d]), :], ggpos.at[:, lane(k)], x_peer(d, 0), block_u)
    ggpos[:, lane(k)] = ggrp[row(k), :]
    weight_sum_hop(3, 1)
    weight_sum_hop(4, 0)

    l_batch.wait()
    skip_batch.wait()
    total = l_all[0].astype(f32)
    for n in range(1, zs):
        total = total + l_all[n].astype(f32)
    tot_all[0:MODES, lane(k)] = total[0:MODES] * inv_norm * scale
    total = skip_all[0]
    for n in range(1, zs):
        total = total + skip_all[n]
    tot_all[MODES : MODES + SUBS, lane(k)] = spread(total, 0) * scale
    tot_batch = Batch(out_zs)
    for d in g_order:
        tot_batch.send(tot_all.at[:, lane(k)], tot_all.at[:, lane(k)], x_peer(d, 0), 3)
    finish(fin_parts[1], near_rows, [(0, 1), (1, 1), (1, 0)])
    fin_pos[xl, :, lane(k)] = fin_y[row(k), lane(xl)]

    writes = []

    def write(n, src, dst):
        copy = pltpu.make_async_copy(src, dst, load_sems.at[n])
        copy.start()
        writes.append(copy)

    gg_batch.wait()
    spread_grad = ggpos[...].astype(f32)
    gq_ref[...] = (spread_grad * key_ref[...].astype(f32)).astype(bf16)
    gk_ref[...] = (spread_grad * q_ref[...].astype(f32)).astype(bf16)
    write(1, gq_ref, gq_hbm)
    write(2, gk_ref, gk_hbm)
    gate_batch.wait()
    write(3, gg_ref, gg_hbm)

    weight_sum_hop(4, 1)
    weight_sum_hop(5, 0)
    for c in (0, 1):
        part = gp[chunk[c], lane(z)].astype(f32)
        for long in (0, 1):
            for d, other, hops in ways[long]:
                if other == c:
                    part = part + rsbuf[slots[d, c, hops]].astype(f32)
        gw_ref[chunk[c], :] = (part * scale).astype(bf16)
    write(4, gw_ref, gw_hbm)

    tot_batch.wait()
    write(5, tot_all.at[pl.ds(0, MODES), :], gres_hbm)
    write(6, tot_all.at[pl.ds(MODES, 1), :], gskip_hbm)
    out_batch.wait()
    final_ref[...] = (fin_pos[0].astype(f32) + fin_pos[1].astype(f32)).astype(bf16)
    write(0, final_ref, final_hbm)
    for out in (out_x, out_y, out_z, out_zs, out_s, out_one):
        out.wait()
    for copy in writes:
        copy.wait()
    assert counts == [RECEIVES, SENDS], counts


def store_kernel(*refs):
    count = (len(refs) - 2) // 3
    srcs, dsts, bufs = refs[:count], refs[count : 2 * count], refs[2 * count : 3 * count]
    in_sems, out_sems = refs[3 * count :]
    reads = [pltpu.make_async_copy(srcs[n], bufs[n], in_sems.at[n]) for n in range(count)]
    writes = [pltpu.make_async_copy(bufs[n], dsts[n], out_sems.at[n]) for n in range(count)]
    for copy in reads:
        copy.start()
    for read, write in zip(reads, writes):
        read.wait()
        write.start()
    for copy in writes:
        copy.wait()


def shards(mesh, *args):
    q, key_input, gate, cot, weight, rates, residues, skip = args
    zs, chans = mesh.shape["ctx"] // GROUP, mesh.shape["chan"]
    rows, width = q.shape
    depth = weight.shape[0]
    span = rows * GROUP
    length = rows * mesh.shape["ctx"]
    columns = zs * LANES
    hbm = pl.BlockSpec(memory_space=pltpu.HBM)
    shape = jax.ShapeDtypeStruct
    out_shape = (
        shape((rows, width), bf16),
        shape((rows, width), bf16),
        shape((rows, width), bf16),
        shape((rows, width), bf16),
        shape((depth, LANES), bf16),
        shape((MODES, width), f32),
        shape((1, width), f32),
    )
    outs = pl.pallas_call(
        functools.partial(kernel, zs, chans, length),
        out_shape=out_shape,
        in_specs=[hbm] * 8,
        out_specs=(hbm,) * 7,
        scratch_shapes=[
            pltpu.VMEM((rows, width), bf16),
            pltpu.VMEM((rows, width), bf16),
            pltpu.VMEM((rows, width), bf16),
            pltpu.VMEM((rows, width), bf16),
            pltpu.VMEM((depth, LANES), bf16),
            pltpu.VMEM((MODES, width), f32),
            pltpu.VMEM((MODES, width), f32),
            pltpu.VMEM((1, width), f32),
            pltpu.VMEM((rows, width), bf16),
            pltpu.VMEM((rows, width), bf16),
            pltpu.VMEM((span, columns), bf16),
            pltpu.VMEM((depth, columns), bf16),
            pltpu.VMEM((span, LANES), bf16),
            pltpu.VMEM((span, LANES), bf16),
            pltpu.VMEM((span, LANES), f32),
            pltpu.VMEM((span, LANES), f32),
            pltpu.VMEM((span, LANES), f32),
            pltpu.VMEM((MODES, SUBS, LANES), f32),
            pltpu.VMEM((MODES, SUBS, LANES), f32),
            pltpu.VMEM((zs, MODES, LANES), bf16),
            pltpu.VMEM((zs, MODES, LANES), bf16),
            pltpu.VMEM((MODES, LANES), f32),
            pltpu.VMEM((MODES, LANES), f32),
            pltpu.VMEM((zs, MODES, LANES), bf16),
            pltpu.VMEM((zs, 1, LANES), f32),
            pltpu.VMEM((zs, 1, LANES), f32),
            pltpu.VMEM((span, width), bf16),
            pltpu.VMEM((span, width), f32),
            pltpu.VMEM((3, span, LANES), bf16),
            pltpu.VMEM((3, span, LANES), bf16),
            pltpu.VMEM((span, columns), bf16),
            pltpu.VMEM((chans // PAIR - 1, span, PAIR * LANES), bf16),
            pltpu.VMEM((span, PAIR * LANES), bf16),
            pltpu.VMEM((PAIR, rows, width), bf16),
            pltpu.VMEM((depth, columns), bf16),
            pltpu.VMEM((2 * (zs - 1), depth // 2, LANES), bf16),
            pltpu.VMEM((span, LANES), bf16),
            pltpu.VMEM((rows, width), bf16),
            pltpu.VMEM((span, LANES), bf16),
            pltpu.VMEM((MODES + 8, width), f32),
            pltpu.VMEM((512, 16, LANES), bf16),
            *[pltpu.VMEM(a.shape, a.dtype) for a in out_shape[:5]],
            pltpu.SemaphoreType.DMA((RECEIVES,)),
            pltpu.SemaphoreType.DMA((SENDS,)),
            pltpu.SemaphoreType.DMA((8,)),
        ],
        compiler_params=pltpu.CompilerParams(
            collective_id=0, has_side_effects=True, vmem_limit_bytes=65000 * 1024
        ),
    )(q, key_input, gate, cot, weight, rates.T, residues.T, skip.reshape(1, -1))
    outs = pl.pallas_call(
        store_kernel,
        out_shape=out_shape,
        in_specs=[hbm] * 7,
        out_specs=(hbm,) * 7,
        scratch_shapes=[
            *[pltpu.VMEM(a.shape, a.dtype) for a in out_shape],
            pltpu.SemaphoreType.DMA((7,)),
            pltpu.SemaphoreType.DMA((7,)),
        ],
        compiler_params=pltpu.CompilerParams(vmem_limit_bytes=65000 * 1024),
    )(*outs)
    return (*outs[:5], outs[5].T, outs[6].reshape(-1))


def solution(mesh):
    placed = (
        P("ctx", "chan"),
        P("ctx", "chan"),
        P("ctx", "chan"),
        P("ctx", "chan"),
        P("chan", "ctx"),
        P("chan", None),
        P("chan", None),
        P("chan"),
    )
    return jax.shard_map(
        functools.partial(shards, mesh),
        mesh=mesh,
        in_specs=placed,
        out_specs=(
            P("ctx", "chan"),
            P("ctx", "chan"),
            P("ctx", "chan"),
            P("ctx", "chan"),
            P("chan", "ctx"),
            P("chan", None),
            P("chan"),
        ),
        check_vma=False,
    )
```
